128 devices in a mesh: lon: 32 (over z, y_hi, x), lat: 2 (over core), dp: 2 (over y_lo).
Axes of the slice: x: 4, y: 4 (y_hi: 2, y_lo: 2; y = y_hi * 2 + y_lo), z: 4, core: 2. Of those that a mesh axis runs over, the one named last changes fastest.
Arguments:
- fields: bfloat16 [4, 3, 16, 640, 1024], P('dp', None, 'lat', 'lon'), may hold values from -6 to 6
- grad_y: bfloat16 [4, 3, 16, 640, 1024], P('dp', None, 'lat', 'lon'), may hold values from -6 to 6
- w_qkv: bfloat16 [1024, 3072], replicated
- w_out: bfloat16 [1024, 1024], replicated, may hold values from -0.1875 to 0.1875
- mask_ids: int32 [16, 640], replicated, may hold values from 0 to 2
Outputs:
- out_y: bfloat16 [4, 3, 16, 640, 1024], P('dp', None, 'lat', 'lon')
- grad_fields: bfloat16 [4, 3, 16, 640, 1024], P('dp', None, 'lat', 'lon')
- grad_w_qkv: float32 [1024, 3072], P('lon', ('lat', 'dp'))
- grad_w_out: float32 [1024, 1024], P('lon', ('lat', 'dp'))
The draws below stay inside these ranges and needn't reach their ends.
All inputs are finite; a program needn't handle non-finite values.
Results may differ from the reference program's by a relative error of at most 0.033.
Values may be sent and summed in bfloat16 or wider, within the bound.
No kernel may reach another device: no remote copies, remote signals or barrier semaphores. Data moves between devices by JAX's collectives and lax.ppermute only.
A program may use at most 192 MiB of HBM per device.

```python
import jax
import jax.numpy as jnp
from jax import lax

D = 1024
HEADS = 16
LEV = 3
WLAT = 4
WLON = 5
SLAT = 2
SLON = 2
BATCH = 4
NLAT = 16
NLON = 640


def draw_w_qkv(key, part):
    key = jax.random.fold_in(key, 11)
    first_key = jax.random.fold_in(key, 0)
    drawn_all = jax.random.normal(first_key, (D, 3 * D), jnp.float32) * D ** (-0.5)
    return drawn_all.astype(jnp.bfloat16)


def plant(entries, own_key, low, top_value):
    longest = entries.shape.index(max(entries.shape))
    spots = []
    for shift in (0, 1):
        where = [jax.random.randint(jax.random.fold_in(own_key, axis), (), 0, length) for axis, length in enumerate(entries.shape)]
        where[longest] = (where[longest] + shift) % entries.shape[longest]
        spots.append(tuple(where))
    return entries.at[spots[0]].set(low).at[spots[1]].set(top_value)


def block_levels(rng, extent, shards, smallest, largest):
    def one(dim, parts):
        heights = jax.random.uniform(jax.random.fold_in(jax.random.fold_in(rng, 6), dim), (parts,), jnp.float32, smallest / len(shards), largest / len(shards))
        return jnp.repeat(jnp.exp(heights), extent[dim] // parts).reshape((-1,) + (1,) * (len(extent) - dim - 1))

    loudness = one(*shards[0])
    for cut in shards[1:]:
        loudness = loudness * one(*cut)
    return loudness


def scatter_about(stream_key, dims, width, reach, shards=(), held_as=jnp.bfloat16):
    level = block_levels(stream_key, dims, shards, -0.22, 0.18) if shards else 1.0
    drawn = jax.random.normal(stream_key, dims, jnp.float32) * width * level
    return jnp.minimum(jnp.maximum(drawn, -reach), reach).astype(held_as)


def setup_inputs(seed: int = 0) -> dict:
    arg_keys = jax.random.split(jax.random.key(seed), 6)
    return {
        "fields": scatter_about(arg_keys[0], (BATCH, LEV, NLAT, NLON, D), 1.0, 6.0, ((0, 2), (2, 2), (3, 32))),
        "grad_y": scatter_about(arg_keys[1], (BATCH, LEV, NLAT, NLON, D), 1.0, 6.0, ((0, 2), (2, 2), (3, 32))),
        "w_qkv": draw_w_qkv(jax.random.fold_in(arg_keys[5], 71), 0),
        "w_out": scatter_about(arg_keys[3], (D, D), D ** -0.5, 0.1875),
        "mask_ids": plant(jax.random.randint(arg_keys[4], (NLAT, NLON), 0, 3), jax.random.fold_in(arg_keys[4], 1), 0, 2).astype(jnp.int32),
    }


EPS = 1e-05

def layer_norm(values_in):
    as_float = values_in.astype(jnp.float32)
    row_mean = lax.optimization_barrier(jnp.mean(as_float, axis=-1, keepdims=True))
    centred = as_float - row_mean
    variance = lax.optimization_barrier(jnp.mean(centred * centred, axis=-1, keepdims=True))
    inv_std = lax.rsqrt(variance + EPS)
    return (centred * inv_std, inv_std)

def to_windows(grid_field):
    samples, levels, lat_rows, lon_cols, model_width = grid_field.shape
    shaped = grid_field.reshape(samples, levels, lat_rows // WLAT, WLAT, lon_cols // WLON, WLON, model_width)
    shaped = shaped.transpose(0, 2, 4, 1, 3, 5, 6)
    return shaped.reshape(samples * (lat_rows // WLAT) * (lon_cols // WLON), levels * WLAT * WLON, model_width)

def from_windows(windowed, samples, levels, lat_rows, lon_cols):
    model_width = windowed.shape[-1]
    shaped = windowed.reshape(samples, lat_rows // WLAT, lon_cols // WLON, levels, WLAT, WLON, model_width)
    shaped = shaped.transpose(0, 3, 1, 4, 2, 5, 6)
    return shaped.reshape(samples, levels, lat_rows, lon_cols, model_width)

def window_pass(normed, grad_win, allowed, w_qkv, w_out):
    wins, count, model_width = normed.shape
    head_size = model_width // HEADS
    score_scale = head_size ** (-0.5)
    flat_tokens = normed.reshape(wins * count, model_width)
    projected = jnp.dot(flat_tokens, w_qkv, preferred_element_type=jnp.float32).astype(jnp.bfloat16)
    projected = projected.reshape(wins, count, 3, HEADS, head_size).astype(jnp.float32)
    queries, key_rows, values = (projected[:, :, 0], projected[:, :, 1], projected[:, :, 2])
    scores = jnp.einsum('wihd,wjhd->whij', queries, key_rows) * score_scale
    scores = jnp.where(allowed[:, None], scores, -jnp.inf)
    row_max = lax.optimization_barrier(jnp.max(scores, axis=-1, keepdims=True))
    exp_score = jnp.exp(scores - row_max)
    attn_prob = exp_score / lax.optimization_barrier(jnp.sum(exp_score, axis=-1, keepdims=True))
    prob16 = attn_prob.astype(jnp.bfloat16).astype(jnp.float32)
    attended = jnp.einsum('whij,wjhd->wihd', prob16, values).astype(jnp.bfloat16)
    attended = attended.reshape(wins * count, model_width)
    branch = jnp.dot(attended, w_out, preferred_element_type=jnp.float32).astype(jnp.bfloat16)
    grad_flat = grad_win.reshape(wins * count, model_width)
    d_attended = jnp.dot(grad_flat, w_out.T, preferred_element_type=jnp.float32).astype(jnp.bfloat16)
    grad_out_w = jnp.dot(attended.T, grad_flat, preferred_element_type=jnp.float32)
    d_heads = d_attended.reshape(wins, count, HEADS, head_size).astype(jnp.float32)
    d_values = jnp.einsum('whij,wihd->wjhd', prob16, d_heads)
    d_prob = jnp.einsum('wihd,wjhd->whij', d_heads, values)
    row_delta = lax.optimization_barrier(jnp.sum(attn_prob * d_prob, axis=-1, keepdims=True))
    d_score = (attn_prob * (d_prob - row_delta) * score_scale).astype(jnp.bfloat16).astype(jnp.float32)
    d_queries = jnp.einsum('whij,wjhd->wihd', d_score, key_rows)
    d_keys = jnp.einsum('whij,wihd->wjhd', d_score, queries)
    d_projected = jnp.stack([d_queries, d_keys, d_values], axis=2).astype(jnp.bfloat16)
    d_projected = d_projected.reshape(wins * count, 3 * model_width)
    grad_qkv_w = jnp.dot(flat_tokens.T, d_projected, preferred_element_type=jnp.float32)
    d_normed = jnp.dot(d_projected, w_qkv.T, preferred_element_type=jnp.float32).astype(jnp.bfloat16)
    return (branch, d_normed, grad_qkv_w, grad_out_w)

def reference(fields, grad_y, w_qkv, w_out, mask_ids):
    levels = fields.shape[1]
    lat_total = fields.shape[2]
    lon_total = fields.shape[3]
    model_width = fields.shape[4]
    lat_global = ((jnp.arange(lat_total, dtype=jnp.int32) + SLAT) % lat_total).astype(jnp.int32)
    lon_global = ((jnp.arange(lon_total, dtype=jnp.int32) + SLON) % lon_total).astype(jnp.int32)
    region_ids = jnp.take(jnp.take(mask_ids, lat_global, axis=0), lon_global, axis=1)
    region_code = region_ids * 2 + (lat_global < SLAT).astype(jnp.int32)[:, None]
    code_grid = jnp.broadcast_to(region_code[None, None, :, :, None], (1, levels, lat_total, lon_total, 1))
    code_win = to_windows(code_grid)[..., 0]
    allowed = code_win[:, :, None] == code_win[:, None, :]

    def one_sample(carry, inputs):
        sample_x, sample_dy = inputs
        normed_f, inv_std = layer_norm(sample_x)
        normed = normed_f.astype(jnp.bfloat16)
        rolled_n = jnp.roll(normed, (-SLAT, -SLON), axis=(1, 2))[None]
        rolled_d = jnp.roll(sample_dy, (-SLAT, -SLON), axis=(1, 2))[None]
        branch_w, dnorm_w, grad_qkv_w, grad_out_w = window_pass(to_windows(rolled_n), to_windows(rolled_d), allowed, w_qkv, w_out)
        branch = jnp.roll(from_windows(branch_w, 1, levels, lat_total, lon_total)[0], (SLAT, SLON), axis=(1, 2))
        d_normed = jnp.roll(from_windows(dnorm_w, 1, levels, lat_total, lon_total)[0], (SLAT, SLON), axis=(1, 2))
        out_y = (sample_x.astype(jnp.float32) + branch.astype(jnp.float32)).astype(jnp.bfloat16)
        grad_g = d_normed.astype(jnp.float32)
        grad_x = sample_dy.astype(jnp.float32) + inv_std * (grad_g - lax.optimization_barrier(jnp.mean(grad_g, axis=-1, keepdims=True)) - normed_f * lax.optimization_barrier(jnp.mean(grad_g * normed_f, axis=-1, keepdims=True)))
        return ((carry[0] + grad_qkv_w, carry[1] + grad_out_w), (out_y, grad_x.astype(jnp.bfloat16)))
    start = (jnp.zeros((model_width, 3 * model_width), jnp.float32), jnp.zeros((model_width, model_width), jnp.float32))
    totals, outputs = lax.scan(one_sample, start, (fields, grad_y))
    return (outputs[0], outputs[1], totals[0], totals[1])
```

```python
import functools

import jax
import jax.numpy as jnp
import numpy as np
from jax import lax
from jax.experimental import pallas as pl
from jax.experimental.pallas import tpu as pltpu
from jax.sharding import PartitionSpec as P

HEADS = 16
WLAT = 4
WLON = 5
SLAT = 2
SLON = 2
EPS = 1e-05

SLOT = 32
GROUP = 128
QUADS = 4
BF = jnp.bfloat16
F32 = jnp.float32
VMEM = pltpu.CompilerParams(vmem_limit_bytes=56 * 1024 * 1024)
NT = (((1,), (1,)), ((), ()))


def dot(a, b):
    return jnp.dot(a, b, preferred_element_type=F32)


def dot_nt(a, b):
    return lax.dot_general(a, b, NT, preferred_element_type=F32)


X, Y, Z = 4, 2, 4
UNIT = 32
LON, LAT = 0, 1


def place_of(lon):
    return lon % X, (lon // X) % Y, lon // (X * Y)


def relative(block, pos_ref):
    lon = pos_ref[LON]
    x, y, z = place_of(block)
    x0, y0, z0 = lax.rem(lon, X), lax.rem(lax.div(lon, X), Y), lax.div(lon, X * Y)
    dx, dy, dz = lax.rem(x - x0 + X, X), lax.rem(y - y0 + Y, Y), lax.rem(z - z0 + Z, Z)
    return (dx * Z + dz) * Y + dy


def gather_matrix(levels, lon_cols):
    out = np.zeros((2, GROUP, levels * WLAT * SLOT), np.float32)
    for pair in range(2):
        for seg in range(levels * WLAT):
            for c in range(2 * WLON):
                place = (2 * WLON * pair + c + SLON) % lon_cols
                out[pair, seg * 2 * WLON + c, seg * SLOT + place] = 1.0
    return out.astype(jnp.bfloat16)


PLACES = ((2, 3, 4, 5), (6, 7, 0, 1))


def gather_kernel(
    pos_ref, pick_ref, f_ref, g_ref, lon_ref, lat_ref, cor_ref,
    xw_ref, nw_ref, nt_ref, gw_ref, xs, gs,
):
    levels, lon_cols, width = f_ref.shape[1], f_ref.shape[3], f_ref.shape[4]
    xs[...] = jnp.zeros_like(xs)
    gs[...] = jnp.zeros_like(gs)
    for half in range(2):
        for arr, (src, dst) in enumerate(((f_ref, xs), (g_ref, gs))):
            for level in range(levels):
                for r, place in enumerate(PLACES[half]):
                    base = (level * WLAT + r) * SLOT
                    if place < SLAT:
                        dst[base : base + lon_cols, :] = lat_ref[arr, 0, level, place]
                        dst[base : base + SLON, :] = cor_ref[arr, 0, level, place]
                    else:
                        dst[base : base + lon_cols, :] = src[0, level, place]
                        dst[base : base + SLON, :] = lon_ref[arr, 0, level, place]
        for pair in range(2):
            rows = slice((half * 2 + pair) * GROUP, (half * 2 + pair + 1) * GROUP)
            x = dot(pick_ref[pair], xs[...])
            gw_ref[rows, :] = dot(pick_ref[pair], gs[...]).astype(BF)
            xw_ref[rows, :] = x.astype(BF)
            centred = x - jnp.mean(x, axis=-1, keepdims=True)
            inv = lax.rsqrt(jnp.mean(centred * centred, axis=-1, keepdims=True) + EPS)
            normed = (centred * inv).astype(BF)
            nw_ref[rows, :] = normed
            turned = normed.T
            for block in range(width // UNIT):
                dst = pl.multiple_of(relative(block, pos_ref) * UNIT, UNIT)
                nt_ref[pl.ds(dst, UNIT), rows] = turned[block * UNIT : (block + 1) * UNIT]


def gather(pos, fields, grad_y, lon_in, lat_in, cor_in):
    samples, levels, rows, lon_cols, width = fields.shape
    tokens = samples * 4 * GROUP
    pick = jnp.asarray(gather_matrix(levels, lon_cols))
    block = (1, levels, rows, lon_cols, width)
    slots = levels * WLAT * SLOT
    return pl.pallas_call(
        gather_kernel,
        grid=(samples,),
        in_specs=[
            pl.BlockSpec(memory_space=pltpu.SMEM),
            pl.BlockSpec(pick.shape, lambda b: (0, 0, 0)),
            pl.BlockSpec(block, lambda b: (b, 0, 0, 0, 0)),
            pl.BlockSpec(block, lambda b: (b, 0, 0, 0, 0)),
            pl.BlockSpec((2, 1, levels, rows, SLON, width), lambda b: (0, b, 0, 0, 0, 0)),
            pl.BlockSpec((2, 1, levels, SLAT, lon_cols, width), lambda b: (0, b, 0, 0, 0, 0)),
            pl.BlockSpec((2, 1, levels, SLAT, SLON, width), lambda b: (0, b, 0, 0, 0, 0)),
        ],
        out_specs=[
            pl.BlockSpec((4 * GROUP, width), lambda b: (b, 0)),
            pl.BlockSpec((4 * GROUP, width), lambda b: (b, 0)),
            pl.BlockSpec((width, 4 * GROUP), lambda b: (0, b)),
            pl.BlockSpec((4 * GROUP, width), lambda b: (b, 0)),
        ],
        out_shape=[
            jax.ShapeDtypeStruct((tokens, width), BF),
            jax.ShapeDtypeStruct((tokens, width), BF),
            jax.ShapeDtypeStruct((width, tokens), BF),
            jax.ShapeDtypeStruct((tokens, width), BF),
        ],
        scratch_shapes=[pltpu.VMEM((slots, width), BF)] * 2,
        compiler_params=VMEM,
        name="gather",
    )(pos, pick, fields, grad_y, lon_in, lat_in, cor_in)


def attention_kernel(quads, pos_ref, bias_ref, nw_ref, gw_ref, nt_ref, wq_ref, wk_ref, wv_ref, wo_ref, *rest):
    if len(quads) == 1:
        kin_ref, att_ref, dq_ref, dk_ref, dv_ref, keep_ref, send_ref, gall, att_t = rest
    else:
        att_ref, dq_ref, dk_ref, dv_ref, keep_ref, send_ref, gok_ref, gos_ref, kout_ref, gall, att_t = rest
    turn, step = pl.program_id(0), pl.program_id(1)
    steps = pl.num_programs(1)
    rows, width = nw_ref.shape
    cols = wq_ref.shape[1]
    head = 64
    scale = head**-0.5
    base = pl.multiple_of(step * rows, rows)
    lat0 = pos_ref[LAT] == 0
    x0 = lax.rem(pos_ref[LON], X)
    normed = nw_ref[...]
    grad = gw_ref[...]
    gall[pl.ds(base, rows), :] = grad
    q_all = dot(normed, wq_ref[...]).astype(BF)
    k_all = dot(normed, wk_ref[...]).astype(BF)
    v_all = dot(normed, wv_ref[...]).astype(BF)
    da_all = dot_nt(grad, wo_ref[...]).astype(BF)
    first = lax.broadcasted_iota(jnp.int32, (GROUP, 2 * head), 1) < head
    upper = lax.broadcasted_iota(jnp.int32, (2 * head, GROUP), 0) < head
    zero = jnp.zeros((GROUP, 2 * head), BF)

    def split(pair):
        return jnp.concatenate([jnp.where(first, pair, zero), jnp.where(first, zero, pair)], axis=0)

    def side(turned):
        return jnp.concatenate(
            [jnp.where(upper, turned, zero), jnp.where(upper, zero, turned)], axis=1
        )

    def stacked(both):
        return jnp.concatenate([both[:, :GROUP], both[:, GROUP:]], axis=0)

    for group in range(rows // GROUP):
        bias = bias_ref[group]
        bias2 = jnp.concatenate([bias, bias], axis=1)
        here = pl.ds(pl.multiple_of(base + group * GROUP, GROUP), GROUP)
        for pair in range(2):
            at = (slice(group * GROUP, (group + 1) * GROUP), slice(pair * 128, (pair + 1) * 128))
            q, k, v, da = q_all[at], k_all[at], v_all[at], da_all[at]
            q2, da2 = split(q), split(da)
            scores = dot_nt(k, q2) * scale + bias2
            top = jnp.max(scores, axis=0, keepdims=True)
            expd = jnp.exp(scores - top)
            prob = expd / jnp.sum(expd, axis=0, keepdims=True)
            prob16 = prob.astype(BF)
            d_prob = dot_nt(v, da2)
            delta = jnp.sum(prob * d_prob, axis=0, keepdims=True)
            d_score = (prob * (d_prob - delta) * scale).astype(BF)
            out_t = dot(side(v.T), stacked(prob16)).astype(BF)
            att_ref[at] = out_t.T
            for block in range(128 // UNIT):
                dst = lax.rem(block - x0 + X, X) * (2 * UNIT) + pair * UNIT
                att_t[pl.ds(pl.multiple_of(dst, UNIT), UNIT), here] = out_t[
                    block * UNIT : (block + 1) * UNIT
                ]
            both = slice(pair * 128, (pair + 1) * 128)
            dq_ref[here, both] = dot(side(k.T), stacked(d_score)).astype(BF).T
            dk_ref[here, both] = dot(d_score, q2).astype(BF)
            dv_ref[here, both] = dot(prob16, da2).astype(BF)

    @pl.when(step == steps - 1)
    def _():
        grad_out = dot(att_t[...], gall[...])
        left, right = grad_out[:, : width // 2], grad_out[:, width // 2 :]
        mine, other = jnp.where(lat0, left, right).astype(BF), jnp.where(lat0, right, left).astype(BF)
        if len(quads) == 1:
            keep_ref[width:, :] = mine
            send_ref[width:, :] = other
        else:
            gok_ref[...] = mine
            gos_ref[...] = other

        def piece(i, carry):
            at = pl.ds(pl.multiple_of(i * 256, 256), 256)
            part = nt_ref[at, :]
            of_q = dot(part, dq_ref[...])
            of_v = dot(part, dv_ref[...])
            of_k = dot(part, dk_ref[...]).astype(BF)
            mine = jnp.where(lat0, of_q, of_v).astype(BF)
            other = jnp.where(lat0, of_v, of_q).astype(BF)
            if len(quads) == 1:
                keep_ref[at, :cols] = mine
                send_ref[at, :cols] = other
                before = kin_ref[at, :]
                keep_ref[at, cols:] = jnp.where(lat0, before, of_k)
                send_ref[at, cols:] = jnp.where(lat0, of_k, before)
            else:
                last = len(quads) * cols
                for which in range(len(quads)):

                    @pl.when(turn == which)
                    def _():
                        keep_ref[at, which * cols : (which + 1) * cols] = mine
                        send_ref[at, which * cols : (which + 1) * cols] = other
                        if quads[which] == 1:
                            kout_ref[at, :] = of_k
                        else:
                            stays = lat0 if quads[which] < 2 else jnp.logical_not(lat0)

                            @pl.when(stays)
                            def _():
                                keep_ref[at, last:] = of_k

                            @pl.when(jnp.logical_not(stays))
                            def _():
                                send_ref[at, last:] = of_k

            return carry

        lax.fori_loop(0, nt_ref.shape[0] // 256, piece, 0)


def attention(quads, pos, bias, nw, gw, nt, w_qkv, w_out, before=None):
    tokens, width = nw.shape
    cols = width // QUADS
    rows = 2 * GROUP
    count = len(quads)

    def quad(n):
        return 3 if count == 1 else jnp.where(n == 0, 0, 3 - n)

    whole = lambda n, s: (0, 0)
    tall = jax.ShapeDtypeStruct((tokens, count * cols), BF)
    in_specs = [
        pl.BlockSpec(memory_space=pltpu.SMEM),
        pl.BlockSpec((2, GROUP, GROUP), lambda n, s: (lax.rem(s, 2), 0, 0)),
        pl.BlockSpec((rows, width), lambda n, s: (s, 0)),
        pl.BlockSpec((rows, width), lambda n, s: (s, 0)),
        pl.BlockSpec((width, tokens), whole),
        pl.BlockSpec((width, cols), lambda n, s: (0, quad(n))),
        pl.BlockSpec((width, cols), lambda n, s: (0, QUADS + quad(n))),
        pl.BlockSpec((width, cols), lambda n, s: (0, 2 * QUADS + quad(n))),
        pl.BlockSpec((cols, width), lambda n, s: (quad(n), 0)),
    ]
    out_specs = [pl.BlockSpec((rows, cols), lambda n, s: (s, n))]
    out_specs += [pl.BlockSpec((tokens, cols), lambda n, s: (0, n))] * 3
    out_shape = [tall] * 4
    operands = [pos, bias, nw, gw, nt, w_qkv, w_qkv, w_qkv, w_out]
    if count == 1:
        in_specs.append(pl.BlockSpec((width, cols), whole))
        operands.append(before)
        shape = (width + cols, 2 * cols)
        out_specs += [pl.BlockSpec(shape, whole)] * 2
        out_shape += [jax.ShapeDtypeStruct(shape, BF)] * 2
    else:
        shape = (width, (count + 1) * cols)
        out_specs += [pl.BlockSpec(shape, whole)] * 2
        out_shape += [jax.ShapeDtypeStruct(shape, BF)] * 2
        out_specs += [pl.BlockSpec((cols, width // 2), lambda n, s: (n, 0))] * 2
        out_shape += [jax.ShapeDtypeStruct((count * cols, width // 2), BF)] * 2
        out_specs += [pl.BlockSpec((width, cols), whole)]
        out_shape += [jax.ShapeDtypeStruct((width, cols), BF)]
    return pl.pallas_call(
        functools.partial(attention_kernel, quads),
        grid=(count, tokens // rows),
        in_specs=in_specs,
        out_specs=out_specs,
        out_shape=out_shape,
        scratch_shapes=[pltpu.VMEM((tokens, width), BF), pltpu.VMEM((cols, tokens), BF)],
        compiler_params=VMEM,
        cost_estimate=pl.CostEstimate(
            flops=count * 14 * 10**9, bytes_accessed=16 * 10**6, transcendentals=10**6
        ),
        name="attention",
    )(*operands)


ORDER = (0, 2, 1, 3)


def output_kernel(pick_ref, xw_ref, gw_ref, wqkv_ref, wo_ref, *rest):
    first, last = rest[:4], rest[4:8]
    y_ref, gx_ref = rest[8:]
    levels, lon_cols, width = y_ref.shape[1], y_ref.shape[3], y_ref.shape[4]
    cols = width // QUADS

    def by_quad(i):
        parts = [first[i][:, n * cols : (n + 1) * cols] for n in range(QUADS - 1)] + [last[i][...]]
        return [parts[ORDER.index(quad)] for quad in range(QUADS)]

    branch = dot(jnp.concatenate(by_quad(0), axis=1), wo_ref[...]).astype(BF)
    d_all = jnp.concatenate([a for i in (1, 2, 3) for a in by_quad(i)], axis=1)
    g = dot_nt(d_all, wqkv_ref[...]).astype(BF).astype(F32)
    x = xw_ref[...].astype(F32)
    y = (x + branch.astype(F32)).astype(BF)
    centred = x - jnp.mean(x, axis=-1, keepdims=True)
    inv = lax.rsqrt(jnp.mean(centred * centred, axis=-1, keepdims=True) + EPS)
    normed = centred * inv
    gx = gw_ref[...].astype(F32) + inv * (
        g - jnp.mean(g, axis=-1, keepdims=True) - normed * jnp.mean(g * normed, axis=-1, keepdims=True)
    )
    gx = gx.astype(BF)
    place = dot(pick_ref[...], y).astype(BF)
    place_g = dot(pick_ref[...], gx).astype(BF)
    half = pl.program_id(1)

    for which in range(2):

        @pl.when(half == which)
        def _():
            for level in range(levels):
                for r, row in enumerate(PLACES[which]):
                    base = (level * WLAT + r) * SLOT
                    y_ref[0, level, row] = place[base : base + lon_cols, :]
                    gx_ref[0, level, row] = place_g[base : base + lon_cols, :]


def outputs(shape, xw, gw, w_qkv, w_out, first, last):
    samples, levels, lat_rows, lon_cols, width = shape
    rows = 2 * GROUP
    pick = np.asarray(gather_matrix(levels, lon_cols)).reshape(rows, -1).T
    pick = jnp.asarray(pick)
    cols = width // QUADS
    tall = pl.BlockSpec((rows, width), lambda b, h: (b * 2 + h, 0))
    narrow = lambda n: pl.BlockSpec((rows, n * cols), lambda b, h: (b * 2 + h, 0))
    whole = lambda b, h: (0, 0)
    out = pl.BlockSpec((1, levels, lat_rows, lon_cols, width), lambda b, h: (b, 0, 0, 0, 0))
    return pl.pallas_call(
        output_kernel,
        grid=(samples, 2),
        in_specs=[
            pl.BlockSpec(pick.shape, whole),
            tall,
            tall,
            pl.BlockSpec(w_qkv.shape, whole),
            pl.BlockSpec(w_out.shape, whole),
        ]
        + [narrow(QUADS - 1)] * 4
        + [narrow(1)] * 4,
        out_specs=[out, out],
        out_shape=[jax.ShapeDtypeStruct(shape, BF)] * 2,
        compiler_params=VMEM,
        name="outputs",
    )(pick, xw, gw, w_qkv, w_out, *first[:4], *last[:4])


def shifted(value, axis, steps):
    count = lax.axis_size(axis)
    pairs = [(source, (source + steps) % count) for source in range(count)]
    return lax.ppermute(value, axis, pairs)


def shifted_both(value, steps):
    lon, lat = lax.axis_size("lon"), lax.axis_size("lat")
    pairs = [
        (i * lat + j, ((i + steps) % lon) * lat + (j + steps) % lat)
        for i in range(lon)
        for j in range(lat)
    ]
    return lax.ppermute(value, ("lon", "lat"), pairs)


def allowed_bias(mask_ids, lat_rows, lon_cols, levels):
    lat_total, lon_total = mask_ids.shape
    lat_global = (lax.axis_index("lat") * lat_rows + SLAT + np.arange(lat_rows, dtype=np.int32)) % lat_total
    wide = jnp.concatenate([mask_ids, mask_ids[:, :SLON]], axis=1)
    wide = jnp.concatenate([wide, wide[:SLAT]], axis=0)
    ids = lax.dynamic_slice(
        wide,
        (lax.axis_index("lat") * lat_rows + SLAT, lax.axis_index("lon") * lon_cols + SLON),
        (lat_rows, lon_cols),
    )
    code = ids * 2 + (lat_global < SLAT).astype(jnp.int32)[:, None]
    window = np.arange(lon_cols, dtype=np.int32) // WLON
    code = code + 16 * window[None, :]
    code = code.reshape(lat_rows // WLAT, WLAT, lon_cols // (2 * WLON), 2 * WLON)
    code = code.transpose(0, 2, 1, 3).reshape(-1, 1, WLAT * 2 * WLON)
    code = jnp.broadcast_to(code, (code.shape[0], levels, code.shape[2])).reshape(code.shape[0], -1)
    code = jnp.pad(code, ((0, 0), (0, GROUP - code.shape[1])), constant_values=-1)
    same = code[:, :, None] == code[:, None, :]
    return jnp.where(same, 0.0, -jnp.inf).astype(F32)


def swapped(value, axis):
    return lax.ppermute(value, axis, [(0, 1), (1, 0)])


def to_distance(value, dx=0, dy=0, dz=0):
    pairs = []
    for lon in range(X * Y * Z):
        x, y, z = place_of(lon)
        pairs.append((lon, ((z + dz) % Z * Y + (y + dy) % Y) * X + (x + dx) % X))
    return lax.ppermute(value, "lon", pairs)


def added(*terms):
    total = terms[0].astype(F32)
    for term in terms[1:]:
        total = total + term.astype(F32)
    return total


def ring_sum(chunks, name):
    got = [to_distance(chunks[d], **{name: d}) for d in range(1, len(chunks))]
    return added(chunks[0], *got)


def first_sums(first):
    keep, send, go_keep, go_send = first[4:8]
    width = keep.shape[0]
    cols = width // QUADS
    total = added(keep, swapped(send, "lat")).astype(BF).reshape(X, Z, Y * UNIT, -1)
    by_z = ring_sum([total[:, d].reshape(X * Y * UNIT, -1) for d in range(Z)], "dz").astype(BF)
    by_z = by_z.reshape(X, Y * UNIT, -1)
    half = by_z.shape[2] // 2
    out = added(go_keep, swapped(go_send, "lat")).astype(BF)
    out = out.reshape(QUADS - 1, X, Y * UNIT, width // 2)
    chunks = [
        jnp.concatenate(
            [by_z[d, :, :half], by_z[d, :, half:], out[:, d].reshape(-1, width // 2)], axis=0
        )
        for d in range(X)
    ]
    total = ring_sum(chunks, "dx").astype(BF).reshape(2 + QUADS - 1, Y * UNIT, half)
    return total[0], total[1], [total[2 + n] for n in range(QUADS - 1)]


def last_sums(last, out_first):
    keep, send = last[4:6]
    half = keep.shape[1]
    lon = lax.axis_index("lon")
    total = added(keep, swapped(send, "lat")).astype(BF)
    width = Z * X * Y * UNIT
    rows = Z * Y * UNIT
    chunks = [
        jnp.concatenate(
            [
                total[d * rows : (d + 1) * rows],
                total[width + d * Y * UNIT : width + (d + 1) * Y * UNIT],
            ],
            axis=0,
        )
        for d in range(X)
    ]
    total = ring_sum(chunks, "dx").astype(BF)
    qkv = total[:rows].reshape(Z, Y * UNIT, half)
    out = out_first + [total[rows:]]
    out = jnp.stack([out[ORDER.index(quad)] for quad in range(QUADS)])
    out = out.reshape(Z, Y, UNIT, half)
    _, y0, z0 = place_of(lon)
    out = jnp.where(y0 == 0, out, out[:, ::-1]).reshape(Z, Y * UNIT, half)
    chunks = [
        jnp.concatenate([qkv[d], lax.dynamic_index_in_dim(out, (z0 + d) % Z, keepdims=False)], axis=0)
        for d in range(Z)
    ]
    total = ring_sum(chunks, "dz").astype(BF).reshape(2, Y * UNIT, half)
    return total[0], total[1]


def weight_sums(first, last):
    a0, a1, out_first = first_sums(first)
    b, out = last_sums(last, out_first)
    total = jnp.concatenate([a0, a1, b, out], axis=1).reshape(Y, UNIT, -1)
    total = ring_sum([total[0], total[1]], "dy").astype(BF)
    cols = total.shape[1] // 8
    piece = [total[:, i * cols : (i + 1) * cols] for i in range(8)]
    pick = lambda *which: jnp.concatenate([piece[i] for i in which], axis=1)
    lat0 = lax.axis_index("lat") == 0
    low = jnp.where(lat0, pick(0, 2, 1, 6), pick(3, 5, 0, 6))
    high = jnp.where(lat0, pick(4, 3, 5, 7), pick(2, 1, 4, 7))
    dp0 = lax.axis_index("dp") == 0
    got = swapped(jnp.where(dp0, high, low), "dp")
    total = added(jnp.where(dp0, low, high), got)
    return total[:, : 3 * cols], total[:, 3 * cols :]


def per_device(fields, grad_y, w_qkv, w_out, mask_ids):
    samples, levels, lat_rows, lon_cols, width = fields.shape
    pos = jnp.stack([lax.axis_index("lon"), lax.axis_index("lat")]).astype(jnp.int32)
    both = lambda f: jnp.stack([f(fields), f(grad_y)])
    lon_in = shifted(both(lambda a: a[:, :, :, :SLON]), "lon", -1)
    lat_in = shifted(both(lambda a: a[:, :, :SLAT]), "lat", -1)
    cor_in = shifted_both(both(lambda a: a[:, :, :SLAT, :SLON]), -1)
    bias = allowed_bias(mask_ids, lat_rows, lon_cols, levels)
    xw, nw, nt, gw = gather(pos, fields, grad_y, lon_in, lat_in, cor_in)
    first = attention(ORDER[:3], pos, bias, nw, gw, nt, w_qkv, w_out)
    last = attention(ORDER[3:], pos, bias, nw, gw, nt, w_qkv, w_out, before=first[8])
    y, gx = outputs(fields.shape, xw, gw, w_qkv, w_out, first, last)
    back = jnp.stack([y, gx])
    lon_out = shifted(back[:, :, :, SLAT:, :SLON], "lon", 1)
    lat_out = shifted(back[:, :, :, :SLAT, SLON:], "lat", 1)
    cor_out = shifted_both(back[:, :, :, :SLAT, :SLON], 1)
    res = []
    for i, own in enumerate((y, gx)):
        own = lax.dynamic_update_slice(own, lon_out[i], (0, 0, SLAT, 0, 0))
        own = lax.dynamic_update_slice(own, lat_out[i], (0, 0, 0, SLON, 0))
        own = lax.dynamic_update_slice(own, cor_out[i], (0, 0, 0, 0, 0))
        res.append(own)
    return (res[0], res[1], *weight_sums(first, last))


def solution(mesh):
    grid = P("dp", None, "lat", "lon", None)
    return jax.shard_map(
        per_device,
        mesh=mesh,
        in_specs=(grid, grid, P(), P(), P()),
        out_specs=(grid, grid, P("lon", ("lat", "dp")), P("lon", ("lat", "dp"))),
        check_vma=False,
    )
```

```python
import functools

import jax
import jax.numpy as jnp
import numpy as np
from jax import lax
from jax.experimental import pallas as pl
from jax.experimental.pallas import tpu as pltpu
from jax.sharding import PartitionSpec as P

HEADS = 16
LEV = 3
WLAT = 4
WLON = 5
SLAT = 2
SLON = 2
ROWS = 8
COLS = 20
EPS = 1e-05

SIDE = 2 * WLON
GROUP = 128
HALF = 4 * GROUP
OWN = LEV * SIDE * ROWS
RIM = 128
COR = 16
BACK = 64
QUADS = 4
ORDER = (0, 2, 1, 3)
BF = jnp.bfloat16
F32 = jnp.float32
NT = (((1,), (1,)), ((), ()))

X, Y, Z = 4, 2, 4
UNIT = 32
LON, LAT = 0, 1


def params():
    return pltpu.CompilerParams(vmem_limit_bytes=56 * 1024 * 1024)


def cost(micros):
    return pl.CostEstimate(flops=int(micros * 1.1e9), bytes_accessed=10**6, transcendentals=0)


def dot(a, b):
    return jnp.dot(a, b, preferred_element_type=F32)


def dot_nt(a, b):
    return lax.dot_general(a, b, NT, preferred_element_type=F32)


def place_of(lon):
    return lon % X, (lon // X) % Y, lon // (X * Y)


def relative(block, pos_ref):
    lon = pos_ref[LON]
    x, y, z = place_of(block)
    x0, y0, z0 = lax.rem(lon, X), lax.rem(lax.div(lon, X), Y), lax.div(lon, X * Y)
    dx, dy, dz = lax.rem(x - x0 + X, X), lax.rem(y - y0 + Y, Y), lax.rem(z - z0 + Z, Z)
    return (dx * Z + dz) * Y + dy


def token(level, r, c):
    return (level * WLAT + r) * SIDE + c


def every():
    for level in range(LEV):
        for c in range(SIDE):
            for i in range(ROWS):
                wr, r = divmod((i - SLAT) % ROWS, WLAT)
                yield level, c, i, wr, r


def one_hot(shape, places):
    out = np.zeros(shape, np.float32)
    for at in places:
        out[at] = 1.0
    return jnp.asarray(out.astype(jnp.bfloat16))


def pick_own():
    return one_hot(
        (2, GROUP, OWN),
        [
            (wr, token(level, r, c), (level * SIDE + c) * ROWS + i)
            for level, c, i, wr, r in every()
            if i >= SLAT
        ],
    )


def pick_rim(side):
    places = []
    for level, c, i, wr, r in every():
        if i < SLAT:
            column = SLON + side * SIDE + c
            if column < COLS:
                src = (level * COLS + column) * SLAT + i
            else:
                src = RIM + (level * SLON + column - COLS) * SLAT + i
            places.append((token(level, r, c), src))
    return one_hot((GROUP, RIM + COR), places)


def pick_out():
    return one_hot(
        (OWN, 2 * GROUP),
        [
            ((level * SIDE + c) * ROWS + i, wr * GROUP + token(level, r, c))
            for level, c, i, wr, r in every()
        ],
    )


def pick_back():
    return one_hot(
        (BACK + COR, GROUP),
        [
            ((level * SIDE + c) * SLAT + i, token(level, r, c))
            for level, c, i, wr, r in every()
            if i < SLAT
        ]
        + [
            (BACK + (level * SLON + c - SIDE + SLON) * SLAT + i, token(level, r, c))
            for level, c, i, wr, r in every()
            if i < SLAT and c >= SIDE - SLON
        ],
    )


def pick_strip():
    rim = [
        ((level * COLS + column) * SLAT + i, (level * COLS + column) * ROWS + i)
        for level in range(LEV)
        for column in range(COLS)
        for i in range(SLAT)
    ]
    cor = [
        (RIM + (level * SLON + column) * SLAT + i, (level * COLS + column) * ROWS + i)
        for level in range(LEV)
        for column in range(SLON)
        for i in range(SLAT)
    ]
    return one_hot((RIM + COR, LEV * COLS * ROWS), rim + cor)


def pick_place(columns, offset, height):
    return one_hot(
        (LEV, columns * ROWS, height),
        [
            (level, c * ROWS + i, (level * (columns + offset) + c) * SLAT + i)
            for level in range(LEV)
            for c in range(columns)
            for i in range(SLAT)
        ],
    )


def strips_kernel(pick_ref, f_ref, g_ref, lon_ref, rim_ref, cor_ref):
    for arr, ref in enumerate((f_ref, g_ref)):
        block = ref[0]
        lon_ref[arr, 0] = block[:, : SLON * ROWS]
        strip = dot(pick_ref[...], block.reshape(-1, block.shape[-1])).astype(BF)
        rim_ref[arr, 0] = strip[:RIM]
        cor_ref[arr, 0] = strip[RIM:]


def strips(f, g):
    samples, levels, rows, width = f.shape
    pick = pick_strip()
    block = pl.BlockSpec((1, levels, rows, width), lambda b: (b, 0, 0, 0))
    shapes = [(levels, SLON * ROWS, width), (RIM, width), (COR, width)]
    return pl.pallas_call(
        strips_kernel,
        grid=(samples,),
        in_specs=[pl.BlockSpec(pick.shape, lambda b: (0, 0)), block, block],
        out_specs=[
            pl.BlockSpec((2, 1) + s, lambda b, n=len(s): (0, b) + (0,) * n) for s in shapes
        ],
        out_shape=[jax.ShapeDtypeStruct((2, samples) + s, BF) for s in shapes],
        compiler_params=params(),
        cost_estimate=cost(3),
        name="strips",
    )(pick, f, g)


def project_kernel(
    side, pos_ref, own_ref, pick_ref, f_ref, g_ref, lon_ref, rim_ref, cor_ref, wq_ref, wk_ref, wv_ref, wo_ref,
    xw_ref, gw_ref, nt_ref, q_ref, k_ref, v_ref, da_ref, nw,
):
    samples, levels, _, width = f_ref.shape

    @pl.when(pl.program_id(0) == 0)
    def _():
        for b in range(samples):
            got = []
            for arr, ref in enumerate((f_ref, g_ref)):
                parts = []
                for level in range(levels):
                    if side == 0:
                        parts.append(ref[b, level, SLON * ROWS : (SLON + SIDE) * ROWS])
                    else:
                        parts.append(ref[b, level, (SLON + SIDE) * ROWS :])
                        parts.append(lon_ref[arr, b, level])
                own = jnp.concatenate(parts, axis=0)
                rim = jnp.concatenate([rim_ref[arr, b], cor_ref[arr, b]], axis=0)
                got.append((own, rim))
            for wr in range(2):
                at = slice((b * 2 + wr) * GROUP, (b * 2 + wr + 1) * GROUP)
                x, g = (dot(own_ref[wr], own) for own, _ in got)
                if wr == 1:
                    x, g = (a + dot(pick_ref[...], rim) for a, (_, rim) in zip((x, g), got))
                gw_ref[at, :] = g.astype(BF)
                xw_ref[at, :] = x.astype(BF)
                centred = x - jnp.mean(x, axis=-1, keepdims=True)
                inv = lax.rsqrt(jnp.mean(centred * centred, axis=-1, keepdims=True) + EPS)
                normed = (centred * inv).astype(BF)
                nw[at, :] = normed
                turned = normed.T
                for block in range(width // UNIT):
                    dst = pl.multiple_of(relative(block, pos_ref) * UNIT, UNIT)
                    nt_ref[pl.ds(dst, UNIT), at] = turned[block * UNIT : (block + 1) * UNIT]

    q_ref[...] = dot(nw[...], wq_ref[...]).astype(BF)
    k_ref[...] = dot(nw[...], wk_ref[...]).astype(BF)
    v_ref[...] = dot(nw[...], wv_ref[...]).astype(BF)
    da_ref[...] = dot_nt(gw_ref[...], wo_ref[...]).astype(BF)


def project(side, pos, f, g, lon_in, rim_in, cor_in, w_qkv, w_out):
    width = f.shape[-1]
    cols = width // QUADS
    whole = lambda n: (0, 0)
    full = lambda a: pl.BlockSpec(a.shape, lambda n: (0,) * a.ndim)
    own, pick = pick_own(), pick_rim(side)
    tall = jax.ShapeDtypeStruct((HALF, width), BF)
    return pl.pallas_call(
        functools.partial(project_kernel, side),
        grid=(QUADS,),
        in_specs=[
            pl.BlockSpec(memory_space=pltpu.SMEM),
            full(own),
            full(pick),
            full(f),
            full(g),
            full(lon_in),
            full(rim_in),
            full(cor_in),
            pl.BlockSpec((width, cols), lambda n: (0, n)),
            pl.BlockSpec((width, cols), lambda n: (0, QUADS + n)),
            pl.BlockSpec((width, cols), lambda n: (0, 2 * QUADS + n)),
            pl.BlockSpec((cols, width), lambda n: (n, 0)),
        ],
        out_specs=[
            pl.BlockSpec((HALF, width), whole),
            pl.BlockSpec((HALF, width), whole),
            pl.BlockSpec((width, HALF), whole),
        ]
        + [pl.BlockSpec((HALF, cols), lambda n: (0, n))] * 4,
        out_shape=[tall, tall, jax.ShapeDtypeStruct((width, HALF), BF)] + [tall] * 4,
        scratch_shapes=[pltpu.VMEM((HALF, width), BF)],
        compiler_params=params(),
        cost_estimate=cost(9),
        name="project",
    )(pos, own, pick, f, g, lon_in, rim_in, cor_in, w_qkv, w_qkv, w_qkv, w_out)


def attention_kernel(quads, pos_ref, bias_ref, *rest):
    sides, rest = (rest[:6], rest[6:12]), rest[12:]
    if len(quads) == 1:
        kin_ref, att_ref, dq_ref, dk_ref, dv_ref, keep_ref, send_ref, att_t = rest
    else:
        att_ref, dq_ref, dk_ref, dv_ref, keep_ref, send_ref, gok_ref, gos_ref, kout_ref, att_t = rest
    turn = pl.program_id(0)
    width = sides[0][0].shape[0]
    cols = att_ref.shape[1]
    head = 64
    scale = head**-0.5
    lat0 = pos_ref[LAT] == 0
    x0 = lax.rem(pos_ref[LON], X)
    first = lax.broadcasted_iota(jnp.int32, (GROUP, 2 * head), 1) < head
    upper = lax.broadcasted_iota(jnp.int32, (2 * head, GROUP), 0) < head
    zero = jnp.zeros((GROUP, 2 * head), BF)

    def split(pair):
        return jnp.concatenate([jnp.where(first, pair, zero), jnp.where(first, zero, pair)], axis=0)

    def beside(turned):
        return jnp.concatenate(
            [jnp.where(upper, turned, zero), jnp.where(upper, zero, turned)], axis=1
        )

    def stacked(both):
        return jnp.concatenate([both[:, :GROUP], both[:, GROUP:]], axis=0)

    def unit(refs, side, group, wr, pair):
        _, _, q_ref, k_ref, v_ref, da_ref = refs
        both = slice(pair * 128, (pair + 1) * 128)
        at = (pl.ds(pl.multiple_of(group * GROUP, GROUP), GROUP), both)
        here = pl.ds(pl.multiple_of(side * HALF + group * GROUP, GROUP), GROUP)
        bias = bias_ref[side * 2 + wr]
        q, k, v, da = q_ref[at], k_ref[at], v_ref[at], da_ref[at]
        q2, da2 = split(q), split(da)
        scores = dot_nt(k, q2) * scale + jnp.concatenate([bias, bias], axis=1)
        d_prob = dot_nt(v, da2)
        top = jnp.max(scores, axis=0, keepdims=True)
        expd = jnp.exp(scores - top)
        prob = expd * (1.0 / jnp.sum(expd, axis=0, keepdims=True))
        prob16 = prob.astype(BF)
        part = prob * d_prob
        delta = jnp.sum(part, axis=0, keepdims=True)
        d_score = ((part - prob * delta) * scale).astype(BF)
        out_t = dot(beside(v.T), stacked(prob16)).astype(BF)
        att_ref[here, both] = out_t.T
        for block in range(128 // UNIT):
            dst = lax.rem(block - x0 + X, X) * (2 * UNIT) + pair * UNIT
            att_t[pl.ds(pl.multiple_of(dst, UNIT), UNIT), here] = out_t[
                block * UNIT : (block + 1) * UNIT
            ]
        dv_ref[here, both] = dot(prob16, da2).astype(BF)
        dk_ref[here, both] = dot(d_score, q2).astype(BF)
        dq_ref[here, both] = dot(beside(k.T), stacked(d_score)).astype(BF).T

    for side in range(2):

        def sample(b, carry):
            for wr in range(2):
                for pair in range(2):
                    unit(sides[side], side, b * 2 + wr, wr, pair)
            return carry

        lax.fori_loop(0, HALF // (2 * GROUP), sample, 0)

    low, high = slice(0, HALF), slice(HALF, 2 * HALF)

    def total(left, i, right):
        return dot(sides[0][i][left, :], right[low, :]) + dot(sides[1][i][left, :], right[high, :])

    grad_out = dot(att_t[:, low], sides[0][1][...]) + dot(att_t[:, high], sides[1][1][...])
    left, right = grad_out[:, : width // 2], grad_out[:, width // 2 :]
    mine, other = jnp.where(lat0, left, right).astype(BF), jnp.where(lat0, right, left).astype(BF)
    if len(quads) == 1:
        keep_ref[width:, :] = mine
        send_ref[width:, :] = other
    else:
        gok_ref[...] = mine
        gos_ref[...] = other

    def piece(i, carry):
        at = pl.ds(pl.multiple_of(i * 256, 256), 256)
        of_q = total(at, 0, dq_ref)
        of_v = total(at, 0, dv_ref)
        of_k = total(at, 0, dk_ref).astype(BF)
        mine = jnp.where(lat0, of_q, of_v).astype(BF)
        other = jnp.where(lat0, of_v, of_q).astype(BF)
        if len(quads) == 1:
            keep_ref[at, :cols] = mine
            send_ref[at, :cols] = other
            before = kin_ref[at, :]
            keep_ref[at, cols:] = jnp.where(lat0, before, of_k)
            send_ref[at, cols:] = jnp.where(lat0, of_k, before)
        else:
            last = len(quads) * cols
            for which in range(len(quads)):

                @pl.when(turn == which)
                def _():
                    keep_ref[at, which * cols : (which + 1) * cols] = mine
                    send_ref[at, which * cols : (which + 1) * cols] = other
                    if quads[which] == 1:
                        kout_ref[at, :] = of_k
                    else:
                        stays = lat0 if quads[which] < 2 else jnp.logical_not(lat0)

                        @pl.when(stays)
                        def _():
                            keep_ref[at, last:] = of_k

                        @pl.when(jnp.logical_not(stays))
                        def _():
                            send_ref[at, last:] = of_k

        return carry

    lax.fori_loop(0, width // 256, piece, 0)


def attention(quads, pos, bias, sides, before=None):
    width = sides[0][0].shape[1]
    cols = width // QUADS
    tokens = 2 * HALF
    count = len(quads)

    def quad(n):
        return 3 if count == 1 else jnp.where(n == 0, 0, 3 - n)

    whole = lambda n: (0, 0)
    tall = jax.ShapeDtypeStruct((tokens, count * cols), BF)
    in_specs = [
        pl.BlockSpec(memory_space=pltpu.SMEM),
        pl.BlockSpec(bias.shape, lambda n: (0, 0, 0)),
    ]
    operands = [pos, bias]
    for _, gw, nt, q, k, v, da in sides:
        in_specs += [pl.BlockSpec((width, HALF), whole), pl.BlockSpec((HALF, width), whole)]
        in_specs += [pl.BlockSpec((HALF, cols), lambda n: (0, quad(n)))] * 4
        operands += [nt, gw, q, k, v, da]
    out_specs = [pl.BlockSpec((tokens, cols), lambda n: (0, n))] * 4
    out_shape = [tall] * 4
    if count == 1:
        in_specs.append(pl.BlockSpec((width, cols), whole))
        operands.append(before)
        shape = (width + cols, 2 * cols)
        out_specs += [pl.BlockSpec(shape, whole)] * 2
        out_shape += [jax.ShapeDtypeStruct(shape, BF)] * 2
    else:
        shape = (width, (count + 1) * cols)
        out_specs += [pl.BlockSpec(shape, whole)] * 2
        out_shape += [jax.ShapeDtypeStruct(shape, BF)] * 2
        out_specs += [pl.BlockSpec((cols, width // 2), lambda n: (n, 0))] * 2
        out_shape += [jax.ShapeDtypeStruct((count * cols, width // 2), BF)] * 2
        out_specs += [pl.BlockSpec((width, cols), whole)]
        out_shape += [jax.ShapeDtypeStruct((width, cols), BF)]
    return pl.pallas_call(
        functools.partial(attention_kernel, quads),
        grid=(count,),
        in_specs=in_specs,
        out_specs=out_specs,
        out_shape=out_shape,
        scratch_shapes=[pltpu.VMEM((cols, tokens), BF)],
        compiler_params=params(),
        cost_estimate=cost(11 * count),
        name="attention",
    )(*operands)


def output_kernel(out_ref, back_ref, x0, x1, dy0, dy1, wqkv_ref, wo_ref, *rest):
    first, last = rest[:4], rest[4:8]
    y0, g0, y1, g1, rim_ref, cor_ref, lon_ref, branch_at, g_at = rest[8:]
    levels = y0.shape[1]
    cols = last[0].shape[1]
    step = pl.program_id(1)

    def by_quad(i):
        parts = [first[i][:, n * cols : (n + 1) * cols] for n in range(QUADS - 1)] + [last[i][...]]
        return [parts[ORDER.index(quad)] for quad in range(QUADS)]

    branch_at[step] = dot(jnp.concatenate(by_quad(0), axis=1), wo_ref[...]).astype(BF)
    d_all = jnp.concatenate([a for i in (1, 2, 3) for a in by_quad(i)], axis=1)
    g_at[step] = dot_nt(d_all, wqkv_ref[...]).astype(BF)

    def finish(side, x_ref, dy_ref, refs):
        def sample(b, carry):
            at = pl.ds(pl.multiple_of(b * 2 * GROUP, 2 * GROUP), 2 * GROUP)
            joined = lambda ref: jnp.concatenate([ref[n, at] for n in range(QUADS)], axis=1).astype(F32)
            x = x_ref[at, :].astype(F32)
            y = (x + joined(branch_at)).astype(BF)
            g = joined(g_at)
            centred = x - jnp.mean(x, axis=-1, keepdims=True)
            inv = lax.rsqrt(jnp.mean(centred * centred, axis=-1, keepdims=True) + EPS)
            normed = centred * inv
            gx = dy_ref[at, :].astype(F32) + inv * (
                g
                - jnp.mean(g, axis=-1, keepdims=True)
                - normed * jnp.mean(g * normed, axis=-1, keepdims=True)
            )
            for arr, (value, ref) in enumerate(zip((y, gx.astype(BF)), refs)):
                placed = dot(out_ref[...], value).astype(BF)
                back = dot(back_ref[...], value[GROUP:]).astype(BF)
                rim_ref[side, arr, b] = back[:BACK]
                if side == 1:
                    cor_ref[arr, b] = back[BACK:]
                kept = (SIDE if side == 0 else SIDE - SLON) * ROWS
                for level in range(levels):
                    start = level * SIDE * ROWS
                    ref[b, level] = placed[start : start + kept]
                    if side == 1:
                        lon_ref[arr, b, level] = placed[start + kept : start + SIDE * ROWS]
            return carry

        lax.fori_loop(0, HALF // (2 * GROUP), sample, 0)

    ends = step == pl.num_programs(1) - 1

    @pl.when(jnp.logical_and(ends, pl.program_id(0) == 0))
    def _():
        finish(0, x0, dy0, (y0, g0))

    @pl.when(jnp.logical_and(ends, pl.program_id(0) == 1))
    def _():
        finish(1, x1, dy1, (y1, g1))


def outputs(samples, sides, w_qkv, w_out, first, last):
    width = w_out.shape[0]
    cols = width // QUADS
    out, back = pick_out(), pick_back()
    full = lambda shape: pl.BlockSpec(shape, lambda s, n: (0,) * len(shape))
    kept = (SIDE - SLON) * ROWS
    shapes = [(samples, LEV, SIDE * ROWS, width)] * 2 + [(samples, LEV, kept, width)] * 2
    shapes += [(2, 2, samples, BACK, width), (2, samples, COR, width)]
    shapes += [(2, samples, LEV, SLON * ROWS, width)]
    return pl.pallas_call(
        output_kernel,
        grid=(2, QUADS),
        in_specs=[full(out.shape), full(back.shape)]
        + [full((HALF, width))] * 4
        + [
            pl.BlockSpec((cols, 3 * width), lambda s, n: (n, 0)),
            pl.BlockSpec((width, cols), lambda s, n: (0, n)),
        ]
        + [pl.BlockSpec((HALF, (QUADS - 1) * cols), lambda s, n: (s, 0))] * 4
        + [pl.BlockSpec((HALF, cols), lambda s, n: (s, 0))] * 4,
        out_specs=[full(s) for s in shapes],
        out_shape=[jax.ShapeDtypeStruct(s, BF) for s in shapes],
        scratch_shapes=[pltpu.VMEM((QUADS, HALF, cols), BF)] * 2,
        compiler_params=params(),
        cost_estimate=cost(18),
        name="outputs",
    )(
        out, back, sides[0][0], sides[1][0], sides[0][1], sides[1][1], w_qkv, w_out,
        *first[:4], *last[:4],
    )


def merge_kernel(place0_ref, place1_ref, placec_ref, y0, g0, y1, g1, rim, cor, lon, y_ref, gx_ref):
    levels = y_ref.shape[1]
    for arr, (low, high, out) in enumerate(((y0, y1, y_ref), (g0, g1, gx_ref))):
        for level in range(levels):
            start = 0
            for mine, pick, strip in (
                (lon[arr, 0, level], placec_ref, cor[arr, 0]),
                (low[0, level], place0_ref, rim[0, arr, 0]),
                (high[0, level], place1_ref, rim[1, arr, 0]),
            ):
                rows = mine.shape[0]
                here = lax.broadcasted_iota(jnp.int32, mine.shape, 0) % ROWS < SLAT
                placed = dot(pick[level], strip).astype(BF)
                out[0, level, start : start + rows] = jnp.where(here, placed, mine)
                start += rows


def merge(y0, g0, y1, g1, rim, cor, lon):
    samples, levels, _, width = y0.shape
    picks = [pick_place(SIDE, 0, BACK), pick_place(SIDE - SLON, SLON, BACK), pick_place(SLON, 0, COR)]
    full = lambda a: pl.BlockSpec(a.shape, lambda b: (0,) * a.ndim)
    own = lambda a: pl.BlockSpec((1,) + a.shape[1:], lambda b: (b,) + (0,) * (a.ndim - 1))
    strip = lambda a: pl.BlockSpec((2, 1) + a.shape[2:], lambda b: (0, b) + (0,) * (a.ndim - 2))
    shape = jax.ShapeDtypeStruct((samples, levels, COLS * ROWS, width), BF)
    return pl.pallas_call(
        merge_kernel,
        grid=(samples,),
        in_specs=[full(a) for a in picks]
        + [own(a) for a in (y0, g0, y1, g1)]
        + [pl.BlockSpec((2, 2, 1) + rim.shape[3:], lambda b: (0, 0, b, 0, 0))]
        + [strip(a) for a in (cor, lon)],
        out_specs=[own(shape)] * 2,
        out_shape=[shape] * 2,
        compiler_params=params(),
        cost_estimate=cost(4),
        name="merge",
    )(*picks, y0, g0, y1, g1, rim, cor, lon)


def shifted(value, axis, steps):
    count = lax.axis_size(axis)
    pairs = [(source, (source + steps) % count) for source in range(count)]
    return lax.ppermute(value, axis, pairs)


def shifted_both(value, steps):
    lon, lat = lax.axis_size("lon"), lax.axis_size("lat")
    pairs = [
        (i * lat + j, ((i + steps) % lon) * lat + (j + steps) % lat)
        for i in range(lon)
        for j in range(lat)
    ]
    return lax.ppermute(value, ("lon", "lat"), pairs)


def allowed_bias(mask_ids):
    lat_total = mask_ids.shape[0]
    start = lax.axis_index("lat") * ROWS + SLAT
    lat_global = (start + np.arange(ROWS, dtype=np.int32)) % lat_total
    wide = jnp.concatenate([mask_ids, mask_ids[:, :SLON]], axis=1)
    wide = jnp.concatenate([wide, wide[:SLAT]], axis=0)
    ids = lax.dynamic_slice(wide, (start, lax.axis_index("lon") * COLS + SLON), (ROWS, COLS))
    code = ids * 2 + (lat_global < SLAT).astype(jnp.int32)[:, None]
    code = code + 16 * (np.arange(COLS, dtype=np.int32) // WLON)[None, :]
    code = code.reshape(2, WLAT, 2, SIDE).transpose(2, 0, 1, 3).reshape(4, 1, WLAT * SIDE)
    code = jnp.broadcast_to(code, (4, LEV, WLAT * SIDE)).reshape(4, -1)
    code = jnp.pad(code, ((0, 0), (0, GROUP - code.shape[1])), constant_values=-1)
    same = code[:, :, None] == code[:, None, :]
    return jnp.where(same, 0.0, -jnp.inf).astype(F32)


def swapped(value, axis):
    return lax.ppermute(value, axis, [(0, 1), (1, 0)])


def to_distance(value, dx=0, dy=0, dz=0):
    pairs = []
    for lon in range(X * Y * Z):
        x, y, z = place_of(lon)
        pairs.append((lon, ((z + dz) % Z * Y + (y + dy) % Y) * X + (x + dx) % X))
    return lax.ppermute(value, "lon", pairs)


def added(*terms):
    total = terms[0].astype(F32)
    for term in terms[1:]:
        total = total + term.astype(F32)
    return total


def ring_sum(chunks, name):
    got = [to_distance(chunks[d], **{name: d}) for d in range(1, len(chunks))]
    return added(chunks[0], *got)


def first_chunks(first):
    keep, send, go_keep, go_send = first[4:8]
    total = added(keep, swapped(send, "lat")).astype(BF).reshape(X, Z, Y * UNIT, -1)
    return [total[:, d].reshape(X * Y * UNIT, -1) for d in range(Z)]


def first_sums(by_z):
    by_z = by_z.reshape(X, Y * UNIT, -1)
    return ring_sum([by_z[d] for d in range(X)], "dx").astype(BF)


def last_chunks(first, last):
    go_keep, go_send = first[6:8]
    keep, send = last[4:6]
    half = keep.shape[1]
    total = added(keep, swapped(send, "lat")).astype(BF)
    out = added(go_keep, swapped(go_send, "lat")).astype(BF).reshape(QUADS - 1, X, Y * UNIT, half)
    rows = Z * Y * UNIT
    chunks = []
    for d in range(X):
        last_out = total[X * rows + d * Y * UNIT : X * rows + (d + 1) * Y * UNIT]
        by_quad = [*(out[n, d] for n in range(QUADS - 1)), last_out]
        by_quad = [by_quad[ORDER.index(quad)] for quad in range(QUADS)]
        chunks.append(jnp.concatenate([total[d * rows : (d + 1) * rows], *by_quad], axis=0))
    return chunks


def last_sums(total):
    half = total.shape[1]
    total = total.reshape(2, Z, Y * UNIT, half)
    qkv, out = total[0], total[1].reshape(Z, Y, UNIT, half)
    _, y0, z0 = place_of(lax.axis_index("lon"))
    out = jnp.where(y0 == 0, out, out[:, ::-1]).reshape(Z, Y * UNIT, half)
    chunks = [
        jnp.concatenate([qkv[d], lax.dynamic_index_in_dim(out, (z0 + d) % Z, keepdims=False)], axis=0)
        for d in range(Z)
    ]
    total = ring_sum(chunks, "dz").astype(BF).reshape(2, Y * UNIT, half)
    return total[0], total[1]


def final_sums(a, b, out):
    total = jnp.concatenate([a, b, out], axis=1).reshape(Y, UNIT, -1)
    total = ring_sum([total[0], total[1]], "dy").astype(BF)
    cols = total.shape[1] // 8
    piece = [total[:, i * cols : (i + 1) * cols] for i in range(8)]
    pick = lambda *which: jnp.concatenate([piece[i] for i in which], axis=1)
    lat0 = lax.axis_index("lat") == 0
    low = jnp.where(lat0, pick(0, 2, 1, 6), pick(3, 5, 0, 6))
    high = jnp.where(lat0, pick(4, 3, 5, 7), pick(2, 1, 4, 7))
    dp0 = lax.axis_index("dp") == 0
    got = swapped(jnp.where(dp0, high, low), "dp")
    total = added(jnp.where(dp0, low, high), got)
    return total[:, : 3 * cols], total[:, 3 * cols :]


def per_device(fields, grad_y, w_qkv, w_out, mask_ids):
    samples, levels, lat_rows, lon_cols, width = fields.shape
    flat = lambda a: a.transpose(0, 1, 3, 2, 4).reshape(samples, levels, lon_cols * lat_rows, width)
    f, g = flat(fields), flat(grad_y)
    pos = jnp.stack([lax.axis_index("lon"), lax.axis_index("lat")]).astype(jnp.int32)
    lon_out, rim_out, cor_out = strips(f, g)
    rim_in = shifted(rim_out, "lat", -1)
    cor_in = shifted_both(cor_out, -1)
    lon_in = shifted(lon_out, "lon", -1)
    bias = allowed_bias(mask_ids)
    side0 = project(0, pos, f, g, lon_out, rim_in, cor_out, w_qkv, w_out)
    side1 = project(1, pos, f, g, lon_in, rim_in, cor_in, w_qkv, w_out)
    sides = (side0, side1)
    first = attention(ORDER[:3], pos, bias, sides)
    by_z, before = lax.optimization_barrier((first_chunks(first), first[8]))
    last = attention(ORDER[3:], pos, bias, sides, before=before)
    got_z = [to_distance(by_z[d], dz=d) for d in range(1, Z)]
    by_x, got_z, att = lax.optimization_barrier((last_chunks(first, last), got_z, last[0]))
    got_x = [to_distance(by_x[d], dx=d) for d in range(1, X)]
    by_z = added(by_z[0], *got_z).astype(BF)
    by_z, att = lax.optimization_barrier((by_z, att))
    y0, g0, y1, g1, rim, cor, lon = outputs(samples, sides, w_qkv, w_out, first, (att, *last[1:]))
    got_x, rim, cor, lon = lax.optimization_barrier((got_x, rim, cor, lon))
    lon = shifted(lon, "lon", 1)
    cor = shifted_both(cor, 1)
    rim = shifted(rim, "lat", 1)
    a = first_sums(by_z)
    b, out = last_sums(added(by_x[0], *got_x).astype(BF))
    y, gx = merge(y0, g0, y1, g1, rim, cor, lon)
    unflat = lambda a: a.reshape(samples, levels, lon_cols, lat_rows, width).transpose(0, 1, 3, 2, 4)
    return (unflat(y), unflat(gx), *final_sums(a, b, out))


def solution(mesh):
    grid = P("dp", None, "lat", "lon", None)
    return jax.shard_map(
        per_device,
        mesh=mesh,
        in_specs=(grid, grid, P(), P(), P()),
        out_specs=(grid, grid, P("lon", ("lat", "dp")), P("lon", ("lat", "dp"))),
        check_vma=False,
    )
```

```python
import functools

import jax
import jax.numpy as jnp
import numpy as np
from jax import lax
from jax.experimental import pallas as pl
from jax.experimental.pallas import tpu as pltpu
from jax.sharding import PartitionSpec as P

HEADS = 16
LEV = 3
WLAT = 4
WLON = 5
SLAT = 2
SLON = 2
ROWS = 8
COLS = 20
EPS = 1e-05

SIDE = 2 * WLON
GROUP = 128
HALF = 4 * GROUP
OWN = LEV * SIDE * ROWS
RIM = 128
COR = 16
BACK = 64
QUADS = 4
BF = jnp.bfloat16
F32 = jnp.float32
NT = (((1,), (1,)), ((), ()))

X, Y, Z = 4, 2, 4
UNIT = 32
LON, LAT = 0, 1


def params():
    return pltpu.CompilerParams(vmem_limit_bytes=56 * 1024 * 1024)


def cost(micros):
    return pl.CostEstimate(flops=int(micros * 1.1e9), bytes_accessed=10**6, transcendentals=0)


def dot(a, b):
    return jnp.dot(a, b, preferred_element_type=F32)


def dot_nt(a, b):
    return lax.dot_general(a, b, NT, preferred_element_type=F32)


def place_of(lon):
    return lon % X, (lon // X) % Y, lon // (X * Y)


def relative(block, pos_ref):
    lon = pos_ref[LON]
    x, y, z = place_of(block)
    x0, y0, z0 = lax.rem(lon, X), lax.rem(lax.div(lon, X), Y), lax.div(lon, X * Y)
    dx, dy, dz = lax.rem(x - x0 + X, X), lax.rem(y - y0 + Y, Y), lax.rem(z - z0 + Z, Z)
    return (dx * Z + dz) * Y + dy


def token(level, r, c):
    return (level * WLAT + r) * SIDE + c


def every():
    for level in range(LEV):
        for c in range(SIDE):
            for i in range(ROWS):
                wr, r = divmod((i - SLAT) % ROWS, WLAT)
                yield level, c, i, wr, r


def one_hot(shape, places):
    out = np.zeros(shape, np.float32)
    for at in places:
        out[at] = 1.0
    return jnp.asarray(out.astype(jnp.bfloat16))


def pick_own():
    return one_hot(
        (2, GROUP, OWN),
        [
            (wr, token(level, r, c), (level * SIDE + c) * ROWS + i)
            for level, c, i, wr, r in every()
            if i >= SLAT
        ],
    )


def pick_rim(side):
    places = []
    for level, c, i, wr, r in every():
        if i < SLAT:
            column = SLON + side * SIDE + c
            if column < COLS:
                src = (level * COLS + column) * SLAT + i
            else:
                src = RIM + (level * SLON + column - COLS) * SLAT + i
            places.append((token(level, r, c), src))
    return one_hot((GROUP, RIM + COR), places)


def pick_out():
    return one_hot(
        (OWN, 2 * GROUP),
        [
            ((level * SIDE + c) * ROWS + i, wr * GROUP + token(level, r, c))
            for level, c, i, wr, r in every()
        ],
    )


def pick_back():
    return one_hot(
        (BACK + COR, GROUP),
        [
            ((level * SIDE + c) * SLAT + i, token(level, r, c))
            for level, c, i, wr, r in every()
            if i < SLAT
        ]
        + [
            (BACK + (level * SLON + c - SIDE + SLON) * SLAT + i, token(level, r, c))
            for level, c, i, wr, r in every()
            if i < SLAT and c >= SIDE - SLON
        ],
    )


def pick_strip():
    rim = [
        ((level * COLS + column) * SLAT + i, (level * COLS + column) * ROWS + i)
        for level in range(LEV)
        for column in range(COLS)
        for i in range(SLAT)
    ]
    cor = [
        (RIM + (level * SLON + column) * SLAT + i, (level * COLS + column) * ROWS + i)
        for level in range(LEV)
        for column in range(SLON)
        for i in range(SLAT)
    ]
    return one_hot((RIM + COR, LEV * COLS * ROWS), rim + cor)


def pick_place(columns, offset, height):
    return one_hot(
        (LEV, columns * ROWS, height),
        [
            (level, c * ROWS + i, (level * (columns + offset) + c) * SLAT + i)
            for level in range(LEV)
            for c in range(columns)
            for i in range(SLAT)
        ],
    )


def strips_kernel(pick_ref, f_ref, g_ref, lon_ref, rim_ref, cor_ref):
    for arr, ref in enumerate((f_ref, g_ref)):
        block = ref[0]
        lon_ref[arr, 0] = block[:, : SLON * ROWS]
        strip = dot(pick_ref[...], block.reshape(-1, block.shape[-1])).astype(BF)
        rim_ref[arr, 0] = strip[:RIM]
        cor_ref[arr, 0] = strip[RIM:]


def strips(f, g):
    samples, levels, rows, width = f.shape
    pick = pick_strip()
    block = pl.BlockSpec((1, levels, rows, width), lambda b: (b, 0, 0, 0))
    shapes = [(levels, SLON * ROWS, width), (RIM, width), (COR, width)]
    return pl.pallas_call(
        strips_kernel,
        grid=(samples,),
        in_specs=[pl.BlockSpec(pick.shape, lambda b: (0, 0)), block, block],
        out_specs=[
            pl.BlockSpec((2, 1) + s, lambda b, n=len(s): (0, b) + (0,) * n) for s in shapes
        ],
        out_shape=[jax.ShapeDtypeStruct((2, samples) + s, BF) for s in shapes],
        compiler_params=params(),
        cost_estimate=cost(3),
        name="strips",
    )(pick, f, g)


def project_kernel(
    side, pos_ref, own_ref, pick_ref, f_ref, g_ref, lon_ref, rim_ref, cor_ref, wq_ref, wk_ref, wv_ref, wo_ref,
    xw_ref, gw_ref, nt_ref, q_ref, k_ref, v_ref, da_ref, nw,
):
    samples, levels, _, width = f_ref.shape

    @pl.when(pl.program_id(0) == 0)
    def _():
        for b in range(samples):
            got = []
            for arr, ref in enumerate((f_ref, g_ref)):
                parts = []
                for level in range(levels):
                    if side == 0:
                        parts.append(ref[b, level, SLON * ROWS : (SLON + SIDE) * ROWS])
                    else:
                        parts.append(ref[b, level, (SLON + SIDE) * ROWS :])
                        parts.append(lon_ref[arr, b, level])
                own = jnp.concatenate(parts, axis=0)
                rim = jnp.concatenate([rim_ref[arr, b], cor_ref[arr, b]], axis=0)
                got.append((own, rim))
            for wr in range(2):
                at = slice((b * 2 + wr) * GROUP, (b * 2 + wr + 1) * GROUP)
                x, g = (dot(own_ref[wr], own) for own, _ in got)
                if wr == 1:
                    x, g = (a + dot(pick_ref[...], rim) for a, (_, rim) in zip((x, g), got))
                gw_ref[at, :] = g.astype(BF)
                xw_ref[at, :] = x.astype(BF)
                centred = x - jnp.mean(x, axis=-1, keepdims=True)
                inv = lax.rsqrt(jnp.mean(centred * centred, axis=-1, keepdims=True) + EPS)
                normed = (centred * inv).astype(BF)
                nw[at, :] = normed
                turned = normed.T
                for block in range(width // UNIT):
                    dst = pl.multiple_of(relative(block, pos_ref) * UNIT, UNIT)
                    nt_ref[pl.ds(dst, UNIT), at] = turned[block * UNIT : (block + 1) * UNIT]

    q_ref[...] = dot(nw[...], wq_ref[...]).astype(BF)
    k_ref[...] = dot(nw[...], wk_ref[...]).astype(BF)
    v_ref[...] = dot(nw[...], wv_ref[...]).astype(BF)
    da_ref[...] = dot_nt(gw_ref[...], wo_ref[...]).astype(BF)


def project(side, pos, f, g, lon_in, rim_in, cor_in, w_qkv, w_out):
    width = f.shape[-1]
    cols = width // QUADS
    whole = lambda n: (0, 0)
    full = lambda a: pl.BlockSpec(a.shape, lambda n: (0,) * a.ndim)
    own, pick = pick_own(), pick_rim(side)
    tall = jax.ShapeDtypeStruct((HALF, width), BF)
    return pl.pallas_call(
        functools.partial(project_kernel, side),
        grid=(QUADS,),
        in_specs=[
            pl.BlockSpec(memory_space=pltpu.SMEM),
            full(own),
            full(pick),
            full(f),
            full(g),
            full(lon_in),
            full(rim_in),
            full(cor_in),
            pl.BlockSpec((width, cols), lambda n: (0, n)),
            pl.BlockSpec((width, cols), lambda n: (0, QUADS + n)),
            pl.BlockSpec((width, cols), lambda n: (0, 2 * QUADS + n)),
            pl.BlockSpec((cols, width), lambda n: (n, 0)),
        ],
        out_specs=[
            pl.BlockSpec((HALF, width), whole),
            pl.BlockSpec((HALF, width), whole),
            pl.BlockSpec((width, HALF), whole),
        ]
        + [pl.BlockSpec((HALF, cols), lambda n: (0, n))] * 4,
        out_shape=[tall, tall, jax.ShapeDtypeStruct((width, HALF), BF)] + [tall] * 4,
        scratch_shapes=[pltpu.VMEM((HALF, width), BF)],
        compiler_params=params(),
        cost_estimate=cost(9),
        name="project",
    )(pos, own, pick, f, g, lon_in, rim_in, cor_in, w_qkv, w_qkv, w_qkv, w_out)


def attention_kernel(quads, pos_ref, bias_ref, *rest):
    sides, rest = (rest[:6], rest[6:12]), rest[12:]
    if quads == (3,):
        kin_ref, rest = rest[0], rest[1:]
    if quads == (1,):
        att_ref, dq_ref, dk_ref, dv_ref, keep_ref, send_ref, kout_ref, att_t = rest
    elif quads == (3,):
        att_ref, dq_ref, dk_ref, dv_ref, keep_ref, send_ref, att_t = rest
    else:
        att_ref, dq_ref, dk_ref, dv_ref, keep_ref, send_ref, gok_ref, gos_ref, att_t = rest
    turn = pl.program_id(0)
    width = sides[0][0].shape[0]
    cols = att_ref.shape[1]
    head = 64
    scale = head**-0.5
    lat0 = pos_ref[LAT] == 0
    x0 = lax.rem(pos_ref[LON], X)
    first = lax.broadcasted_iota(jnp.int32, (GROUP, 2 * head), 1) < head
    upper = lax.broadcasted_iota(jnp.int32, (2 * head, GROUP), 0) < head
    zero = jnp.zeros((GROUP, 2 * head), BF)

    def split(pair):
        return jnp.concatenate([jnp.where(first, pair, zero), jnp.where(first, zero, pair)], axis=0)

    def beside(turned):
        return jnp.concatenate(
            [jnp.where(upper, turned, zero), jnp.where(upper, zero, turned)], axis=1
        )

    def stacked(both):
        return jnp.concatenate([both[:, :GROUP], both[:, GROUP:]], axis=0)

    def unit(refs, side, group, wr, pair):
        _, _, q_ref, k_ref, v_ref, da_ref = refs
        both = slice(pair * 128, (pair + 1) * 128)
        at = (pl.ds(pl.multiple_of(group * GROUP, GROUP), GROUP), both)
        here = pl.ds(pl.multiple_of(side * HALF + group * GROUP, GROUP), GROUP)
        bias = bias_ref[side * 2 + wr]
        q, k, v, da = q_ref[at], k_ref[at], v_ref[at], da_ref[at]
        q2, da2 = split(q), split(da)
        scores = dot_nt(k, q2) * scale + jnp.concatenate([bias, bias], axis=1)
        d_prob = dot_nt(v, da2)
        top = jnp.max(scores, axis=0, keepdims=True)
        expd = jnp.exp(scores - top)
        prob = expd * (1.0 / jnp.sum(expd, axis=0, keepdims=True))
        prob16 = prob.astype(BF)
        part = prob * d_prob
        delta = jnp.sum(part, axis=0, keepdims=True)
        d_score = ((part - prob * delta) * scale).astype(BF)
        out_t = dot(beside(v.T), stacked(prob16)).astype(BF)
        att_ref[here, both] = out_t.T
        for block in range(128 // UNIT):
            dst = lax.rem(block - x0 + X, X) * (2 * UNIT) + pair * UNIT
            att_t[pl.ds(pl.multiple_of(dst, UNIT), UNIT), here] = out_t[
                block * UNIT : (block + 1) * UNIT
            ]
        dv_ref[here, both] = dot(prob16, da2).astype(BF)
        dk_ref[here, both] = dot(d_score, q2).astype(BF)
        dq_ref[here, both] = dot(beside(k.T), stacked(d_score)).astype(BF).T

    for side in range(2):

        def sample(b, carry):
            for wr in range(2):
                for pair in range(2):
                    unit(sides[side], side, b * 2 + wr, wr, pair)
            return carry

        lax.fori_loop(0, HALF // (2 * GROUP), sample, 0)

    low, high = slice(0, HALF), slice(HALF, 2 * HALF)

    def total(left, i, right):
        return dot(sides[0][i][left, :], right[low, :]) + dot(sides[1][i][left, :], right[high, :])

    grad_out = dot(att_t[:, low], sides[0][1][...]) + dot(att_t[:, high], sides[1][1][...])
    left, right = grad_out[:, : width // 2], grad_out[:, width // 2 :]
    mine, other = jnp.where(lat0, left, right).astype(BF), jnp.where(lat0, right, left).astype(BF)
    if quads == (1,):
        for half in range(2):
            below = slice(width + half * cols, width + (half + 1) * cols)
            keep_ref[below, :] = mine[:, half * cols : (half + 1) * cols]
            send_ref[below, :] = other[:, half * cols : (half + 1) * cols]
    elif quads == (3,):
        keep_ref[width:, :] = mine
        send_ref[width:, :] = other
    else:
        gok_ref[...] = mine
        gos_ref[...] = other

    def piece(i, carry):
        at = pl.ds(pl.multiple_of(i * 256, 256), 256)
        of_q = total(at, 0, dq_ref)
        of_v = total(at, 0, dv_ref)
        of_k = total(at, 0, dk_ref).astype(BF)
        mine = jnp.where(lat0, of_q, of_v).astype(BF)
        other = jnp.where(lat0, of_v, of_q).astype(BF)
        if quads == (0, 2):
            for which in range(2):

                @pl.when(turn == which)
                def _():
                    keep_ref[at, which * cols : (which + 1) * cols] = mine
                    send_ref[at, which * cols : (which + 1) * cols] = other
                    stays = lat0 if which == 0 else jnp.logical_not(lat0)

                    @pl.when(stays)
                    def _():
                        keep_ref[at, 2 * cols :] = of_k

                    @pl.when(jnp.logical_not(stays))
                    def _():
                        send_ref[at, 2 * cols :] = of_k

        else:
            keep_ref[at, :cols] = mine
            send_ref[at, :cols] = other
            if quads == (1,):
                kout_ref[at, :] = of_k
            else:
                before = kin_ref[at, :]
                keep_ref[at, cols:] = jnp.where(lat0, before, of_k)
                send_ref[at, cols:] = jnp.where(lat0, of_k, before)

        return carry

    lax.fori_loop(0, width // 256, piece, 0)


def attention(quads, pos, bias, sides, before=None):
    width = sides[0][0].shape[1]
    cols = width // QUADS
    tokens = 2 * HALF
    count = len(quads)

    def quad(n):
        return 2 * n if count == 2 else quads[0]

    whole = lambda n: (0, 0)
    tall = jax.ShapeDtypeStruct((tokens, count * cols), BF)
    in_specs = [
        pl.BlockSpec(memory_space=pltpu.SMEM),
        pl.BlockSpec(bias.shape, lambda n: (0, 0, 0)),
    ]
    operands = [pos, bias]
    for _, gw, nt, q, k, v, da in sides:
        in_specs += [pl.BlockSpec((width, HALF), whole), pl.BlockSpec((HALF, width), whole)]
        in_specs += [pl.BlockSpec((HALF, cols), lambda n: (0, quad(n)))] * 4
        operands += [nt, gw, q, k, v, da]
    out_specs = [pl.BlockSpec((tokens, cols), lambda n: (0, n))] * 4
    out_shape = [tall] * 4
    if before is not None:
        in_specs.append(pl.BlockSpec((width, cols), whole))
        operands.append(before)
    shape = {0: (width, 3 * cols), 1: (width + 2 * cols, cols), 3: (width + cols, 2 * cols)}[quads[0]]
    out_specs += [pl.BlockSpec(shape, whole)] * 2
    out_shape += [jax.ShapeDtypeStruct(shape, BF)] * 2
    if quads == (0, 2):
        out_specs += [pl.BlockSpec((cols, width // 2), lambda n: (n, 0))] * 2
        out_shape += [jax.ShapeDtypeStruct((count * cols, width // 2), BF)] * 2
    elif quads == (1,):
        out_specs += [pl.BlockSpec((width, cols), whole)]
        out_shape += [jax.ShapeDtypeStruct((width, cols), BF)]
    return pl.pallas_call(
        functools.partial(attention_kernel, quads),
        grid=(count,),
        in_specs=in_specs,
        out_specs=out_specs,
        out_shape=out_shape,
        scratch_shapes=[pltpu.VMEM((cols, tokens), BF)],
        compiler_params=params(),
        cost_estimate=cost(11 * count),
        name="attention",
    )(*operands)


def output_kernel(out_ref, back_ref, x0, x1, dy0, dy1, wqkv_ref, wo_ref, *rest):
    first, second, last = rest[:4], rest[4:8], rest[8:12]
    y0, g0, y1, g1, rim_ref, cor_ref, lon_ref, branch_at, g_at = rest[12:]
    levels = y0.shape[1]
    cols = last[0].shape[1]
    step = pl.program_id(1)

    def by_quad(i):
        return [first[i][:, :cols], second[i][...], first[i][:, cols:], last[i][...]]

    branch_at[step] = dot(jnp.concatenate(by_quad(0), axis=1), wo_ref[...]).astype(BF)
    d_all = jnp.concatenate([a for i in (1, 2, 3) for a in by_quad(i)], axis=1)
    g_at[step] = dot_nt(d_all, wqkv_ref[...]).astype(BF)

    def finish(side, x_ref, dy_ref, refs):
        def sample(b, carry):
            at = pl.ds(pl.multiple_of(b * 2 * GROUP, 2 * GROUP), 2 * GROUP)
            joined = lambda ref: jnp.concatenate([ref[n, at] for n in range(QUADS)], axis=1).astype(F32)
            x = x_ref[at, :].astype(F32)
            y = (x + joined(branch_at)).astype(BF)
            g = joined(g_at)
            centred = x - jnp.mean(x, axis=-1, keepdims=True)
            inv = lax.rsqrt(jnp.mean(centred * centred, axis=-1, keepdims=True) + EPS)
            normed = centred * inv
            gx = dy_ref[at, :].astype(F32) + inv * (
                g
                - jnp.mean(g, axis=-1, keepdims=True)
                - normed * jnp.mean(g * normed, axis=-1, keepdims=True)
            )
            for arr, (value, ref) in enumerate(zip((y, gx.astype(BF)), refs)):
                placed = dot(out_ref[...], value).astype(BF)
                back = dot(back_ref[...], value[GROUP:]).astype(BF)
                rim_ref[side, arr, b] = back[:BACK]
                if side == 1:
                    cor_ref[arr, b] = back[BACK:]
                kept = (SIDE if side == 0 else SIDE - SLON) * ROWS
                for level in range(levels):
                    start = level * SIDE * ROWS
                    ref[b, level] = placed[start : start + kept]
                    if side == 1:
                        lon_ref[arr, b, level] = placed[start + kept : start + SIDE * ROWS]
            return carry

        lax.fori_loop(0, HALF // (2 * GROUP), sample, 0)

    ends = step == pl.num_programs(1) - 1

    @pl.when(jnp.logical_and(ends, pl.program_id(0) == 0))
    def _():
        finish(0, x0, dy0, (y0, g0))

    @pl.when(jnp.logical_and(ends, pl.program_id(0) == 1))
    def _():
        finish(1, x1, dy1, (y1, g1))


def outputs(samples, sides, w_qkv, w_out, first, second, last):
    width = w_out.shape[0]
    cols = width // QUADS
    out, back = pick_out(), pick_back()
    full = lambda shape: pl.BlockSpec(shape, lambda s, n: (0,) * len(shape))
    kept = (SIDE - SLON) * ROWS
    shapes = [(samples, LEV, SIDE * ROWS, width)] * 2 + [(samples, LEV, kept, width)] * 2
    shapes += [(2, 2, samples, BACK, width), (2, samples, COR, width)]
    shapes += [(2, samples, LEV, SLON * ROWS, width)]
    return pl.pallas_call(
        output_kernel,
        grid=(2, QUADS),
        in_specs=[full(out.shape), full(back.shape)]
        + [full((HALF, width))] * 4
        + [
            pl.BlockSpec((cols, 3 * width), lambda s, n: (n, 0)),
            pl.BlockSpec((width, cols), lambda s, n: (0, n)),
        ]
        + [pl.BlockSpec((HALF, 2 * cols), lambda s, n: (s, 0))] * 4
        + [pl.BlockSpec((HALF, cols), lambda s, n: (s, 0))] * 8,
        out_specs=[full(s) for s in shapes],
        out_shape=[jax.ShapeDtypeStruct(s, BF) for s in shapes],
        scratch_shapes=[pltpu.VMEM((QUADS, HALF, cols), BF)] * 2,
        compiler_params=params(),
        cost_estimate=cost(18),
        name="outputs",
    )(
        out, back, sides[0][0], sides[1][0], sides[0][1], sides[1][1], w_qkv, w_out,
        *first[:4], *second[:4], *last[:4],
    )


def merge_kernel(place0_ref, place1_ref, placec_ref, y0, g0, y1, g1, rim, cor, lon, y_ref, gx_ref):
    levels = y_ref.shape[1]
    for arr, (low, high, out) in enumerate(((y0, y1, y_ref), (g0, g1, gx_ref))):
        for level in range(levels):
            start = 0
            for mine, pick, strip in (
                (lon[arr, 0, level], placec_ref, cor[arr, 0]),
                (low[0, level], place0_ref, rim[0, arr, 0]),
                (high[0, level], place1_ref, rim[1, arr, 0]),
            ):
                rows = mine.shape[0]
                here = lax.broadcasted_iota(jnp.int32, mine.shape, 0) % ROWS < SLAT
                placed = dot(pick[level], strip).astype(BF)
                out[0, level, start : start + rows] = jnp.where(here, placed, mine)
                start += rows


def merge(y0, g0, y1, g1, rim, cor, lon):
    samples, levels, _, width = y0.shape
    picks = [pick_place(SIDE, 0, BACK), pick_place(SIDE - SLON, SLON, BACK), pick_place(SLON, 0, COR)]
    full = lambda a: pl.BlockSpec(a.shape, lambda b: (0,) * a.ndim)
    own = lambda a: pl.BlockSpec((1,) + a.shape[1:], lambda b: (b,) + (0,) * (a.ndim - 1))
    strip = lambda a: pl.BlockSpec((2, 1) + a.shape[2:], lambda b: (0, b) + (0,) * (a.ndim - 2))
    shape = jax.ShapeDtypeStruct((samples, levels, COLS * ROWS, width), BF)
    return pl.pallas_call(
        merge_kernel,
        grid=(samples,),
        in_specs=[full(a) for a in picks]
        + [own(a) for a in (y0, g0, y1, g1)]
        + [pl.BlockSpec((2, 2, 1) + rim.shape[3:], lambda b: (0, 0, b, 0, 0))]
        + [strip(a) for a in (cor, lon)],
        out_specs=[own(shape)] * 2,
        out_shape=[shape] * 2,
        compiler_params=params(),
        cost_estimate=cost(4),
        name="merge",
    )(*picks, y0, g0, y1, g1, rim, cor, lon)


def shifted(value, axis, steps):
    count = lax.axis_size(axis)
    pairs = [(source, (source + steps) % count) for source in range(count)]
    return lax.ppermute(value, axis, pairs)


def shifted_both(value, steps):
    lon, lat = lax.axis_size("lon"), lax.axis_size("lat")
    pairs = [
        (i * lat + j, ((i + steps) % lon) * lat + (j + steps) % lat)
        for i in range(lon)
        for j in range(lat)
    ]
    return lax.ppermute(value, ("lon", "lat"), pairs)


def allowed_bias(mask_ids):
    lat_total = mask_ids.shape[0]
    start = lax.axis_index("lat") * ROWS + SLAT
    lat_global = (start + np.arange(ROWS, dtype=np.int32)) % lat_total
    wide = jnp.concatenate([mask_ids, mask_ids[:, :SLON]], axis=1)
    wide = jnp.concatenate([wide, wide[:SLAT]], axis=0)
    ids = lax.dynamic_slice(wide, (start, lax.axis_index("lon") * COLS + SLON), (ROWS, COLS))
    code = ids * 2 + (lat_global < SLAT).astype(jnp.int32)[:, None]
    code = code + 16 * (np.arange(COLS, dtype=np.int32) // WLON)[None, :]
    code = code.reshape(2, WLAT, 2, SIDE).transpose(2, 0, 1, 3).reshape(4, 1, WLAT * SIDE)
    code = jnp.broadcast_to(code, (4, LEV, WLAT * SIDE)).reshape(4, -1)
    code = jnp.pad(code, ((0, 0), (0, GROUP - code.shape[1])), constant_values=-1)
    same = code[:, :, None] == code[:, None, :]
    return jnp.where(same, 0.0, -jnp.inf).astype(F32)


def swapped(value, axis):
    return lax.ppermute(value, axis, [(0, 1), (1, 0)])


def to_distance(value, dx=0, dy=0, dz=0):
    pairs = []
    for lon in range(X * Y * Z):
        x, y, z = place_of(lon)
        pairs.append((lon, ((z + dz) % Z * Y + (y + dy) % Y) * X + (x + dx) % X))
    return lax.ppermute(value, "lon", pairs)


def added(*terms):
    total = terms[0].astype(F32)
    for term in terms[1:]:
        total = total + term.astype(F32)
    return total


def ring_sum(chunks, name):
    got = [to_distance(chunks[d], **{name: d}) for d in range(1, len(chunks))]
    return added(chunks[0], *got)


def swap_sum(keep, got):
    return added(keep, got).astype(BF)


def chunks_by_z(total):
    total = total.reshape(X, Z, Y * UNIT, -1)
    return [total[:, d].reshape(X * Y * UNIT, -1) for d in range(Z)]


def chunks_by_x(second, last, outs):
    rows = Z * Y * UNIT
    outs = [o.reshape(X, -1, o.shape[1]) for o in outs]
    return [
        jnp.concatenate(
            [
                second[d * rows : (d + 1) * rows],
                last[d * rows : (d + 1) * rows],
                jnp.concatenate([o[d] for o in outs], axis=0),
            ],
            axis=1,
        )
        for d in range(X)
    ]


def final_chunks_by_z(total, split):
    qkv = total[:, :split].reshape(Z, Y * UNIT, split)
    out = total[:, split:].reshape(Z, Y, UNIT, -1)
    _, y0, z0 = place_of(lax.axis_index("lon"))
    out = jnp.where(y0 == 0, out, out[:, ::-1]).reshape(Z, Y * UNIT, -1)
    return [
        jnp.concatenate([qkv[d], lax.dynamic_index_in_dim(out, (z0 + d) % Z, keepdims=False)], axis=1)
        for d in range(Z)
    ]


def final_sums(total):
    cols = total.shape[1] // 8
    piece = [total[:, i * cols : (i + 1) * cols] for i in range(8)]
    pick = lambda *which: jnp.concatenate([piece[i] for i in which], axis=1)
    lat0 = lax.axis_index("lat") == 0
    low = jnp.where(lat0, pick(0, 3, 1, 6), pick(2, 5, 0, 6))
    high = jnp.where(lat0, pick(4, 2, 5, 7), pick(3, 1, 4, 7))
    dp0 = lax.axis_index("dp") == 0
    got = swapped(jnp.where(dp0, high, low), "dp")
    total = added(jnp.where(dp0, low, high), got)
    return total[:, : 3 * cols], total[:, 3 * cols :]


def per_device(fields, grad_y, w_qkv, w_out, mask_ids):
    samples, levels, lat_rows, lon_cols, width = fields.shape
    flat = lambda a: a.transpose(0, 1, 3, 2, 4).reshape(samples, levels, lon_cols * lat_rows, width)
    f, g = flat(fields), flat(grad_y)
    pos = jnp.stack([lax.axis_index("lon"), lax.axis_index("lat")]).astype(jnp.int32)
    lon_out, rim_out, cor_out = strips(f, g)
    rim_in = shifted(rim_out, "lat", -1)
    cor_in = shifted_both(cor_out, -1)
    lon_in = shifted(lon_out, "lon", -1)
    bias = allowed_bias(mask_ids)
    side0 = project(0, pos, f, g, lon_out, rim_in, cor_out, w_qkv, w_out)
    side1 = project(1, pos, f, g, lon_in, rim_in, cor_in, w_qkv, w_out)
    sides = (side0, side1)
    first = attention((0, 2), pos, bias, sides)
    got, got_out = swapped(first[5], "lat"), swapped(first[7], "lat")
    pos1, att = lax.optimization_barrier((pos, first[0]))
    first = (att, *first[1:])
    second = attention((1,), pos1, bias, sides)
    got, got_out, before = lax.optimization_barrier((got, got_out, second[6]))
    by_z = chunks_by_z(swap_sum(first[4], got))
    outs = swap_sum(first[6], got_out)
    by_z, before = lax.optimization_barrier((by_z, before))
    got_z = [to_distance(by_z[d], dz=d) for d in range(1, Z)]
    last = attention((3,), pos, bias, sides, before=before)
    got_z, sends = lax.optimization_barrier((got_z, (second[5], last[5])))
    by_z = added(by_z[0], *got_z).astype(BF).reshape(X, Y * UNIT, -1)
    got_first = [to_distance(by_z[d], dx=d) for d in range(1, X)]
    got, got_last = [swapped(send, "lat") for send in sends]
    total = swap_sum(second[4], got)
    cols = total.shape[1]
    out = jnp.concatenate([total[-2 * cols : -cols], total[-cols:]], axis=1)
    total_last = swap_sum(last[4], got_last)
    outs = [outs[:cols], out, outs[cols:], total_last[-cols:]]
    by_x = chunks_by_x(total[: -2 * cols], total_last[:-cols], outs)
    by_x, att, got_first = lax.optimization_barrier((by_x, last[0], got_first))
    first_total = added(by_z[0], *got_first).astype(BF)
    got_x = [to_distance(by_x[d], dx=d) for d in range(1, X)]
    y0, g0, y1, g1, rim, cor, lon = outputs(
        samples, sides, w_qkv, w_out, first, second, (att, *last[1:])
    )
    got_x, rim, cor, lon = lax.optimization_barrier((got_x, rim, cor, lon))
    lon = shifted(lon, "lon", 1)
    cor = shifted_both(cor, 1)
    rim = shifted(rim, "lat", 1)
    total = added(by_x[0], *got_x).astype(BF)
    chunks = final_chunks_by_z(total, 3 * cols)
    chunks[2], rim, cor = lax.optimization_barrier((chunks[2], rim, cor))
    total = ring_sum(chunks, "dz").astype(BF)
    total = jnp.concatenate([first_total, total], axis=1).reshape(Y, UNIT, -1)
    got_y = to_distance(total[1], dy=1)
    y, gx = merge(y0, g0, y1, g1, rim, cor, lon)
    got_y, y, gx = lax.optimization_barrier((got_y, y, gx))
    sums = final_sums(added(total[0], got_y).astype(BF))
    unflat = lambda a: a.reshape(samples, levels, lon_cols, lat_rows, width).transpose(0, 1, 3, 2, 4)
    return (unflat(y), unflat(gx), *sums)


def solution(mesh):
    grid = P("dp", None, "lat", "lon", None)
    return jax.shard_map(
        per_device,
        mesh=mesh,
        in_specs=(grid, grid, P(), P(), P()),
        out_specs=(grid, grid, P("lon", ("lat", "dp")), P("lon", ("lat", "dp"))),
        check_vma=False,
    )
```

```python
import functools

import jax
import jax.numpy as jnp
import numpy as np
from jax import lax
from jax.experimental import pallas as pl
from jax.experimental.pallas import tpu as pltpu
from jax.sharding import PartitionSpec as P

HEADS = 16
LEV = 3
WLAT = 4
WLON = 5
SLAT = 2
SLON = 2
ROWS = 8
COLS = 20
EPS = 1e-05

SIDE = 2 * WLON
GROUP = 128
HALF = 4 * GROUP
OWN = LEV * SIDE * ROWS
RIM = 128
COR = 16
BACK = 64
QUADS = 4
SCALE = 0.125
BF = jnp.bfloat16
F32 = jnp.float32
NT = (((1,), (1,)), ((), ()))

X, Y, Z = 4, 2, 4
UNIT = 32
LON, LAT = 0, 1


def params(mebibytes):
    return pltpu.CompilerParams(vmem_limit_bytes=mebibytes * 1024 * 1024)


def cost(micros):
    return pl.CostEstimate(flops=int(micros * 1.1e9), bytes_accessed=10**6, transcendentals=0)


SCALARS = pl.BlockSpec(memory_space=pltpu.SMEM)
WHOLE = pl.BlockSpec(memory_space=pltpu.VMEM)


def dot(a, b):
    return jnp.dot(a, b, preferred_element_type=F32)


def dot_nt(a, b):
    return lax.dot_general(a, b, NT, preferred_element_type=F32)


def place_of(lon):
    return lon % X, (lon // X) % Y, lon // (X * Y)


def relative(block, pos_ref):
    lon = pos_ref[LON]
    x, y, z = place_of(block)
    x0, y0, z0 = lax.rem(lon, X), lax.rem(lax.div(lon, X), Y), lax.div(lon, X * Y)
    dx, dy, dz = lax.rem(x - x0 + X, X), lax.rem(y - y0 + Y, Y), lax.rem(z - z0 + Z, Z)
    return (dx * Z + dz) * Y + dy


def token(level, r, c):
    return (level * WLAT + r) * SIDE + c


def every():
    for level in range(LEV):
        for c in range(SIDE):
            for i in range(ROWS):
                wr, r = divmod((i - SLAT) % ROWS, WLAT)
                yield level, c, i, wr, r


def one_hot(shape, places):
    out = np.zeros(shape, np.float32)
    for at in places:
        out[at] = 1.0
    return jnp.asarray(out.astype(jnp.bfloat16))


def pick_own():
    return one_hot(
        (2, GROUP, OWN),
        [
            (wr, token(level, r, c), (level * SIDE + c) * ROWS + i)
            for level, c, i, wr, r in every()
            if i >= SLAT
        ],
    )


def pick_rim(side):
    places = []
    for level, c, i, wr, r in every():
        if i < SLAT:
            column = SLON + side * SIDE + c
            if column < COLS:
                src = (level * COLS + column) * SLAT + i
            else:
                src = RIM + (level * SLON + column - COLS) * SLAT + i
            places.append((token(level, r, c), src))
    return one_hot((GROUP, RIM + COR), places)


def pick_out():
    return one_hot(
        (OWN, 2 * GROUP),
        [
            ((level * SIDE + c) * ROWS + i, wr * GROUP + token(level, r, c))
            for level, c, i, wr, r in every()
        ],
    )


def pick_back():
    return one_hot(
        (BACK + COR, GROUP),
        [
            ((level * SIDE + c) * SLAT + i, token(level, r, c))
            for level, c, i, wr, r in every()
            if i < SLAT
        ]
        + [
            (BACK + (level * SLON + c - SIDE + SLON) * SLAT + i, token(level, r, c))
            for level, c, i, wr, r in every()
            if i < SLAT and c >= SIDE - SLON
        ],
    )


def pick_strip():
    rim = [
        ((level * COLS + column) * SLAT + i, (level * COLS + column) * ROWS + i)
        for level in range(LEV)
        for column in range(COLS)
        for i in range(SLAT)
    ]
    cor = [
        (RIM + (level * SLON + column) * SLAT + i, (level * COLS + column) * ROWS + i)
        for level in range(LEV)
        for column in range(SLON)
        for i in range(SLAT)
    ]
    return one_hot((RIM + COR, LEV * COLS * ROWS), rim + cor)


def pick_place(columns, offset, height):
    return one_hot(
        (LEV, columns * ROWS, height),
        [
            (level, c * ROWS + i, (level * (columns + offset) + c) * SLAT + i)
            for level in range(LEV)
            for c in range(columns)
            for i in range(SLAT)
        ],
    )


def strips_kernel(pick_ref, f_ref, g_ref, lon_ref, rim_ref, cor_ref):
    for arr, ref in enumerate((f_ref, g_ref)):
        block = ref[0]
        lon_ref[arr, 0] = block[:, : SLON * ROWS]
        strip = dot(pick_ref[...], block.reshape(-1, block.shape[-1])).astype(BF)
        rim_ref[arr, 0] = strip[:RIM]
        cor_ref[arr, 0] = strip[RIM:]


def strips(f, g):
    samples, levels, rows, width = f.shape
    pick = pick_strip()
    block = pl.BlockSpec((1, levels, rows, width), lambda b: (b, 0, 0, 0))
    shapes = [(levels, SLON * ROWS, width), (RIM, width), (COR, width)]
    return pl.pallas_call(
        strips_kernel,
        grid=(samples,),
        in_specs=[pl.BlockSpec(pick.shape, lambda b: (0, 0)), block, block],
        out_specs=[
            pl.BlockSpec((2, 1) + s, lambda b, n=len(s): (0, b) + (0,) * n) for s in shapes
        ],
        out_shape=[jax.ShapeDtypeStruct((2, samples) + s, BF) for s in shapes],
        compiler_params=params(16),
        cost_estimate=cost(3),
        name="strips",
    )(pick, f, g)


def project_kernel(
    side, pos_ref, own_ref, pick_ref, f_ref, g_ref, lon_ref, rim_ref, cor_ref, w_ref, wo_ref,
    xw_ref, gw_ref, nt_ref, q_ref, k_ref, v_ref, da_ref, nw,
):
    samples, levels, _, width = f_ref.shape
    cols = width // QUADS
    for b in range(samples):
        got = []
        for arr, ref in enumerate((f_ref, g_ref)):
            parts = []
            for level in range(levels):
                if side == 0:
                    parts.append(ref[b, level, SLON * ROWS : (SLON + SIDE) * ROWS])
                else:
                    parts.append(ref[b, level, (SLON + SIDE) * ROWS :])
                    parts.append(lon_ref[arr, b, level])
            own = jnp.concatenate(parts, axis=0)
            rim = jnp.concatenate([rim_ref[arr, b], cor_ref[arr, b]], axis=0)
            got.append((own, rim))
        for wr in range(2):
            at = slice((b * 2 + wr) * GROUP, (b * 2 + wr + 1) * GROUP)
            x, g = (dot(own_ref[wr], own) for own, _ in got)
            if wr == 1:
                x, g = (a + dot(pick_ref[...], rim) for a, (_, rim) in zip((x, g), got))
            gw_ref[at, :] = g.astype(BF)
            xw_ref[at, :] = x.astype(BF)
            centred = x - jnp.mean(x, axis=-1, keepdims=True)
            inv = lax.rsqrt(jnp.mean(centred * centred, axis=-1, keepdims=True) + EPS)
            normed = (centred * inv).astype(BF)
            nw[at, :] = normed
            turned = normed.T
            for block in range(width // UNIT):
                dst = pl.multiple_of(relative(block, pos_ref) * UNIT, UNIT)
                nt_ref[pl.ds(dst, UNIT), at] = turned[block * UNIT : (block + 1) * UNIT]

    def quad(n, carry):
        at = pl.ds(pl.multiple_of(n * cols, cols), cols)
        for i, ref in enumerate((q_ref, k_ref, v_ref)):
            part = pl.ds(pl.multiple_of(i * width + n * cols, cols), cols)
            ref[:, at] = dot(nw[...], w_ref[:, part]).astype(BF)
        da_ref[:, at] = dot_nt(gw_ref[...], wo_ref[at, :]).astype(BF)
        return carry

    lax.fori_loop(0, QUADS, quad, 0)


def project(side, pos, f, g, lon_in, rim_in, cor_in, w_qkv, w_out):
    width = f.shape[-1]
    own, pick = pick_own(), pick_rim(side)
    tall = jax.ShapeDtypeStruct((HALF, width), BF)
    operands = (pos, own, pick, f, g, lon_in, rim_in, cor_in, w_qkv, w_out)
    return pl.pallas_call(
        functools.partial(project_kernel, side),
        in_specs=[SCALARS] + [WHOLE] * (len(operands) - 1),
        out_specs=[WHOLE] * 7,
        out_shape=[tall, tall, jax.ShapeDtypeStruct((width, HALF), BF)] + [tall] * 4,
        scratch_shapes=[pltpu.VMEM((HALF, width), BF)],
        compiler_params=params(26),
        cost_estimate=cost(9),
        name="project",
    )(*operands)


def attention_kernel(quads, pos_ref, bias_ref, *rest):
    sides, rest = (rest[:6], rest[6:12]), rest[12:]
    if quads == (3,):
        kin_ref, rest = rest[0], rest[1:]
    if quads == (1,):
        att_ref, dq_ref, dk_ref, dv_ref, keep_ref, send_ref, kout_ref, att_t = rest
    elif quads == (3,):
        att_ref, dq_ref, dk_ref, dv_ref, keep_ref, send_ref, att_t = rest
    else:
        att_ref, dq_ref, dk_ref, dv_ref, keep_ref, send_ref, gok_ref, gos_ref, att_t = rest
    width = sides[0][0].shape[0]
    cols = width // QUADS
    head = 64
    lat0 = pos_ref[LAT] == 0
    x0 = lax.rem(pos_ref[LON], X)
    first = lax.broadcasted_iota(jnp.int32, (GROUP, 2 * head), 1) < head
    upper = lax.broadcasted_iota(jnp.int32, (2 * head, GROUP), 0) < head
    zero = jnp.zeros((GROUP, 2 * head), BF)

    def split(pair):
        return jnp.concatenate([jnp.where(first, pair, zero), jnp.where(first, zero, pair)], axis=0)

    def beside(turned):
        return jnp.concatenate(
            [jnp.where(upper, turned, zero), jnp.where(upper, zero, turned)], axis=1
        )

    def stacked(both):
        return jnp.concatenate([both[:, :GROUP], both[:, GROUP:]], axis=0)

    def lanes(start, size):
        return pl.ds(start if isinstance(start, int) else pl.multiple_of(start, 128), size)

    def unit(refs, side, group, wr, pair, src, dst):
        _, _, q_ref, k_ref, v_ref, da_ref = refs
        at = (pl.ds(pl.multiple_of(group * GROUP, GROUP), GROUP), lanes(src + pair * 128, 128))
        here = pl.ds(pl.multiple_of(side * HALF + group * GROUP, GROUP), GROUP)
        both = lanes(dst + pair * 128, 128)
        bias = bias_ref[side * 2 + wr]
        q, k, v, da = q_ref[at], k_ref[at], v_ref[at], da_ref[at]
        q2, da2 = split(q * SCALE), split(da)
        scores = dot_nt(k, q2)
        d_prob = dot_nt(v, da2)
        yield
        scores = scores + jnp.concatenate([bias, bias], axis=1)
        top = jnp.max(scores, axis=0, keepdims=True)
        expd = jnp.exp(scores - top)
        prob = expd * (1.0 / jnp.sum(expd, axis=0, keepdims=True))
        prob16 = prob.astype(BF)
        part = prob * d_prob
        delta = jnp.sum(part, axis=0, keepdims=True)
        d_score = (part - prob * delta).astype(BF)
        yield
        out_t = dot(beside(v.T), stacked(prob16)).astype(BF)
        dq_t = dot(beside((k * SCALE).T), stacked(d_score)).astype(BF)
        dv_ref[here, both] = dot(prob16, da2).astype(BF)
        dk_ref[here, both] = dot(d_score, q2).astype(BF)
        yield
        att_ref[here, both] = out_t.T
        for block in range(128 // UNIT):
            row = lax.rem(block - x0 + X, X) * (2 * UNIT) + pair * UNIT
            att_t[pl.ds(pl.multiple_of(row, UNIT), UNIT), here] = out_t[
                block * UNIT : (block + 1) * UNIT
            ]
        dq_ref[here, both] = dq_t.T
        yield

    low, high = slice(0, HALF), slice(HALF, 2 * HALF)

    def units(src, dst):
        for side in range(2):

            def sample(b, carry):
                works = [
                    unit(sides[side], side, b * 2 + wr, wr, pair, src, dst)
                    for wr in range(2)
                    for pair in range(2)
                ]
                for _ in range(4):
                    for work in works:
                        next(work)
                return carry

            lax.fori_loop(0, HALF // (2 * GROUP), sample, 0)

    def out_sums():
        grad_out = dot(att_t[:, low], sides[0][1][...]) + dot(att_t[:, high], sides[1][1][...])
        left, right = grad_out[:, : width // 2], grad_out[:, width // 2 :]
        return jnp.where(lat0, left, right).astype(BF), jnp.where(lat0, right, left).astype(BF)

    def qkv_sums(store, dst):
        def piece(i, carry):
            at = pl.ds(pl.multiple_of(i * 256, 256), 256)
            left = (sides[0][0][at, :], sides[1][0][at, :])
            of_q, of_k, of_v = (
                dot(left[0], ref[low, lanes(dst, cols)]) + dot(left[1], ref[high, lanes(dst, cols)])
                for ref in (dq_ref, dk_ref, dv_ref)
            )
            mine = jnp.where(lat0, of_q, of_v).astype(BF)
            other = jnp.where(lat0, of_v, of_q).astype(BF)
            store(at, mine, other, of_k.astype(BF))
            return carry

        lax.fori_loop(0, width // 256, piece, 0)

    if quads == (0, 2):

        def turn(n, carry):
            dst = n * cols
            units(n * 2 * cols, dst)
            rows = pl.ds(pl.multiple_of(n * cols, cols), cols)
            gok_ref[rows, :], gos_ref[rows, :] = out_sums()
            stays = jnp.logical_xor(lat0, n == 1)

            def store(at, mine, other, of_k):
                keep_ref[at, lanes(dst, cols)] = mine
                send_ref[at, lanes(dst, cols)] = other

                @pl.when(stays)
                def _():
                    keep_ref[at, 2 * cols :] = of_k

                @pl.when(jnp.logical_not(stays))
                def _():
                    send_ref[at, 2 * cols :] = of_k

            qkv_sums(store, dst)
            return carry

        lax.fori_loop(0, 2, turn, 0)
        return

    units(quads[0] * cols, 0)
    mine, other = out_sums()
    if quads == (1,):
        for half in range(2):
            below = slice(width + half * cols, width + (half + 1) * cols)
            keep_ref[below, :] = mine[:, half * cols : (half + 1) * cols]
            send_ref[below, :] = other[:, half * cols : (half + 1) * cols]
    else:
        keep_ref[width:, :] = mine
        send_ref[width:, :] = other

    def store(at, mine, other, of_k):
        keep_ref[at, :cols] = mine
        send_ref[at, :cols] = other
        if quads == (1,):
            kout_ref[at, :] = of_k
        else:
            before = kin_ref[at, :]
            keep_ref[at, cols:] = jnp.where(lat0, before, of_k)
            send_ref[at, cols:] = jnp.where(lat0, of_k, before)

    qkv_sums(store, 0)


def attention(quads, pos, bias, sides, before=None):
    width = sides[0][0].shape[1]
    cols = width // QUADS
    count = len(quads)
    operands = [pos, bias] + [a for side in sides for a in side[1:]]
    for side in range(2):
        at = 2 + side * 6
        operands[at], operands[at + 1] = operands[at + 1], operands[at]
    if before is not None:
        operands.append(before)
    shapes = [(2 * HALF, count * cols)] * 4
    shapes += [{0: (width, 3 * cols), 1: (width + 2 * cols, cols), 3: (width + cols, 2 * cols)}[quads[0]]] * 2
    if quads == (0, 2):
        shapes += [(count * cols, width // 2)] * 2
    elif quads == (1,):
        shapes += [(width, cols)]
    return pl.pallas_call(
        functools.partial(attention_kernel, quads),
        in_specs=[SCALARS] + [WHOLE] * (len(operands) - 1),
        out_specs=[WHOLE] * len(shapes),
        out_shape=[jax.ShapeDtypeStruct(s, BF) for s in shapes],
        scratch_shapes=[pltpu.VMEM((cols, 2 * HALF), BF)],
        compiler_params=params(28),
        cost_estimate=cost(11 * count),
        name="attention",
    )(*operands)


def output_kernel(side, out_ref, back_ref, x_ref, dy_ref, wqkv_ref, wo_ref, *rest):
    first, second, last = rest[:4], rest[4:8], rest[8:12]
    if side == 0:
        y_ref, gx_ref, rim_ref, branch_at, g_at = rest[12:]
    else:
        y_ref, gx_ref, rim_ref, cor_ref, lon_ref, branch_at, g_at = rest[12:]
    levels = y_ref.shape[1]
    cols = last[0].shape[1]
    step = pl.program_id(0)

    def by_quad(i):
        return [first[i][:, :cols], second[i][...], first[i][:, cols:], last[i][...]]

    branch_at[step] = dot(jnp.concatenate(by_quad(0), axis=1), wo_ref[...]).astype(BF)
    d_all = jnp.concatenate([a for i in (1, 2, 3) for a in by_quad(i)], axis=1)
    g_at[step] = dot_nt(d_all, wqkv_ref[...]).astype(BF)

    @pl.when(step == pl.num_programs(0) - 1)
    def _():
        def sample(b, carry):
            at = pl.ds(pl.multiple_of(b * 2 * GROUP, 2 * GROUP), 2 * GROUP)
            joined = lambda ref: jnp.concatenate([ref[n, at] for n in range(QUADS)], axis=1).astype(F32)
            x = x_ref[at, :].astype(F32)
            y = (x + joined(branch_at)).astype(BF)
            g = joined(g_at)
            centred = x - jnp.mean(x, axis=-1, keepdims=True)
            inv = lax.rsqrt(jnp.mean(centred * centred, axis=-1, keepdims=True) + EPS)
            normed = centred * inv
            gx = dy_ref[at, :].astype(F32) + inv * (
                g
                - jnp.mean(g, axis=-1, keepdims=True)
                - normed * jnp.mean(g * normed, axis=-1, keepdims=True)
            )
            for arr, (value, ref) in enumerate(((y, y_ref), (gx.astype(BF), gx_ref))):
                placed = dot(out_ref[...], value).astype(BF)
                back = dot(back_ref[...], value[GROUP:]).astype(BF)
                rim_ref[arr, b] = back[:BACK]
                if side == 1:
                    cor_ref[arr, b] = back[BACK:]
                kept = (SIDE if side == 0 else SIDE - SLON) * ROWS
                for level in range(levels):
                    start = level * SIDE * ROWS
                    ref[b, level] = placed[start : start + kept]
                    if side == 1:
                        lon_ref[arr, b, level] = placed[start + kept : start + SIDE * ROWS]
            return carry

        lax.fori_loop(0, HALF // (2 * GROUP), sample, 0)


def outputs(side, samples, xw, gw, w_qkv, w_out, first, second, last):
    width = w_out.shape[0]
    cols = width // QUADS
    out, back = pick_out(), pick_back()
    full = lambda shape: pl.BlockSpec(shape, lambda n: (0,) * len(shape))
    kept = (SIDE if side == 0 else SIDE - SLON) * ROWS
    shapes = [(samples, LEV, kept, width)] * 2 + [(2, samples, BACK, width)]
    if side == 1:
        shapes += [(2, samples, COR, width), (2, samples, LEV, SLON * ROWS, width)]
    return pl.pallas_call(
        functools.partial(output_kernel, side),
        grid=(QUADS,),
        in_specs=[full(a.shape) for a in (out, back, xw, gw)]
        + [
            pl.BlockSpec((cols, 3 * width), lambda n: (n, 0)),
            pl.BlockSpec((width, cols), lambda n: (0, n)),
        ]
        + [pl.BlockSpec((HALF, 2 * cols), lambda n: (side, 0))] * 4
        + [pl.BlockSpec((HALF, cols), lambda n: (side, 0))] * 8,
        out_specs=[full(s) for s in shapes],
        out_shape=[jax.ShapeDtypeStruct(s, BF) for s in shapes],
        scratch_shapes=[pltpu.VMEM((QUADS, HALF, cols), BF)] * 2,
        compiler_params=params(24),
        cost_estimate=cost(8),
        name="outputs",
    )(out, back, xw, gw, w_qkv, w_out, *first[:4], *second[:4], *last[:4])


def merge_kernel(place0_ref, place1_ref, placec_ref, y0, g0, y1, g1, rim0, rim1, cor, lon, y_ref, gx_ref):
    levels = y_ref.shape[1]
    for arr, (low, high, out) in enumerate(((y0, y1, y_ref), (g0, g1, gx_ref))):
        for level in range(levels):
            start = 0
            for mine, pick, strip in (
                (lon[arr, 0, level], placec_ref, cor[arr, 0]),
                (low[0, level], place0_ref, rim0[arr, 0]),
                (high[0, level], place1_ref, rim1[arr, 0]),
            ):
                rows = mine.shape[0]
                here = lax.broadcasted_iota(jnp.int32, mine.shape, 0) % ROWS < SLAT
                placed = dot(pick[level], strip).astype(BF)
                out[0, level, start : start + rows] = jnp.where(here, placed, mine)
                start += rows


def merge(y0, g0, y1, g1, rim0, rim1, cor, lon):
    samples, levels, _, width = y0.shape
    picks = [pick_place(SIDE, 0, BACK), pick_place(SIDE - SLON, SLON, BACK), pick_place(SLON, 0, COR)]
    full = lambda a: pl.BlockSpec(a.shape, lambda b: (0,) * a.ndim)
    own = lambda a: pl.BlockSpec((1,) + a.shape[1:], lambda b: (b,) + (0,) * (a.ndim - 1))
    strip = lambda a: pl.BlockSpec((2, 1) + a.shape[2:], lambda b: (0, b) + (0,) * (a.ndim - 2))
    shape = jax.ShapeDtypeStruct((samples, levels, COLS * ROWS, width), BF)
    return pl.pallas_call(
        merge_kernel,
        grid=(samples,),
        in_specs=[full(a) for a in picks]
        + [own(a) for a in (y0, g0, y1, g1)]
        + [strip(a) for a in (rim0, rim1, cor, lon)],
        out_specs=[own(shape)] * 2,
        out_shape=[shape] * 2,
        compiler_params=params(16),
        cost_estimate=cost(4),
        name="merge",
    )(*picks, y0, g0, y1, g1, rim0, rim1, cor, lon)


def shifted(value, axis, steps):
    count = lax.axis_size(axis)
    pairs = [(source, (source + steps) % count) for source in range(count)]
    return lax.ppermute(value, axis, pairs)


def shifted_both(value, steps):
    lon, lat = lax.axis_size("lon"), lax.axis_size("lat")
    pairs = [
        (i * lat + j, ((i + steps) % lon) * lat + (j + steps) % lat)
        for i in range(lon)
        for j in range(lat)
    ]
    return lax.ppermute(value, ("lon", "lat"), pairs)


def allowed_bias(mask_ids):
    lat_total = mask_ids.shape[0]
    start = lax.axis_index("lat") * ROWS + SLAT
    lat_global = (start + np.arange(ROWS, dtype=np.int32)) % lat_total
    wide = jnp.concatenate([mask_ids, mask_ids[:, :SLON]], axis=1)
    wide = jnp.concatenate([wide, wide[:SLAT]], axis=0)
    ids = lax.dynamic_slice(wide, (start, lax.axis_index("lon") * COLS + SLON), (ROWS, COLS))
    code = ids * 2 + (lat_global < SLAT).astype(jnp.int32)[:, None]
    code = code + 16 * (np.arange(COLS, dtype=np.int32) // WLON)[None, :]
    code = code.reshape(2, WLAT, 2, SIDE).transpose(2, 0, 1, 3).reshape(4, 1, WLAT * SIDE)
    code = jnp.broadcast_to(code, (4, LEV, WLAT * SIDE)).reshape(4, -1)
    code = jnp.pad(code, ((0, 0), (0, GROUP - code.shape[1])), constant_values=-1)
    same = code[:, :, None] == code[:, None, :]
    return jnp.where(same, 0.0, -jnp.inf).astype(F32)


def swapped(value, axis):
    return lax.ppermute(value, axis, [(0, 1), (1, 0)])


def to_distance(value, dx=0, dy=0, dz=0):
    pairs = []
    for lon in range(X * Y * Z):
        x, y, z = place_of(lon)
        pairs.append((lon, ((z + dz) % Z * Y + (y + dy) % Y) * X + (x + dx) % X))
    return lax.ppermute(value, "lon", pairs)


def added(*terms):
    total = terms[0].astype(F32)
    for term in terms[1:]:
        total = total + term.astype(F32)
    return total


def ring_sum(chunks, name):
    got = [to_distance(chunks[d], **{name: d}) for d in range(1, len(chunks))]
    return added(chunks[0], *got)


def relay(chunks, name):
    half = chunks[2].shape[0] // 2
    return [to_distance(chunks[2][:half], **{name: 1}), to_distance(chunks[2][half:], **{name: 3})]


def with_relayed(chunks, got):
    half = got[0].shape[0]
    up = jnp.concatenate([added(chunks[1][:half], got[0]).astype(BF), chunks[1][half:]], axis=0)
    down = jnp.concatenate([chunks[3][:half], added(chunks[3][half:], got[1]).astype(BF)], axis=0)
    return [up, down]


def both_ways(pair, name):
    return [to_distance(pair[0], **{name: 1}), to_distance(pair[1], **{name: 3})]


def swap_sum(keep, got):
    return added(keep, got).astype(BF)


def chunks_by_z(total):
    total = total.reshape(X, Z, Y * UNIT, -1)
    return [total[:, d].reshape(X * Y * UNIT, -1) for d in range(Z)]


def chunks_by_x(qkv, outs):
    rows = Z * Y * UNIT
    outs = [o.reshape(X, -1, o.shape[1]) for o in outs]
    return [
        jnp.concatenate(
            [qkv[d * rows : (d + 1) * rows], jnp.concatenate([o[d] for o in outs], axis=0)], axis=1
        )
        for d in range(X)
    ]


def final_chunks_by_z(total, split):
    qkv = total[:, :split].reshape(Z, Y * UNIT, split)
    out = total[:, split:].reshape(Z, Y, UNIT, -1)
    _, y0, z0 = place_of(lax.axis_index("lon"))
    out = jnp.where(y0 == 0, out, out[:, ::-1]).reshape(Z, Y * UNIT, -1)
    return [
        jnp.concatenate([qkv[d], lax.dynamic_index_in_dim(out, (z0 + d) % Z, keepdims=False)], axis=1)
        for d in range(Z)
    ]


def final_sums(total):
    cols = total.shape[1] // 8
    piece = [total[:, i * cols : (i + 1) * cols] for i in range(8)]
    pick = lambda *which: jnp.concatenate([piece[i] for i in which], axis=1)
    lat0 = lax.axis_index("lat") == 0
    low = jnp.where(lat0, pick(0, 5, 1, 6), pick(2, 4, 0, 6))
    high = jnp.where(lat0, pick(3, 2, 4, 7), pick(5, 1, 3, 7))
    dp0 = lax.axis_index("dp") == 0
    got = swapped(jnp.where(dp0, high, low), "dp")
    total = added(jnp.where(dp0, low, high), got)
    return total[:, : 3 * cols], total[:, 3 * cols :]


def per_device(fields, grad_y, w_qkv, w_out, mask_ids):
    samples, levels, lat_rows, lon_cols, width = fields.shape
    flat = lambda a: a.transpose(0, 1, 3, 2, 4).reshape(samples, levels, lon_cols * lat_rows, width)
    f, g = flat(fields), flat(grad_y)
    pos = jnp.stack([lax.axis_index("lon"), lax.axis_index("lat")]).astype(jnp.int32)
    lon_out, rim_out, cor_out = strips(f, g)
    rim_in = shifted(rim_out, "lat", -1)
    cor_in = shifted_both(cor_out, -1)
    lon_in = shifted(lon_out, "lon", -1)
    bias = allowed_bias(mask_ids)
    side0 = project(0, pos, f, g, lon_out, rim_in, cor_out, w_qkv, w_out)
    side1 = project(1, pos, f, g, lon_in, rim_in, cor_in, w_qkv, w_out)
    sides = (side0, side1)
    barrier = lax.optimization_barrier
    first = attention((0, 2), pos, bias, sides)
    by_z = chunks_by_z(swap_sum(first[4], swapped(first[5], "lat")))
    outs = swap_sum(first[6], swapped(first[7], "lat"))
    by_z, pos1 = barrier((by_z, pos))
    got_z = relay(by_z, "dz")
    second = attention((1,), pos1, bias, sides)
    got_z, before, send = barrier((got_z, second[6], second[5]))
    ways, before = barrier((with_relayed(by_z, got_z), before))
    got_z = both_ways(ways, "dz")
    last = attention((3,), pos, bias, sides, before=before)
    got_z, send, send_last = barrier((got_z, send, last[5]))
    first_total = added(by_z[0], *got_z).astype(BF).reshape(X, Y * UNIT, -1)
    got, got_last = swapped(send, "lat"), swapped(send_last, "lat")
    total = swap_sum(second[4], got)
    cols = total.shape[1]
    out = jnp.concatenate([total[-2 * cols : -cols], total[-cols:]], axis=1)
    total_last = swap_sum(last[4], got_last)
    outs = [outs[:cols], out, outs[cols:], total_last[-cols:]]
    by_x, by_z = chunks_by_x(total[: -2 * cols], outs), chunks_by_z(total_last[:-cols])
    by_x, by_z, att = barrier((by_x, by_z, last[0]))
    got_x, got_z = relay(by_x, "dx"), relay(by_z, "dz")
    last = (att, *last[1:])
    y1, g1, rim1, cor, lon = outputs(1, samples, *side1[:2], w_qkv, w_out, first, second, last)
    got_x, got_z, lon, cor, rim1 = barrier((got_x, got_z, lon, cor, rim1))
    ways_x, ways_z = with_relayed(by_x, got_x), with_relayed(by_z, got_z)
    ways_x, ways_z, lon, xw0 = barrier((ways_x, ways_z, lon, side0[0]))
    got_x, got_z = both_ways(ways_x, "dx"), both_ways(ways_z, "dz")
    lon = shifted(lon, "lon", 1)
    y0, g0, rim0 = outputs(0, samples, xw0, side0[1], w_qkv, w_out, first, second, last)
    got_x, got_z, rim0, rim1, cor = barrier((got_x, got_z, rim0, rim1, cor))
    cor = shifted_both(cor, 1)
    rim1, rim0 = shifted(rim1, "lat", 1), shifted(rim0, "lat", 1)
    total_x = added(by_x[0], *got_x).astype(BF)
    total_z = added(by_z[0], *got_z).astype(BF).reshape(X, Y * UNIT, -1)
    by_z = final_chunks_by_z(total_x, cols)
    by_x = [jnp.concatenate([first_total[d], total_z[d]], axis=1) for d in range(X)]
    total = jnp.concatenate(
        [ring_sum(by_x, "dx").astype(BF), ring_sum(by_z, "dz").astype(BF)], axis=1
    ).reshape(Y, UNIT, -1)
    got_y = to_distance(total[1], dy=1)
    y, gx = merge(y0, g0, y1, g1, rim0, rim1, cor, lon)
    got_y, y, gx = barrier((got_y, y, gx))
    sums = final_sums(added(total[0], got_y).astype(BF))
    unflat = lambda a: a.reshape(samples, levels, lon_cols, lat_rows, width).transpose(0, 1, 3, 2, 4)
    return (unflat(y), unflat(gx), *sums)


def solution(mesh):
    grid = P("dp", None, "lat", "lon", None)
    return jax.shard_map(
        per_device,
        mesh=mesh,
        in_specs=(grid, grid, P(), P(), P()),
        out_specs=(grid, grid, P("lon", ("lat", "dp")), P("lon", ("lat", "dp"))),
        check_vma=False,
    )
```

```python
import functools

import jax
import jax.numpy as jnp
import numpy as np
from jax import lax
from jax.experimental import pallas as pl
from jax.experimental.pallas import tpu as pltpu
from jax.sharding import PartitionSpec as P

HEADS = 16
LEV = 3
WLAT = 4
WLON = 5
SLAT = 2
SLON = 2
ROWS = 8
COLS = 20
EPS = 1e-05

SIDE = 2 * WLON
GROUP = 128
HALF = 4 * GROUP
OWN = LEV * SIDE * ROWS
RIM = 128
COR = 16
BACK = 64
QUADS = 4
SCALE = 0.125
BF = jnp.bfloat16
F32 = jnp.float32
NT = (((1,), (1,)), ((), ()))

X, Y, Z = 4, 2, 4
UNIT = 32
LON, LAT = 0, 1


def params(mebibytes):
    return pltpu.CompilerParams(vmem_limit_bytes=mebibytes * 1024 * 1024)


def cost(micros):
    return pl.CostEstimate(flops=int(micros * 1.1e9), bytes_accessed=10**6, transcendentals=0)


SCALARS = pl.BlockSpec(memory_space=pltpu.SMEM)
WHOLE = pl.BlockSpec(memory_space=pltpu.VMEM)


def dot(a, b):
    return jnp.dot(a, b, preferred_element_type=F32)


def dot_nt(a, b):
    return lax.dot_general(a, b, NT, preferred_element_type=F32)


def place_of(lon):
    return lon % X, (lon // X) % Y, lon // (X * Y)


def relative(block, pos_ref):
    lon = pos_ref[LON]
    x, y, z = place_of(block)
    x0, y0, z0 = lax.rem(lon, X), lax.rem(lax.div(lon, X), Y), lax.div(lon, X * Y)
    dx, dy, dz = lax.rem(x - x0 + X, X), lax.rem(y - y0 + Y, Y), lax.rem(z - z0 + Z, Z)
    return (dx * Z + dz) * Y + dy


def token(level, r, c):
    return (level * WLAT + r) * SIDE + c


def every():
    for level in range(LEV):
        for c in range(SIDE):
            for i in range(ROWS):
                wr, r = divmod((i - SLAT) % ROWS, WLAT)
                yield level, c, i, wr, r


def one_hot(shape, places):
    out = np.zeros(shape, np.float32)
    for at in places:
        out[at] = 1.0
    return jnp.asarray(out.astype(jnp.bfloat16))


def pick_own():
    return one_hot(
        (2, GROUP, OWN),
        [
            (wr, token(level, r, c), (level * SIDE + c) * ROWS + i)
            for level, c, i, wr, r in every()
            if i >= SLAT
        ],
    )


def pick_rim(side):
    places = []
    for level, c, i, wr, r in every():
        if i < SLAT:
            column = SLON + side * SIDE + c
            if column < COLS:
                src = (level * COLS + column) * SLAT + i
            else:
                src = RIM + (level * SLON + column - COLS) * SLAT + i
            places.append((token(level, r, c), src))
    return one_hot((GROUP, RIM + COR), places)


def pick_out():
    return one_hot(
        (OWN, 2 * GROUP),
        [
            ((level * SIDE + c) * ROWS + i, wr * GROUP + token(level, r, c))
            for level, c, i, wr, r in every()
        ],
    )


def pick_back():
    return one_hot(
        (BACK + COR, GROUP),
        [
            ((level * SIDE + c) * SLAT + i, token(level, r, c))
            for level, c, i, wr, r in every()
            if i < SLAT
        ]
        + [
            (BACK + (level * SLON + c - SIDE + SLON) * SLAT + i, token(level, r, c))
            for level, c, i, wr, r in every()
            if i < SLAT and c >= SIDE - SLON
        ],
    )


def pick_strip():
    rim = [
        ((level * COLS + column) * SLAT + i, (level * COLS + column) * ROWS + i)
        for level in range(LEV)
        for column in range(COLS)
        for i in range(SLAT)
    ]
    cor = [
        (RIM + (level * SLON + column) * SLAT + i, (level * COLS + column) * ROWS + i)
        for level in range(LEV)
        for column in range(SLON)
        for i in range(SLAT)
    ]
    return one_hot((RIM + COR, LEV * COLS * ROWS), rim + cor)


def pick_place(columns, offset, height):
    return one_hot(
        (LEV, columns * ROWS, height),
        [
            (level, c * ROWS + i, (level * (columns + offset) + c) * SLAT + i)
            for level in range(LEV)
            for c in range(columns)
            for i in range(SLAT)
        ],
    )


def strips_kernel(pick_ref, f_ref, g_ref, lon_ref, rim_ref, cor_ref):
    for arr, ref in enumerate((f_ref, g_ref)):
        block = ref[0]
        lon_ref[arr, 0] = block[:, : SLON * ROWS]
        strip = dot(pick_ref[...], block.reshape(-1, block.shape[-1])).astype(BF)
        rim_ref[arr, 0] = strip[:RIM]
        cor_ref[arr, 0] = strip[RIM:]


def strips(f, g):
    samples, levels, rows, width = f.shape
    pick = pick_strip()
    block = pl.BlockSpec((1, levels, rows, width), lambda b: (b, 0, 0, 0))
    shapes = [(levels, SLON * ROWS, width), (RIM, width), (COR, width)]
    return pl.pallas_call(
        strips_kernel,
        grid=(samples,),
        in_specs=[pl.BlockSpec(pick.shape, lambda b: (0, 0)), block, block],
        out_specs=[
            pl.BlockSpec((2, 1) + s, lambda b, n=len(s): (0, b) + (0,) * n) for s in shapes
        ],
        out_shape=[jax.ShapeDtypeStruct((2, samples) + s, BF) for s in shapes],
        compiler_params=params(56),
        cost_estimate=cost(3),
        name="strips",
    )(pick, f, g)


def project_kernel(
    side, pos_ref, own_ref, pick_ref, f_ref, g_ref, lon_ref, rim_ref, cor_ref, w_ref, wo_ref,
    xw_ref, gw_ref, nt_ref, q_ref, k_ref, v_ref, da_ref, nw,
):
    samples, levels, _, width = f_ref.shape
    cols = width // QUADS
    for b in range(samples):
        got = []
        for arr, ref in enumerate((f_ref, g_ref)):
            parts = []
            for level in range(levels):
                if side == 0:
                    parts.append(ref[b, level, SLON * ROWS : (SLON + SIDE) * ROWS])
                else:
                    parts.append(ref[b, level, (SLON + SIDE) * ROWS :])
                    parts.append(lon_ref[arr, b, level])
            own = jnp.concatenate(parts, axis=0)
            rim = jnp.concatenate([rim_ref[arr, b], cor_ref[arr, b]], axis=0)
            got.append((own, rim))
        for wr in range(2):
            at = slice((b * 2 + wr) * GROUP, (b * 2 + wr + 1) * GROUP)
            x, g = (dot(own_ref[wr], own) for own, _ in got)
            if wr == 1:
                x, g = (a + dot(pick_ref[...], rim) for a, (_, rim) in zip((x, g), got))
            gw_ref[at, :] = g.astype(BF)
            xw_ref[at, :] = x.astype(BF)
            centred = x - jnp.mean(x, axis=-1, keepdims=True)
            inv = lax.rsqrt(jnp.mean(centred * centred, axis=-1, keepdims=True) + EPS)
            normed = (centred * inv).astype(BF)
            nw[at, :] = normed
            turned = normed.T
            for block in range(width // UNIT):
                dst = pl.multiple_of(relative(block, pos_ref) * UNIT, UNIT)
                nt_ref[pl.ds(dst, UNIT), at] = turned[block * UNIT : (block + 1) * UNIT]

    def quad(n, carry):
        at = pl.ds(pl.multiple_of(n * cols, cols), cols)
        for i, ref in enumerate((q_ref, k_ref, v_ref)):
            part = pl.ds(pl.multiple_of(i * width + n * cols, cols), cols)
            ref[:, at] = dot(nw[...], w_ref[:, part]).astype(BF)
        da_ref[:, at] = dot_nt(gw_ref[...], wo_ref[at, :]).astype(BF)
        return carry

    lax.fori_loop(0, QUADS, quad, 0)


def project(side, pos, f, g, lon_in, rim_in, cor_in, w_qkv, w_out):
    width = f.shape[-1]
    own, pick = pick_own(), pick_rim(side)
    tall = jax.ShapeDtypeStruct((HALF, width), BF)
    operands = (pos, own, pick, f, g, lon_in, rim_in, cor_in, w_qkv, w_out)
    return pl.pallas_call(
        functools.partial(project_kernel, side),
        in_specs=[SCALARS] + [WHOLE] * (len(operands) - 1),
        out_specs=[WHOLE] * 7,
        out_shape=[tall, tall, jax.ShapeDtypeStruct((width, HALF), BF)] + [tall] * 4,
        scratch_shapes=[pltpu.VMEM((HALF, width), BF)],
        compiler_params=params(8),
        cost_estimate=cost(9),
        name="project",
    )(*operands)


def attention_kernel(quads, pos_ref, bias_ref, *rest):
    sides, rest = (rest[:6], rest[6:12]), rest[12:]
    if quads == (3,):
        kin_ref, rest = rest[0], rest[1:]
    if quads == (1,):
        att_ref, dq_ref, dk_ref, dv_ref, keep_ref, send_ref, kout_ref, att_t = rest
    elif quads == (3,):
        att_ref, dq_ref, dk_ref, dv_ref, keep_ref, send_ref, att_t = rest
    else:
        att_ref, dq_ref, dk_ref, dv_ref, keep_ref, send_ref, gok_ref, gos_ref, att_t = rest
    width = sides[0][0].shape[0]
    cols = width // QUADS
    head = 64
    lat0 = pos_ref[LAT] == 0
    x0 = lax.rem(pos_ref[LON], X)
    first = lax.broadcasted_iota(jnp.int32, (GROUP, 2 * head), 1) < head
    upper = lax.broadcasted_iota(jnp.int32, (2 * head, GROUP), 0) < head
    zero = jnp.zeros((GROUP, 2 * head), BF)

    def split(pair):
        return jnp.concatenate([jnp.where(first, pair, zero), jnp.where(first, zero, pair)], axis=0)

    def beside(turned):
        return jnp.concatenate(
            [jnp.where(upper, turned, zero), jnp.where(upper, zero, turned)], axis=1
        )

    def stacked(both):
        return jnp.concatenate([both[:, :GROUP], both[:, GROUP:]], axis=0)

    def lanes(start, size):
        return pl.ds(start if isinstance(start, int) else pl.multiple_of(start, 128), size)

    def unit(refs, side, group, wr, pair, src, dst):
        _, _, q_ref, k_ref, v_ref, da_ref = refs
        at = (pl.ds(pl.multiple_of(group * GROUP, GROUP), GROUP), lanes(src + pair * 128, 128))
        here = pl.ds(pl.multiple_of(side * HALF + group * GROUP, GROUP), GROUP)
        both = lanes(dst + pair * 128, 128)
        bias = bias_ref[side * 2 + wr]
        q, k, v, da = q_ref[at], k_ref[at], v_ref[at], da_ref[at]
        q2, da2 = split(q * SCALE), split(da)
        scores = dot_nt(k, q2)
        d_prob = dot_nt(v, da2)
        yield
        scores = scores + jnp.concatenate([bias, bias], axis=1)
        top = jnp.max(scores, axis=0, keepdims=True)
        expd = jnp.exp(scores - top)
        prob = expd * (1.0 / jnp.sum(expd, axis=0, keepdims=True))
        prob16 = prob.astype(BF)
        part = prob * d_prob
        delta = jnp.sum(part, axis=0, keepdims=True)
        d_score = (part - prob * delta).astype(BF)
        yield
        out_t = dot(beside(v.T), stacked(prob16)).astype(BF)
        dq_t = dot(beside((k * SCALE).T), stacked(d_score)).astype(BF)
        dv_ref[here, both] = dot(prob16, da2).astype(BF)
        dk_ref[here, both] = dot(d_score, q2).astype(BF)
        yield
        att_ref[here, both] = out_t.T
        for block in range(128 // UNIT):
            row = lax.rem(block - x0 + X, X) * (2 * UNIT) + pair * UNIT
            att_t[pl.ds(pl.multiple_of(row, UNIT), UNIT), here] = out_t[
                block * UNIT : (block + 1) * UNIT
            ]
        dq_ref[here, both] = dq_t.T
        yield

    low, high = slice(0, HALF), slice(HALF, 2 * HALF)

    def units(src, dst):
        for side in range(2):

            def sample(b, carry):
                works = [
                    unit(sides[side], side, b * 2 + wr, wr, pair, src, dst)
                    for wr in range(2)
                    for pair in range(2)
                ]
                for _ in range(4):
                    for work in works:
                        next(work)
                return carry

            lax.fori_loop(0, HALF // (2 * GROUP), sample, 0)

    def out_sums():
        grad_out = dot(att_t[:, low], sides[0][1][...]) + dot(att_t[:, high], sides[1][1][...])
        left, right = grad_out[:, : width // 2], grad_out[:, width // 2 :]
        return jnp.where(lat0, left, right).astype(BF), jnp.where(lat0, right, left).astype(BF)

    def qkv_sums(store, dst):
        def piece(i, carry):
            at = pl.ds(pl.multiple_of(i * 256, 256), 256)
            left = (sides[0][0][at, :], sides[1][0][at, :])
            of_q, of_k, of_v = (
                dot(left[0], ref[low, lanes(dst, cols)]) + dot(left[1], ref[high, lanes(dst, cols)])
                for ref in (dq_ref, dk_ref, dv_ref)
            )
            mine = jnp.where(lat0, of_q, of_v).astype(BF)
            other = jnp.where(lat0, of_v, of_q).astype(BF)
            store(at, mine, other, of_k.astype(BF))
            return carry

        lax.fori_loop(0, width // 256, piece, 0)

    if quads == (0, 2):

        def turn(n, carry):
            dst = n * cols
            units(n * 2 * cols, dst)
            rows = pl.ds(pl.multiple_of(n * cols, cols), cols)
            gok_ref[rows, :], gos_ref[rows, :] = out_sums()
            stays = jnp.logical_xor(lat0, n == 1)

            def store(at, mine, other, of_k):
                keep_ref[at, lanes(dst, cols)] = mine
                send_ref[at, lanes(dst, cols)] = other

                @pl.when(stays)
                def _():
                    keep_ref[at, 2 * cols :] = of_k

                @pl.when(jnp.logical_not(stays))
                def _():
                    send_ref[at, 2 * cols :] = of_k

            qkv_sums(store, dst)
            return carry

        lax.fori_loop(0, 2, turn, 0)
        return

    units(quads[0] * cols, 0)
    mine, other = out_sums()
    if quads == (1,):
        for half in range(2):
            below = slice(width + half * cols, width + (half + 1) * cols)
            keep_ref[below, :] = mine[:, half * cols : (half + 1) * cols]
            send_ref[below, :] = other[:, half * cols : (half + 1) * cols]
    else:
        keep_ref[width:, :] = mine
        send_ref[width:, :] = other

    def store(at, mine, other, of_k):
        keep_ref[at, :cols] = mine
        send_ref[at, :cols] = other
        if quads == (1,):
            kout_ref[at, :] = of_k
        else:
            before = kin_ref[at, :]
            keep_ref[at, cols:] = jnp.where(lat0, before, of_k)
            send_ref[at, cols:] = jnp.where(lat0, of_k, before)

    qkv_sums(store, 0)


def attention(quads, pos, bias, sides, before=None):
    width = sides[0][0].shape[1]
    cols = width // QUADS
    count = len(quads)
    operands = [pos, bias] + [a for side in sides for a in side[1:]]
    for side in range(2):
        at = 2 + side * 6
        operands[at], operands[at + 1] = operands[at + 1], operands[at]
    if before is not None:
        operands.append(before)
    shapes = [(2 * HALF, count * cols)] * 4
    shapes += [{0: (width, 3 * cols), 1: (width + 2 * cols, cols), 3: (width + cols, 2 * cols)}[quads[0]]] * 2
    if quads == (0, 2):
        shapes += [(count * cols, width // 2)] * 2
    elif quads == (1,):
        shapes += [(width, cols)]
    return pl.pallas_call(
        functools.partial(attention_kernel, quads),
        in_specs=[SCALARS] + [WHOLE] * (len(operands) - 1),
        out_specs=[WHOLE] * len(shapes),
        out_shape=[jax.ShapeDtypeStruct(s, BF) for s in shapes],
        scratch_shapes=[pltpu.VMEM((cols, 2 * HALF), BF)],
        compiler_params=params(8),
        cost_estimate=cost(11 * count),
        name="attention",
    )(*operands)


def output_kernel(side, out_ref, back_ref, x_ref, dy_ref, wqkv_ref, wo_ref, *rest):
    first, second, last = rest[:4], rest[4:8], rest[8:12]
    if side == 0:
        before, y_ref, gx_ref, rims_ref, branch_at, g_at = rest[12:]
        rim_ref = rims_ref.at[0]
    else:
        y_ref, gx_ref, rim_ref, cor_ref, lon_ref, branch_at, g_at = rest[12:]
    levels = y_ref.shape[1]
    cols = last[0].shape[1]
    step = pl.program_id(0)

    def by_quad(i):
        return [first[i][:, :cols], second[i][...], first[i][:, cols:], last[i][...]]

    branch_at[step] = dot(jnp.concatenate(by_quad(0), axis=1), wo_ref[...]).astype(BF)
    d_all = jnp.concatenate([a for i in (1, 2, 3) for a in by_quad(i)], axis=1)
    g_at[step] = dot_nt(d_all, wqkv_ref[...]).astype(BF)

    @pl.when(step == pl.num_programs(0) - 1)
    def _():
        if side == 0:
            rims_ref[1] = before[...]

        def sample(b, carry):
            at = pl.ds(pl.multiple_of(b * 2 * GROUP, 2 * GROUP), 2 * GROUP)
            joined = lambda ref: jnp.concatenate([ref[n, at] for n in range(QUADS)], axis=1).astype(F32)
            x = x_ref[at, :].astype(F32)
            y = (x + joined(branch_at)).astype(BF)
            g = joined(g_at)
            centred = x - jnp.mean(x, axis=-1, keepdims=True)
            inv = lax.rsqrt(jnp.mean(centred * centred, axis=-1, keepdims=True) + EPS)
            normed = centred * inv
            gx = dy_ref[at, :].astype(F32) + inv * (
                g
                - jnp.mean(g, axis=-1, keepdims=True)
                - normed * jnp.mean(g * normed, axis=-1, keepdims=True)
            )
            for arr, (value, ref) in enumerate(((y, y_ref), (gx.astype(BF), gx_ref))):
                placed = dot(out_ref[...], value).astype(BF)
                back = dot(back_ref[...], value[GROUP:]).astype(BF)
                rim_ref[arr, b] = back[:BACK]
                if side == 1:
                    cor_ref[arr, b] = back[BACK:]
                kept = (SIDE if side == 0 else SIDE - SLON) * ROWS
                for level in range(levels):
                    start = level * SIDE * ROWS
                    ref[b, level] = placed[start : start + kept]
                    if side == 1:
                        lon_ref[arr, b, level] = placed[start + kept : start + SIDE * ROWS]
            return carry

        lax.fori_loop(0, HALF // (2 * GROUP), sample, 0)


def outputs(side, samples, xw, gw, w_qkv, w_out, first, second, last, *before):
    width = w_out.shape[0]
    cols = width // QUADS
    out, back = pick_out(), pick_back()
    full = lambda shape: pl.BlockSpec(shape, lambda n: (0,) * len(shape))
    kept = (SIDE if side == 0 else SIDE - SLON) * ROWS
    shapes = [(samples, LEV, kept, width)] * 2
    if side == 0:
        shapes += [(2, 2, samples, BACK, width)]
    else:
        shapes += [(2, samples, BACK, width), (2, samples, COR, width)]
        shapes += [(2, samples, LEV, SLON * ROWS, width)]
    return pl.pallas_call(
        functools.partial(output_kernel, side),
        grid=(QUADS,),
        in_specs=[full(a.shape) for a in (out, back, xw, gw)]
        + [
            pl.BlockSpec((cols, 3 * width), lambda n: (n, 0)),
            pl.BlockSpec((width, cols), lambda n: (0, n)),
        ]
        + [pl.BlockSpec((HALF, 2 * cols), lambda n: (side, 0))] * 4
        + [pl.BlockSpec((HALF, cols), lambda n: (side, 0))] * 8
        + [full(a.shape) for a in before],
        out_specs=[full(s) for s in shapes],
        out_shape=[jax.ShapeDtypeStruct(s, BF) for s in shapes],
        scratch_shapes=[pltpu.VMEM((QUADS, HALF, cols), BF)] * 2,
        compiler_params=params(14),
        cost_estimate=cost(8),
        name="outputs",
    )(out, back, xw, gw, w_qkv, w_out, *first[:4], *second[:4], *last[:4], *before)


def merge_kernel(place0_ref, place1_ref, placec_ref, y0, g0, y1, g1, rim, cor, lon, y_ref, gx_ref):
    levels = y_ref.shape[1]
    for arr, (low, high, out) in enumerate(((y0, y1, y_ref), (g0, g1, gx_ref))):
        for level in range(levels):
            start = 0
            for mine, pick, strip in (
                (lon[arr, 0, level], placec_ref, cor[arr, 0]),
                (low[0, level], place0_ref, rim[0, arr, 0]),
                (high[0, level], place1_ref, rim[1, arr, 0]),
            ):
                rows = mine.shape[0]
                here = lax.broadcasted_iota(jnp.int32, mine.shape, 0) % ROWS < SLAT
                placed = dot(pick[level], strip).astype(BF)
                out[0, level, start : start + rows] = jnp.where(here, placed, mine)
                start += rows


def merge(y0, g0, y1, g1, rim, cor, lon):
    samples, levels, _, width = y0.shape
    picks = [pick_place(SIDE, 0, BACK), pick_place(SIDE - SLON, SLON, BACK), pick_place(SLON, 0, COR)]
    full = lambda a: pl.BlockSpec(a.shape, lambda b: (0,) * a.ndim)
    own = lambda a: pl.BlockSpec((1,) + a.shape[1:], lambda b: (b,) + (0,) * (a.ndim - 1))
    strip = lambda a: pl.BlockSpec((2, 1) + a.shape[2:], lambda b: (0, b) + (0,) * (a.ndim - 2))
    shape = jax.ShapeDtypeStruct((samples, levels, COLS * ROWS, width), BF)
    return pl.pallas_call(
        merge_kernel,
        grid=(samples,),
        in_specs=[full(a) for a in picks]
        + [own(a) for a in (y0, g0, y1, g1)]
        + [pl.BlockSpec((2, 2, 1) + rim.shape[3:], lambda b: (0, 0, b, 0, 0))]
        + [strip(a) for a in (cor, lon)],
        out_specs=[own(shape)] * 2,
        out_shape=[shape] * 2,
        compiler_params=params(12),
        cost_estimate=cost(4),
        name="merge",
    )(*picks, y0, g0, y1, g1, rim, cor, lon)


def shifted(value, axis, steps):
    count = lax.axis_size(axis)
    pairs = [(source, (source + steps) % count) for source in range(count)]
    return lax.ppermute(value, axis, pairs)


def shifted_both(value, steps):
    lon, lat = lax.axis_size("lon"), lax.axis_size("lat")
    pairs = [
        (i * lat + j, ((i + steps) % lon) * lat + (j + steps) % lat)
        for i in range(lon)
        for j in range(lat)
    ]
    return lax.ppermute(value, ("lon", "lat"), pairs)


def allowed_bias(mask_ids):
    lat_total = mask_ids.shape[0]
    start = lax.axis_index("lat") * ROWS + SLAT
    lat_global = (start + np.arange(ROWS, dtype=np.int32)) % lat_total
    wide = jnp.concatenate([mask_ids, mask_ids[:, :SLON]], axis=1)
    wide = jnp.concatenate([wide, wide[:SLAT]], axis=0)
    ids = lax.dynamic_slice(wide, (start, lax.axis_index("lon") * COLS + SLON), (ROWS, COLS))
    code = ids * 2 + (lat_global < SLAT).astype(jnp.int32)[:, None]
    code = code + 16 * (np.arange(COLS, dtype=np.int32) // WLON)[None, :]
    code = code.reshape(2, WLAT, 2, SIDE).transpose(2, 0, 1, 3).reshape(4, 1, WLAT * SIDE)
    code = jnp.broadcast_to(code, (4, LEV, WLAT * SIDE)).reshape(4, -1)
    code = jnp.pad(code, ((0, 0), (0, GROUP - code.shape[1])), constant_values=-1)
    same = code[:, :, None] == code[:, None, :]
    return jnp.where(same, 0.0, -jnp.inf).astype(F32)


def swapped(value, axis):
    return lax.ppermute(value, axis, [(0, 1), (1, 0)])


def to_distance(value, dx=0, dy=0, dz=0):
    pairs = []
    for lon in range(X * Y * Z):
        x, y, z = place_of(lon)
        pairs.append((lon, ((z + dz) % Z * Y + (y + dy) % Y) * X + (x + dx) % X))
    return lax.ppermute(value, "lon", pairs)


def added(*terms):
    total = terms[0].astype(F32)
    for term in terms[1:]:
        total = total + term.astype(F32)
    return total


def ring_sum(chunks, name):
    got = [to_distance(chunks[d], **{name: d}) for d in range(1, len(chunks))]
    return added(chunks[0], *got)


def relay(chunks, name):
    half = chunks[2].shape[0] // 2
    return [to_distance(chunks[2][:half], **{name: 1}), to_distance(chunks[2][half:], **{name: 3})]


def with_relayed(chunks, got):
    half = got[0].shape[0]
    up = jnp.concatenate([added(chunks[1][:half], got[0]).astype(BF), chunks[1][half:]], axis=0)
    down = jnp.concatenate([chunks[3][:half], added(chunks[3][half:], got[1]).astype(BF)], axis=0)
    return [up, down]


def both_ways(pair, name):
    return [to_distance(pair[0], **{name: 1}), to_distance(pair[1], **{name: 3})]


def swap_sum(keep, got):
    return added(keep, got).astype(BF)


def chunks_by_z(total):
    total = total.reshape(X, Z, Y * UNIT, -1)
    return [total[:, d].reshape(X * Y * UNIT, -1) for d in range(Z)]


def chunks_by_x(total):
    return jnp.split(total, X)


def chunks_with_out(qkv, outs):
    _, y0, z0 = place_of(lax.axis_index("lon"))
    outs = jnp.stack(outs).reshape(Z, X, Y, UNIT, -1)
    outs = jnp.where(y0 == 0, outs, outs[:, :, ::-1]).reshape(Z, X * Y * UNIT, -1)
    return [
        jnp.concatenate([chunk, lax.dynamic_index_in_dim(outs, (z0 + d) % Z, keepdims=False)], axis=1)
        for d, chunk in enumerate(chunks_by_z(qkv))
    ]


def final_sums(total):
    cols = total.shape[1] // 8
    piece = [total[:, i * cols : (i + 1) * cols] for i in range(8)]
    pick = lambda *which: jnp.concatenate([piece[i] for i in which], axis=1)
    lat0 = lax.axis_index("lat") == 0
    low = jnp.where(lat0, pick(0, 3, 1, 4), pick(2, 7, 0, 4))
    high = jnp.where(lat0, pick(6, 2, 7, 5), pick(3, 1, 6, 5))
    dp0 = lax.axis_index("dp") == 0
    got = swapped(jnp.where(dp0, high, low), "dp")
    total = added(jnp.where(dp0, low, high), got)
    return total[:, : 3 * cols], total[:, 3 * cols :]


def per_device(fields, grad_y, w_qkv, w_out, mask_ids):
    samples, levels, lat_rows, lon_cols, width = fields.shape
    flat = lambda a: a.transpose(0, 1, 3, 2, 4).reshape(samples, levels, lon_cols * lat_rows, width)
    f, g = flat(fields), flat(grad_y)
    pos = jnp.stack([lax.axis_index("lon"), lax.axis_index("lat")]).astype(jnp.int32)
    lon_out, rim_out, cor_out = strips(f, g)
    rim_in = shifted(rim_out, "lat", -1)
    cor_in = shifted_both(cor_out, -1)
    lon_in = shifted(lon_out, "lon", -1)
    bias = allowed_bias(mask_ids)
    side0 = project(0, pos, f, g, lon_out, rim_in, cor_out, w_qkv, w_out)
    side1 = project(1, pos, f, g, lon_in, rim_in, cor_in, w_qkv, w_out)
    sides = (side0, side1)
    barrier = lax.optimization_barrier
    first = attention((0, 2), pos, bias, sides)
    by_z = chunks_by_z(swap_sum(first[4], swapped(first[5], "lat")))
    outs = swap_sum(first[6], swapped(first[7], "lat"))
    by_z, pos1 = barrier((by_z, pos))
    got_z = relay(by_z, "dz")
    second = attention((1,), pos1, bias, sides)
    got_z, before, send = barrier((got_z, second[6], second[5]))
    ways, before = barrier((with_relayed(by_z, got_z), before))
    got_z = both_ways(ways, "dz")
    last = attention((3,), pos, bias, sides, before=before)
    got_z, send, send_last = barrier((got_z, send, last[5]))
    first_total = added(by_z[0], *got_z).astype(BF).reshape(X, Y * UNIT, -1)
    got, got_last = swapped(send, "lat"), swapped(send_last, "lat")
    total = swap_sum(second[4], got)
    cols = total.shape[1]
    out = jnp.concatenate([total[-2 * cols : -cols], total[-cols:]], axis=1)
    total_last = swap_sum(last[4], got_last)
    outs = [outs[:cols], out, outs[cols:], total_last[-cols:]]
    by_x = chunks_by_x(total_last[:-cols])
    by_z = chunks_with_out(total[: -2 * cols], outs)
    by_x, by_z, att = barrier((by_x, by_z, last[0]))
    got_x, got_z = relay(by_x, "dx"), relay(by_z, "dz")
    last = (att, *last[1:])
    y1, g1, rim, cor, lon = outputs(1, samples, *side1[:2], w_qkv, w_out, first, second, last)
    got_x, got_z, lon, cor, rim = barrier((got_x, got_z, lon, cor, rim))
    ways_x, ways_z = with_relayed(by_x, got_x), with_relayed(by_z, got_z)
    ways_x, ways_z, lon, xw0 = barrier((ways_x, ways_z, lon, side0[0]))
    got_x, got_z = both_ways(ways_x, "dx"), both_ways(ways_z, "dz")
    lon = shifted(lon, "lon", 1)
    y0, g0, rim = outputs(0, samples, xw0, side0[1], w_qkv, w_out, first, second, last, rim)
    got_x, got_z, rim, cor = barrier((got_x, got_z, rim, cor))
    cor, rim = shifted_both(cor, 1), shifted(rim, "lat", 1)
    by_z_own = by_z[0]
    by_z = added(by_x[0], *got_x).astype(BF).reshape(Z, Y * UNIT, -1)
    total_z = added(by_z_own, *got_z).astype(BF).reshape(X, Y * UNIT, -1)
    by_x = [jnp.concatenate([first_total[d], total_z[d]], axis=1) for d in range(X)]
    total_z = ring_sum(list(by_z), "dz")
    total = jnp.concatenate([ring_sum(by_x, "dx").astype(BF), total_z.astype(BF)], axis=1)
    total = total.reshape(Y, UNIT, -1)
    got_y = to_distance(total[1], dy=1)
    y, gx = merge(y0, g0, y1, g1, rim, cor, lon)
    got_y, y, gx = barrier((got_y, y, gx))
    sums = final_sums(added(total[0], got_y).astype(BF))
    unflat = lambda a: a.reshape(samples, levels, lon_cols, lat_rows, width).transpose(0, 1, 3, 2, 4)
    return (unflat(y), unflat(gx), *sums)


def solution(mesh):
    grid = P("dp", None, "lat", "lon", None)
    return jax.shard_map(
        per_device,
        mesh=mesh,
        in_specs=(grid, grid, P(), P(), P()),
        out_specs=(grid, grid, P("lon", ("lat", "dp")), P("lon", ("lat", "dp"))),
        check_vma=False,
    )
```

```python
import functools

import jax
import jax.numpy as jnp
import numpy as np
from jax import lax
from jax.experimental import pallas as pl
from jax.experimental.pallas import tpu as pltpu
from jax.sharding import PartitionSpec as P

HEADS = 16
LEV = 3
WLAT = 4
WLON = 5
SLAT = 2
SLON = 2
ROWS = 8
COLS = 20
EPS = 1e-05

SIDE = 2 * WLON
GROUP = 128
HALF = 4 * GROUP
OWN = LEV * SIDE * ROWS
RIM = 128
COR = 16
BACK = 64
QUADS = 4
SCALE = 0.125
BF = jnp.bfloat16
F32 = jnp.float32
NT = (((1,), (1,)), ((), ()))

X, Y, Z = 4, 2, 4
UNIT = 32
LON, LAT = 0, 1


def params(mebibytes):
    return pltpu.CompilerParams(vmem_limit_bytes=mebibytes * 1024 * 1024)


def cost(micros):
    return pl.CostEstimate(flops=int(micros * 1.1e9), bytes_accessed=10**6, transcendentals=0)


SCALARS = pl.BlockSpec(memory_space=pltpu.SMEM)


def dot(a, b):
    return jnp.dot(a, b, preferred_element_type=F32)


def dot_nt(a, b):
    return lax.dot_general(a, b, NT, preferred_element_type=F32)


def place_of(lon):
    return lon % X, (lon // X) % Y, lon // (X * Y)


def relative(block, pos_ref):
    lon = pos_ref[LON]
    x, y, z = place_of(block)
    x0, y0, z0 = lax.rem(lon, X), lax.rem(lax.div(lon, X), Y), lax.div(lon, X * Y)
    dx, dy, dz = lax.rem(x - x0 + X, X), lax.rem(y - y0 + Y, Y), lax.rem(z - z0 + Z, Z)
    return (dx * Z + dz) * Y + dy


def token(level, r, c):
    return (level * WLAT + r) * SIDE + c


def every():
    for level in range(LEV):
        for c in range(SIDE):
            for i in range(ROWS):
                wr, r = divmod((i - SLAT) % ROWS, WLAT)
                yield level, c, i, wr, r


def one_hot(shape, places):
    out = np.zeros(shape, np.float32)
    for at in places:
        out[at] = 1.0
    return jnp.asarray(out.astype(jnp.bfloat16))


def pick_own():
    return one_hot(
        (2, GROUP, OWN),
        [
            (wr, token(level, r, c), (level * SIDE + c) * ROWS + i)
            for level, c, i, wr, r in every()
            if i >= SLAT
        ],
    )


def pick_rim(side):
    places = []
    for level, c, i, wr, r in every():
        if i < SLAT:
            column = SLON + side * SIDE + c
            if column < COLS:
                src = (level * COLS + column) * SLAT + i
            else:
                src = RIM + (level * SLON + column - COLS) * SLAT + i
            places.append((token(level, r, c), src))
    return one_hot((GROUP, RIM + COR), places)


def pick_out():
    return one_hot(
        (OWN, 2 * GROUP),
        [
            ((level * SIDE + c) * ROWS + i, wr * GROUP + token(level, r, c))
            for level, c, i, wr, r in every()
        ],
    )


def pick_back():
    return one_hot(
        (BACK, GROUP),
        [
            ((level * SIDE + c) * SLAT + i, token(level, r, c))
            for level, c, i, wr, r in every()
            if i < SLAT
        ],
    )


def pick_strip():
    rim = [
        ((level * COLS + column) * SLAT + i, (level * COLS + column) * ROWS + i)
        for level in range(LEV)
        for column in range(COLS)
        for i in range(SLAT)
    ]
    cor = [
        (RIM + (level * SLON + column) * SLAT + i, (level * COLS + column) * ROWS + i)
        for level in range(LEV)
        for column in range(SLON)
        for i in range(SLAT)
    ]
    return one_hot((RIM + COR, LEV * COLS * ROWS), rim + cor)


def pick_place(columns, start):
    return one_hot(
        (LEV, columns * ROWS, BACK),
        [
            (level, c * ROWS + i, (level * SIDE + start + c) * SLAT + i)
            for level in range(LEV)
            for c in range(columns)
            for i in range(SLAT)
        ],
    )


def strips_kernel(pick_ref, f_ref, g_ref, lon_ref, rim_ref, cor_ref):
    for arr, ref in enumerate((f_ref, g_ref)):
        block = ref[0]
        lon_ref[arr, 0] = block[:, : SLON * ROWS]
        strip = dot(pick_ref[...], block.reshape(-1, block.shape[-1])).astype(BF)
        rim_ref[arr, 0] = strip[:RIM]
        cor_ref[arr, 0] = strip[RIM:]


def strips(f, g):
    samples, levels, rows, width = f.shape
    pick = pick_strip()
    block = pl.BlockSpec((1, levels, rows, width), lambda b: (b, 0, 0, 0))
    shapes = [(levels, SLON * ROWS, width), (RIM, width), (COR, width)]
    return pl.pallas_call(
        strips_kernel,
        grid=(samples,),
        in_specs=[pl.BlockSpec(pick.shape, lambda b: (0, 0)), block, block],
        out_specs=[
            pl.BlockSpec((2, 1) + s, lambda b, n=len(s): (0, b) + (0,) * n) for s in shapes
        ],
        out_shape=[jax.ShapeDtypeStruct((2, samples) + s, BF) for s in shapes],
        compiler_params=params(56),
        cost_estimate=cost(3),
        name="strips",
    )(pick, f, g)


def project_kernel(
    side, pos_ref, own_ref, pick_ref, f_ref, g_ref, lon_ref, rim_ref, cor_ref, wq_ref, wk_ref, wv_ref, wo_ref,
    xw_ref, gw_ref, nt_ref, q_ref, k_ref, v_ref, da_ref, nw,
):
    samples, levels, _, width = f_ref.shape

    @pl.when(pl.program_id(0) == 0)
    def _():
        for b in range(samples):
            got = []
            for arr, ref in enumerate((f_ref, g_ref)):
                parts = []
                for level in range(levels):
                    if side == 0:
                        parts.append(ref[b, level, SLON * ROWS : (SLON + SIDE) * ROWS])
                    else:
                        parts.append(ref[b, level, (SLON + SIDE) * ROWS :])
                        parts.append(lon_ref[arr, b, level])
                own = jnp.concatenate(parts, axis=0)
                rim = jnp.concatenate([rim_ref[arr, b], cor_ref[arr, b]], axis=0)
                got.append((own, rim))
            for wr in range(2):
                at = slice((b * 2 + wr) * GROUP, (b * 2 + wr + 1) * GROUP)
                x, g = (dot(own_ref[wr], own) for own, _ in got)
                if wr == 1:
                    x, g = (a + dot(pick_ref[...], rim) for a, (_, rim) in zip((x, g), got))
                gw_ref[at, :] = g.astype(BF)
                xw_ref[at, :] = x.astype(BF)
                centred = x - jnp.mean(x, axis=-1, keepdims=True)
                inv = lax.rsqrt(jnp.mean(centred * centred, axis=-1, keepdims=True) + EPS)
                normed = (centred * inv).astype(BF)
                nw[at, :] = normed
                turned = normed.T
                for block in range(width // UNIT):
                    dst = pl.multiple_of(relative(block, pos_ref) * UNIT, UNIT)
                    nt_ref[pl.ds(dst, UNIT), at] = turned[block * UNIT : (block + 1) * UNIT]

    q_ref[...] = dot(nw[...], wq_ref[...]).astype(BF)
    k_ref[...] = dot(nw[...], wk_ref[...]).astype(BF)
    v_ref[...] = dot(nw[...], wv_ref[...]).astype(BF)
    da_ref[...] = dot_nt(gw_ref[...], wo_ref[...]).astype(BF)


def project(side, pos, f, g, lon_in, rim_in, cor_in, w_qkv, w_out):
    width = f.shape[-1]
    cols = width // QUADS
    whole = lambda n: (0, 0)
    full = lambda a: pl.BlockSpec(a.shape, lambda n: (0,) * a.ndim)
    own, pick = pick_own(), pick_rim(side)
    tall = jax.ShapeDtypeStruct((HALF, width), BF)
    return pl.pallas_call(
        functools.partial(project_kernel, side),
        grid=(QUADS,),
        in_specs=[
            pl.BlockSpec(memory_space=pltpu.SMEM),
            full(own),
            full(pick),
            full(f),
            full(g),
            full(lon_in),
            full(rim_in),
            full(cor_in),
            pl.BlockSpec((width, cols), lambda n: (0, n)),
            pl.BlockSpec((width, cols), lambda n: (0, QUADS + n)),
            pl.BlockSpec((width, cols), lambda n: (0, 2 * QUADS + n)),
            pl.BlockSpec((cols, width), lambda n: (n, 0)),
        ],
        out_specs=[
            pl.BlockSpec((HALF, width), whole),
            pl.BlockSpec((HALF, width), whole),
            pl.BlockSpec((width, HALF), whole),
        ]
        + [pl.BlockSpec((HALF, cols), lambda n: (0, n))] * 4,
        out_shape=[pltpu.HBM((HALF, width), BF), tall, jax.ShapeDtypeStruct((width, HALF), BF)] + [tall] * 4,
        scratch_shapes=[pltpu.VMEM((HALF, width), BF)],
        compiler_params=params(20),
        cost_estimate=cost(9),
        name="project",
    )(pos, own, pick, f, g, lon_in, rim_in, cor_in, w_qkv, w_qkv, w_qkv, w_out)


def attention_kernel(quads, pos_ref, bias_ref, *rest):
    sides, rest = (rest[:6], rest[6:12]), rest[12:]
    if quads == (3,):
        kin_ref, rest = rest[0], rest[1:]
    if quads == (1,):
        att_ref, dq_ref, dk_ref, dv_ref, keep_ref, send_ref, kout_ref, att_t = rest
    elif quads == (3,):
        att_ref, dq_ref, dk_ref, dv_ref, keep_ref, send_ref, att_t = rest
    else:
        att_ref, dq_ref, dk_ref, dv_ref, keep_ref, send_ref, gok_ref, gos_ref, att_t = rest
    width = sides[0][0].shape[0]
    cols = width // QUADS
    head = 64
    lat0 = pos_ref[LAT] == 0
    x0 = lax.rem(pos_ref[LON], X)
    first = lax.broadcasted_iota(jnp.int32, (GROUP, 2 * head), 1) < head
    upper = lax.broadcasted_iota(jnp.int32, (2 * head, GROUP), 0) < head
    zero = jnp.zeros((GROUP, 2 * head), BF)

    def split(pair):
        return jnp.concatenate([jnp.where(first, pair, zero), jnp.where(first, zero, pair)], axis=0)

    def beside(turned):
        return jnp.concatenate(
            [jnp.where(upper, turned, zero), jnp.where(upper, zero, turned)], axis=1
        )

    def stacked(both):
        return jnp.concatenate([both[:, :GROUP], both[:, GROUP:]], axis=0)

    def lanes(start, size):
        return pl.ds(start if isinstance(start, int) else pl.multiple_of(start, 128), size)

    def unit(refs, side, group, wr, pair, src, dst):
        _, _, q_ref, k_ref, v_ref, da_ref = refs
        at = (pl.ds(pl.multiple_of(group * GROUP, GROUP), GROUP), lanes(src + pair * 128, 128))
        here = pl.ds(pl.multiple_of(side * HALF + group * GROUP, GROUP), GROUP)
        both = lanes(dst + pair * 128, 128)
        bias = bias_ref[side * 2 + wr]
        q, k, v, da = q_ref[at], k_ref[at], v_ref[at], da_ref[at]
        q2, da2 = split(q * SCALE), split(da)
        scores = dot_nt(k, q2)
        d_prob = dot_nt(v, da2)
        yield
        scores = scores + jnp.concatenate([bias, bias], axis=1)
        top = jnp.max(scores, axis=0, keepdims=True)
        expd = jnp.exp(scores - top)
        prob = expd * (1.0 / jnp.sum(expd, axis=0, keepdims=True))
        prob16 = prob.astype(BF)
        part = prob * d_prob
        delta = jnp.sum(part, axis=0, keepdims=True)
        d_score = (part - prob * delta).astype(BF)
        yield
        out_t = dot(beside(v.T), stacked(prob16)).astype(BF)
        dq_t = dot(beside((k * SCALE).T), stacked(d_score)).astype(BF)
        dv_ref[here, both] = dot(prob16, da2).astype(BF)
        dk_ref[here, both] = dot(d_score, q2).astype(BF)
        yield
        att_ref[here, both] = out_t.T
        for block in range(128 // UNIT):
            row = lax.rem(block - x0 + X, X) * (2 * UNIT) + pair * UNIT
            att_t[pl.ds(pl.multiple_of(row, UNIT), UNIT), here] = out_t[
                block * UNIT : (block + 1) * UNIT
            ]
        dq_ref[here, both] = dq_t.T
        yield

    low, high = slice(0, HALF), slice(HALF, 2 * HALF)

    def units(src, dst):
        for side in range(2):

            def sample(b, carry):
                works = [
                    unit(sides[side], side, b * 2 + wr, wr, pair, src, dst)
                    for wr in range(2)
                    for pair in range(2)
                ]
                for _ in range(4):
                    for work in works:
                        next(work)
                return carry

            lax.fori_loop(0, HALF // (2 * GROUP), sample, 0)

    def out_sums():
        grad_out = dot(att_t[:, low], sides[0][1][...]) + dot(att_t[:, high], sides[1][1][...])
        left, right = grad_out[:, : width // 2], grad_out[:, width // 2 :]
        return jnp.where(lat0, left, right).astype(BF), jnp.where(lat0, right, left).astype(BF)

    def qkv_sums(store, dst):
        def piece(i, carry):
            at = pl.ds(pl.multiple_of(i * 256, 256), 256)
            left = (sides[0][0][at, :], sides[1][0][at, :])
            of_q, of_k, of_v = (
                dot(left[0], ref[low, lanes(dst, cols)]) + dot(left[1], ref[high, lanes(dst, cols)])
                for ref in (dq_ref, dk_ref, dv_ref)
            )
            mine = jnp.where(lat0, of_q, of_v).astype(BF)
            other = jnp.where(lat0, of_v, of_q).astype(BF)
            store(at, mine, other, of_k.astype(BF))
            return carry

        lax.fori_loop(0, width // 256, piece, 0)

    if quads == (0, 2):

        units(0, 0)
        gok_ref[...], gos_ref[...] = out_sums()
        n = pl.program_id(0)
        stays = jnp.logical_xor(lat0, n == 1)

        def store(at, mine, other, of_k):
            keep_ref[at, lanes(n * cols, cols)] = mine
            send_ref[at, lanes(n * cols, cols)] = other

            @pl.when(stays)
            def _():
                keep_ref[at, 2 * cols :] = of_k

            @pl.when(jnp.logical_not(stays))
            def _():
                send_ref[at, 2 * cols :] = of_k

        qkv_sums(store, 0)
        return

    units(0, 0)
    mine, other = out_sums()
    if quads == (1,):
        for half in range(2):
            below = slice(width + half * cols, width + (half + 1) * cols)
            keep_ref[below, :] = mine[:, half * cols : (half + 1) * cols]
            send_ref[below, :] = other[:, half * cols : (half + 1) * cols]
    else:
        keep_ref[width:, :] = mine
        send_ref[width:, :] = other

    def store(at, mine, other, of_k):
        keep_ref[at, :cols] = mine
        send_ref[at, :cols] = other
        if quads == (1,):
            kout_ref[at, :] = of_k
        else:
            before = kin_ref[at, :]
            keep_ref[at, cols:] = jnp.where(lat0, before, of_k)
            send_ref[at, cols:] = jnp.where(lat0, of_k, before)

    qkv_sums(store, 0)


def attention(quads, pos, bias, sides, before=None):
    width = sides[0][0].shape[1]
    cols = width // QUADS
    count = len(quads)
    rows = 2 * HALF

    def quad(n):
        return 2 * n if count == 2 else quads[0]

    whole = lambda n: (0, 0)
    in_specs = [SCALARS, pl.BlockSpec(bias.shape, lambda n: (0, 0, 0))]
    operands = [pos, bias]
    for _, gw, nt, q, k, v, da in sides:
        in_specs += [pl.BlockSpec((width, HALF), whole), pl.BlockSpec((HALF, width), whole)]
        in_specs += [pl.BlockSpec((HALF, cols), lambda n: (0, quad(n)))] * 4
        operands += [nt, gw, q, k, v, da]
    if before is not None:
        in_specs.append(pl.BlockSpec((width, cols), whole))
        operands.append(before)
    out_specs = [pl.BlockSpec((rows, cols), lambda n: (0, n))] * 4
    shapes = [(rows, count * cols)] * 4
    sums = {0: (width, 3 * cols), 1: (width + 2 * cols, cols), 3: (width + cols, 2 * cols)}[quads[0]]
    out_specs += [pl.BlockSpec(sums, whole)] * 2
    shapes += [sums] * 2
    if quads == (0, 2):
        out_specs += [pl.BlockSpec((cols, width // 2), lambda n: (n, 0))] * 2
        shapes += [(count * cols, width // 2)] * 2
    elif quads == (1,):
        out_specs += [pl.BlockSpec((width, cols), whole)]
        shapes += [(width, cols)]
    return pl.pallas_call(
        functools.partial(attention_kernel, quads),
        grid=(count,),
        in_specs=in_specs,
        out_specs=out_specs,
        out_shape=[pltpu.HBM(s, BF) if n < 4 and count == 2 else jax.ShapeDtypeStruct(s, BF) for n, s in enumerate(shapes)],
        scratch_shapes=[pltpu.VMEM((cols, 2 * HALF), BF)],
        compiler_params=params(20),
        cost_estimate=cost(11 * count),
        name="attention",
    )(*operands)


def output_kernel(side, out_ref, back_ref, x_ref, dy_ref, wqkv_ref, wo_ref, *rest):
    first, second, last = rest[:4], rest[4:8], rest[8:12]
    if side == 0:
        y_ref, gx_ref, rim_ref, branch_at, g_at = rest[12:]
    else:
        y_ref, gx_ref, rim_ref, lon_ref, branch_at, g_at = rest[12:]
    levels = y_ref.shape[1]
    cols = last[0].shape[1]
    step = pl.program_id(0)

    def by_quad(i):
        return [first[i][:, :cols], second[i][...], first[i][:, cols:], last[i][...]]

    branch_at[step] = dot(jnp.concatenate(by_quad(0), axis=1), wo_ref[...]).astype(BF)
    d_all = jnp.concatenate([a for i in (1, 2, 3) for a in by_quad(i)], axis=1)
    g_at[step] = dot_nt(d_all, wqkv_ref[...]).astype(BF)

    @pl.when(step == pl.num_programs(0) - 1)
    def _():
        def sample(b, carry):
            at = pl.ds(pl.multiple_of(b * 2 * GROUP, 2 * GROUP), 2 * GROUP)
            joined = lambda ref: jnp.concatenate([ref[n, at] for n in range(QUADS)], axis=1).astype(F32)
            x = x_ref[at, :].astype(F32)
            y = (x + joined(branch_at)).astype(BF)
            g = joined(g_at)
            centred = x - jnp.mean(x, axis=-1, keepdims=True)
            inv = lax.rsqrt(jnp.mean(centred * centred, axis=-1, keepdims=True) + EPS)
            normed = centred * inv
            gx = dy_ref[at, :].astype(F32) + inv * (
                g
                - jnp.mean(g, axis=-1, keepdims=True)
                - normed * jnp.mean(g * normed, axis=-1, keepdims=True)
            )
            for arr, (value, ref) in enumerate(((y, y_ref), (gx.astype(BF), gx_ref))):
                placed = dot(out_ref[...], value).astype(BF)
                back = dot(back_ref[...], value[GROUP:]).astype(BF)
                rim_ref[arr, b] = back
                kept = (SIDE if side == 0 else SIDE - SLON) * ROWS
                for level in range(levels):
                    start = level * SIDE * ROWS
                    ref[b, level] = placed[start : start + kept]
                    if side == 1:
                        lon_ref[arr, b, level] = placed[start + kept : start + SIDE * ROWS]
            return carry

        lax.fori_loop(0, HALF // (2 * GROUP), sample, 0)


def outputs(side, samples, xw, gw, w_qkv, w_out, first, second, last):
    width = w_out.shape[0]
    cols = width // QUADS
    out, back = pick_out(), pick_back()
    full = lambda shape: pl.BlockSpec(shape, lambda n: (0,) * len(shape))
    kept = (SIDE if side == 0 else SIDE - SLON) * ROWS
    shapes = [(samples, LEV, kept, width)] * 2 + [(2, samples, BACK, width)]
    if side == 1:
        shapes += [(2, samples, LEV, SLON * ROWS, width)]
    return pl.pallas_call(
        functools.partial(output_kernel, side),
        grid=(QUADS,),
        in_specs=[full(a.shape) for a in (out, back, xw, gw)]
        + [
            pl.BlockSpec((cols, 3 * width), lambda n: (n, 0)),
            pl.BlockSpec((width, cols), lambda n: (0, n)),
        ]
        + [pl.BlockSpec((HALF, 2 * cols), lambda n: (side, 0))] * 4
        + [pl.BlockSpec((HALF, cols), lambda n: (side, 0))] * 8,
        out_specs=[full(s) for s in shapes],
        out_shape=[jax.ShapeDtypeStruct(s, BF) for s in shapes],
        scratch_shapes=[pltpu.VMEM((QUADS, HALF, cols), BF)] * 2,
        compiler_params=params(14),
        cost_estimate=cost(8),
        name="outputs",
    )(out, back, xw, gw, w_qkv, w_out, *first[:4], *second[:4], *last[:4])


def replaced(mine, pick, rim):
    here = lax.broadcasted_iota(jnp.int32, mine.shape, 0) % ROWS < SLAT
    return jnp.where(here, dot(pick, rim).astype(BF), mine)


def patch_kernel(pick_ref, lon_ref, rim_ref, out_ref):
    for arr in range(2):
        for b in range(lon_ref.shape[1]):
            for level in range(lon_ref.shape[2]):
                out_ref[arr, b, level] = replaced(lon_ref[arr, b, level], pick_ref[level], rim_ref[arr, b])


def patch(lon, rim):
    return pl.pallas_call(
        patch_kernel,
        out_shape=jax.ShapeDtypeStruct(lon.shape, BF),
        compiler_params=params(12),
        cost_estimate=cost(1),
        name="patch",
    )(pick_place(SLON, SIDE - SLON), lon, rim)


def merge_kernel(place0_ref, place1_ref, y0, g0, y1, g1, rim0, rim1, lon, y_ref, gx_ref):
    levels = y_ref.shape[1]
    first, second = SLON * ROWS, (SLON + SIDE) * ROWS
    for arr, (low, high, out) in enumerate(((y0, y1, y_ref), (g0, g1, gx_ref))):
        for level in range(levels):
            out[0, level, :first] = lon[arr, 0, level]
            out[0, level, first:second] = replaced(low[0, level], place0_ref[level], rim0[arr, 0])
            out[0, level, second:] = replaced(high[0, level], place1_ref[level], rim1[arr, 0])


def merge(y0, g0, y1, g1, rim0, rim1, lon):
    samples, levels, _, width = y0.shape
    picks = [pick_place(SIDE, 0), pick_place(SIDE - SLON, 0)]
    full = lambda a: pl.BlockSpec(a.shape, lambda b: (0,) * a.ndim)
    own = lambda a: pl.BlockSpec((1,) + a.shape[1:], lambda b: (b,) + (0,) * (a.ndim - 1))
    strip = lambda a: pl.BlockSpec((2, 1) + a.shape[2:], lambda b: (0, b) + (0,) * (a.ndim - 2))
    shape = jax.ShapeDtypeStruct((samples, levels, COLS * ROWS, width), BF)
    return pl.pallas_call(
        merge_kernel,
        grid=(samples,),
        in_specs=[full(a) for a in picks]
        + [own(a) for a in (y0, g0, y1, g1)]
        + [strip(a) for a in (rim0, rim1, lon)],
        out_specs=[own(shape)] * 2,
        out_shape=[shape] * 2,
        compiler_params=params(12),
        cost_estimate=cost(4),
        name="merge",
    )(*picks, y0, g0, y1, g1, rim0, rim1, lon)


def shifted(value, axis, steps):
    count = lax.axis_size(axis)
    pairs = [(source, (source + steps) % count) for source in range(count)]
    return lax.ppermute(value, axis, pairs)


def shifted_both(value, steps):
    lon, lat = lax.axis_size("lon"), lax.axis_size("lat")
    pairs = [
        (i * lat + j, ((i + steps) % lon) * lat + (j + steps) % lat)
        for i in range(lon)
        for j in range(lat)
    ]
    return lax.ppermute(value, ("lon", "lat"), pairs)


def allowed_bias(mask_ids):
    lat_total = mask_ids.shape[0]
    start = lax.axis_index("lat") * ROWS + SLAT
    lat_global = (start + np.arange(ROWS, dtype=np.int32)) % lat_total
    wide = jnp.concatenate([mask_ids, mask_ids[:, :SLON]], axis=1)
    wide = jnp.concatenate([wide, wide[:SLAT]], axis=0)
    ids = lax.dynamic_slice(wide, (start, lax.axis_index("lon") * COLS + SLON), (ROWS, COLS))
    code = ids * 2 + (lat_global < SLAT).astype(jnp.int32)[:, None]
    code = code + 16 * (np.arange(COLS, dtype=np.int32) // WLON)[None, :]
    code = code.reshape(2, WLAT, 2, SIDE).transpose(2, 0, 1, 3).reshape(4, 1, WLAT * SIDE)
    code = jnp.broadcast_to(code, (4, LEV, WLAT * SIDE)).reshape(4, -1)
    code = jnp.pad(code, ((0, 0), (0, GROUP - code.shape[1])), constant_values=-1)
    same = code[:, :, None] == code[:, None, :]
    return jnp.where(same, 0.0, -jnp.inf).astype(F32)


def swapped(value, axis):
    return lax.ppermute(value, axis, [(0, 1), (1, 0)])


def to_distance(value, dx=0, dy=0, dz=0):
    pairs = []
    for lon in range(X * Y * Z):
        x, y, z = place_of(lon)
        pairs.append((lon, ((z + dz) % Z * Y + (y + dy) % Y) * X + (x + dx) % X))
    return lax.ppermute(value, "lon", pairs)


def added(*terms):
    total = terms[0].astype(F32)
    for term in terms[1:]:
        total = total + term.astype(F32)
    return total


def ring_sum(chunks, name):
    got = [to_distance(chunks[d], **{name: d}) for d in range(1, len(chunks))]
    return added(chunks[0], *got)


def relay(chunks, name):
    half = chunks[2].shape[0] // 2
    return [to_distance(chunks[2][:half], **{name: 1}), to_distance(chunks[2][half:], **{name: 3})]


def with_relayed(chunks, got):
    half = got[0].shape[0]
    up = jnp.concatenate([added(chunks[1][:half], got[0]).astype(BF), chunks[1][half:]], axis=0)
    down = jnp.concatenate([chunks[3][:half], added(chunks[3][half:], got[1]).astype(BF)], axis=0)
    return [up, down]


def both_ways(pair, name):
    return [to_distance(pair[0], **{name: 1}), to_distance(pair[1], **{name: 3})]


def swap_sum(keep, got):
    return added(keep, got).astype(BF)


def chunks_by_z(total):
    total = total.reshape(X, Z, Y * UNIT, -1)
    return [total[:, d].reshape(X * Y * UNIT, -1) for d in range(Z)]


def chunks_by_x(total):
    return jnp.split(total, X)


def chunks_with_out(qkv, outs):
    _, y0, z0 = place_of(lax.axis_index("lon"))
    outs = jnp.stack(outs).reshape(Z, X, Y, UNIT, -1)
    outs = jnp.where(y0 == 0, outs, outs[:, :, ::-1]).reshape(Z, X * Y * UNIT, -1)
    return [
        jnp.concatenate([chunk, lax.dynamic_index_in_dim(outs, (z0 + d) % Z, keepdims=False)], axis=1)
        for d, chunk in enumerate(chunks_by_z(qkv))
    ]


def final_sums(total):
    cols = total.shape[1] // 8
    piece = [total[:, i * cols : (i + 1) * cols] for i in range(8)]
    pick = lambda *which: jnp.concatenate([piece[i] for i in which], axis=1)
    lat0 = lax.axis_index("lat") == 0
    low = jnp.where(lat0, pick(0, 3, 1, 4), pick(2, 7, 0, 4))
    high = jnp.where(lat0, pick(6, 2, 7, 5), pick(3, 1, 6, 5))
    dp0 = lax.axis_index("dp") == 0
    got = swapped(jnp.where(dp0, high, low), "dp")
    total = added(jnp.where(dp0, low, high), got)
    return total[:, : 3 * cols], total[:, 3 * cols :]


def per_device(fields, grad_y, w_qkv, w_out, mask_ids):
    samples, levels, lat_rows, lon_cols, width = fields.shape
    flat = lambda a: a.transpose(0, 1, 3, 2, 4).reshape(samples, levels, lon_cols * lat_rows, width)
    f, g = flat(fields), flat(grad_y)
    pos = jnp.stack([lax.axis_index("lon"), lax.axis_index("lat")]).astype(jnp.int32)
    lon_out, rim_out, cor_out = strips(f, g)
    rim_in = shifted(rim_out, "lat", -1)
    cor_in = shifted_both(cor_out, -1)
    lon_in = shifted(lon_out, "lon", -1)
    bias = allowed_bias(mask_ids)
    side0 = project(0, pos, f, g, lon_out, rim_in, cor_out, w_qkv, w_out)
    side1 = project(1, pos, f, g, lon_in, rim_in, cor_in, w_qkv, w_out)
    sides = (side0, side1)
    barrier = lax.optimization_barrier
    first = attention((0, 2), pos, bias, sides)
    by_z = chunks_by_z(swap_sum(first[4], swapped(first[5], "lat")))
    outs = swap_sum(first[6], swapped(first[7], "lat"))
    by_z, pos1 = barrier((by_z, pos))
    got_z = relay(by_z, "dz")
    second = attention((1,), pos1, bias, sides)
    got_z, before, send = barrier((got_z, second[6], second[5]))
    ways, before = barrier((with_relayed(by_z, got_z), before))
    got_z = both_ways(ways, "dz")
    last = attention((3,), pos, bias, sides, before=before)
    got_z, send, send_last = barrier((got_z, send, last[5]))
    first_total = added(by_z[0], *got_z).astype(BF).reshape(X, Y * UNIT, -1)
    got, got_last = swapped(send, "lat"), swapped(send_last, "lat")
    total = swap_sum(second[4], got)
    cols = total.shape[1]
    out = jnp.concatenate([total[-2 * cols : -cols], total[-cols:]], axis=1)
    total_last = swap_sum(last[4], got_last)
    outs = [outs[:cols], out, outs[cols:], total_last[-cols:]]
    by_x = chunks_by_x(total_last[:-cols])
    by_z = chunks_with_out(total[: -2 * cols], outs)
    by_x, by_z, att = barrier((by_x, by_z, last[0]))
    got_x, got_z = relay(by_x, "dx"), relay(by_z, "dz")
    last = (att, *last[1:])
    y1, g1, rim1, lon = outputs(1, samples, *side1[:2], w_qkv, w_out, first, second, last)
    rim1 = shifted(rim1, "lat", 1)
    got_x, got_z, lon = barrier((got_x, got_z, lon))
    ways_x, ways_z = with_relayed(by_x, got_x), with_relayed(by_z, got_z)
    lon = patch(lon, rim1)
    ways_x, ways_z, lon, xw0 = barrier((ways_x, ways_z, lon, side0[0]))
    got_x, got_z = both_ways(ways_x, "dx"), both_ways(ways_z, "dz")
    lon = shifted(lon, "lon", 1)
    y0, g0, rim0 = outputs(0, samples, xw0, side0[1], w_qkv, w_out, first, second, last)
    got_x, got_z, rim0 = barrier((got_x, got_z, rim0))
    rim0 = shifted(rim0, "lat", 1)
    by_z_own = by_z[0]
    by_z = added(by_x[0], *got_x).astype(BF).reshape(Z, Y * UNIT, -1)
    total_z = added(by_z_own, *got_z).astype(BF).reshape(X, Y * UNIT, -1)
    by_x = [jnp.concatenate([first_total[d], total_z[d]], axis=1) for d in range(X)]
    total_z = ring_sum(list(by_z), "dz")
    total = jnp.concatenate([ring_sum(by_x, "dx").astype(BF), total_z.astype(BF)], axis=1)
    total = total.reshape(Y, UNIT, -1)
    got_y = to_distance(total[1], dy=1)
    y, gx = merge(y0, g0, y1, g1, rim0, rim1, lon)
    got_y, y, gx = barrier((got_y, y, gx))
    sums = final_sums(added(total[0], got_y).astype(BF))
    unflat = lambda a: a.reshape(samples, levels, lon_cols, lat_rows, width).transpose(0, 1, 3, 2, 4)
    return (unflat(y), unflat(gx), *sums)


def solution(mesh):
    grid = P("dp", None, "lat", "lon", None)
    return jax.shard_map(
        per_device,
        mesh=mesh,
        in_specs=(grid, grid, P(), P(), P()),
        out_specs=(grid, grid, P("lon", ("lat", "dp")), P("lon", ("lat", "dp"))),
        check_vma=False,
    )
```

```python
import functools

import jax
import jax.numpy as jnp
import numpy as np
from jax import lax
from jax.experimental import pallas as pl
from jax.experimental.pallas import tpu as pltpu
from jax.sharding import PartitionSpec as P

HEADS = 16
LEV = 3
WLAT = 4
WLON = 5
SLAT = 2
SLON = 2
ROWS = 8
COLS = 20
EPS = 1e-05

SIDE = 2 * WLON
GROUP = 128
HALF = 4 * GROUP
OWN = LEV * SIDE * ROWS
RIM = 128
COR = 16
BACK = 64
QUADS = 4
SCALE = 0.125
BF = jnp.bfloat16
F32 = jnp.float32
NT = (((1,), (1,)), ((), ()))

X, Y, Z = 4, 2, 4
UNIT = 32
LON, LAT = 0, 1


def params(mebibytes):
    return pltpu.CompilerParams(vmem_limit_bytes=mebibytes * 1024 * 1024)


def cost(micros):
    return pl.CostEstimate(flops=int(micros * 1.1e9), bytes_accessed=10**6, transcendentals=0)


SCALARS = pl.BlockSpec(memory_space=pltpu.SMEM)
IN_HBM = pl.BlockSpec(memory_space=pltpu.HBM)


def in_hbm(a):
    return pltpu.with_memory_space_constraint(a, pltpu.HBM)


def dot(a, b):
    return jnp.dot(a, b, preferred_element_type=F32)


def dot_nt(a, b):
    return lax.dot_general(a, b, NT, preferred_element_type=F32)


def place_of(lon):
    return lon % X, (lon // X) % Y, lon // (X * Y)


def relative(block, pos_ref):
    lon = pos_ref[LON]
    x, y, z = place_of(block)
    x0, y0, z0 = lax.rem(lon, X), lax.rem(lax.div(lon, X), Y), lax.div(lon, X * Y)
    dx, dy, dz = lax.rem(x - x0 + X, X), lax.rem(y - y0 + Y, Y), lax.rem(z - z0 + Z, Z)
    return (dx * Z + dz) * Y + dy


def token(level, r, c):
    return (level * WLAT + r) * SIDE + c


def every():
    for level in range(LEV):
        for c in range(SIDE):
            for i in range(ROWS):
                wr, r = divmod((i - SLAT) % ROWS, WLAT)
                yield level, c, i, wr, r


def one_hot(shape, places):
    out = np.zeros(shape, np.float32)
    for at in places:
        out[at] = 1.0
    return jnp.asarray(out.astype(jnp.bfloat16))


def pick_own():
    return one_hot(
        (2, GROUP, OWN),
        [
            (wr, token(level, r, c), (level * SIDE + c) * ROWS + i)
            for level, c, i, wr, r in every()
            if i >= SLAT
        ],
    )


def pick_rim(side):
    places = []
    for level, c, i, wr, r in every():
        if i < SLAT:
            column = SLON + side * SIDE + c
            if column < COLS:
                src = (level * COLS + column) * SLAT + i
            else:
                src = RIM + (level * SLON + column - COLS) * SLAT + i
            places.append((token(level, r, c), src))
    return one_hot((GROUP, RIM + COR), places)


def pick_out():
    return one_hot(
        (OWN, 2 * GROUP),
        [
            ((level * SIDE + c) * ROWS + i, wr * GROUP + token(level, r, c))
            for level, c, i, wr, r in every()
        ],
    )


def pick_back():
    return one_hot(
        (BACK, GROUP),
        [
            ((level * SIDE + c) * SLAT + i, token(level, r, c))
            for level, c, i, wr, r in every()
            if i < SLAT
        ],
    )


def pick_strip():
    rim = [
        ((level * COLS + column) * SLAT + i, (level * COLS + column) * ROWS + i)
        for level in range(LEV)
        for column in range(COLS)
        for i in range(SLAT)
    ]
    cor = [
        (RIM + (level * SLON + column) * SLAT + i, (level * COLS + column) * ROWS + i)
        for level in range(LEV)
        for column in range(SLON)
        for i in range(SLAT)
    ]
    return one_hot((RIM + COR, LEV * COLS * ROWS), rim + cor)


def pick_place(columns, start):
    return one_hot(
        (LEV, columns * ROWS, BACK),
        [
            (level, c * ROWS + i, (level * SIDE + start + c) * SLAT + i)
            for level in range(LEV)
            for c in range(columns)
            for i in range(SLAT)
        ],
    )


def strips_kernel(pick_ref, f_ref, g_ref, lon_ref, rim_ref, cor_ref):
    for arr, ref in enumerate((f_ref, g_ref)):
        block = ref[0]
        lon_ref[arr, 0] = block[:, : SLON * ROWS]
        strip = dot(pick_ref[...], block.reshape(-1, block.shape[-1])).astype(BF)
        rim_ref[arr, 0] = strip[:RIM]
        cor_ref[arr, 0] = strip[RIM:]


def strips(f, g):
    samples, levels, rows, width = f.shape
    pick = pick_strip()
    block = pl.BlockSpec((1, levels, rows, width), lambda b: (b, 0, 0, 0))
    shapes = [(levels, SLON * ROWS, width), (RIM, width), (COR, width)]
    return pl.pallas_call(
        strips_kernel,
        grid=(samples,),
        in_specs=[pl.BlockSpec(pick.shape, lambda b: (0, 0)), block, block],
        out_specs=[
            pl.BlockSpec((2, 1) + s, lambda b, n=len(s): (0, b) + (0,) * n) for s in shapes
        ],
        out_shape=[jax.ShapeDtypeStruct((2, samples) + s, BF) for s in shapes],
        compiler_params=params(56),
        cost_estimate=cost(3),
        name="strips",
    )(pick, f, g)


def project_kernel(side, pos_ref, own_ref, pick_ref, f_ref, g_ref, wq_ref, wk_ref, wv_ref, wo_ref, rim_ref, *rest):
    if side == 1:
        lon_ref, cor_ref, rest = rest[0], rest[1], rest[2:]
    xw_ref, gw_ref, nt_ref, q_ref, k_ref, v_ref, da_ref, nw, tokens, sems = rest
    samples, levels, _, width = f_ref.shape
    kept = tokens.shape[3]
    start = (SLON if side == 0 else SLON + SIDE) * ROWS

    @pl.when(pl.program_id(0) == 0)
    def _():
        copies = [
            pltpu.make_async_copy(ref.at[:, :, start : start + kept], tokens.at[arr], sems.at[arr])
            for arr, ref in enumerate((f_ref, g_ref))
        ]
        for copy in copies:
            copy.start()
        for copy in copies:
            copy.wait()
        for b in range(samples):
            got = []
            for arr in range(2):
                parts = []
                for level in range(levels):
                    parts.append(tokens[arr, b, level])
                    if side == 1:
                        parts.append(lon_ref[arr, b, level])
                rim = rim_ref[arr, b]
                if side == 1:
                    rim = jnp.concatenate([rim, cor_ref[arr, b]], axis=0)
                got.append((jnp.concatenate(parts, axis=0), rim))
            for wr in range(2):
                at = slice((b * 2 + wr) * GROUP, (b * 2 + wr + 1) * GROUP)
                x, g = (dot(own_ref[wr], own) for own, _ in got)
                if wr == 1:
                    x, g = (a + dot(pick_ref[...], rim) for a, (_, rim) in zip((x, g), got))
                gw_ref[at, :] = g.astype(BF)
                xw_ref[at, :] = x.astype(BF)
                centred = x - jnp.mean(x, axis=-1, keepdims=True)
                inv = lax.rsqrt(jnp.mean(centred * centred, axis=-1, keepdims=True) + EPS)
                normed = (centred * inv).astype(BF)
                nw[at, :] = normed
                turned = normed.T
                for block in range(width // UNIT):
                    dst = pl.multiple_of(relative(block, pos_ref) * UNIT, UNIT)
                    nt_ref[pl.ds(dst, UNIT), at] = turned[block * UNIT : (block + 1) * UNIT]

    q_ref[...] = dot(nw[...], wq_ref[...]).astype(BF)
    k_ref[...] = dot(nw[...], wk_ref[...]).astype(BF)
    v_ref[...] = dot(nw[...], wv_ref[...]).astype(BF)
    da_ref[...] = dot_nt(gw_ref[...], wo_ref[...]).astype(BF)


def project(side, pos, f, g, lon_in, rim_in, cor_in, w_qkv, w_out):
    samples, levels, _, width = f.shape
    cols = width // QUADS
    whole = lambda n: (0, 0)
    full = lambda a: pl.BlockSpec(a.shape, lambda n: (0,) * a.ndim)
    kept = (SIDE if side == 0 else SIDE - SLON) * ROWS
    own, pick = pick_own(), pick_rim(side)
    if side == 0:
        pick = pick[:, :RIM]
    halos = (rim_in,) if side == 0 else (rim_in, lon_in, cor_in)
    tall = jax.ShapeDtypeStruct((HALF, width), BF)
    return pl.pallas_call(
        functools.partial(project_kernel, side),
        grid=(QUADS,),
        in_specs=[SCALARS, full(own), full(pick), IN_HBM, IN_HBM]
        + [
            pl.BlockSpec((width, cols), lambda n: (0, n)),
            pl.BlockSpec((width, cols), lambda n: (0, QUADS + n)),
            pl.BlockSpec((width, cols), lambda n: (0, 2 * QUADS + n)),
            pl.BlockSpec((cols, width), lambda n: (n, 0)),
        ]
        + [full(a) for a in halos],
        out_specs=[
            pl.BlockSpec((HALF, width), whole),
            pl.BlockSpec((HALF, width), whole),
            pl.BlockSpec((width, HALF), whole),
        ]
        + [pl.BlockSpec((HALF, cols), lambda n: (0, n))] * 4,
        out_shape=[pltpu.HBM((HALF, width), BF), tall, jax.ShapeDtypeStruct((width, HALF), BF)] + [tall] * 4,
        scratch_shapes=[
            pltpu.VMEM((HALF, width), BF),
            pltpu.VMEM((2, samples, levels, kept, width), BF),
            pltpu.SemaphoreType.DMA((2,)),
        ],
        compiler_params=params(20),
        cost_estimate=cost(9),
        name="project",
    )(pos, own, pick, in_hbm(f), in_hbm(g), w_qkv, w_qkv, w_qkv, w_out, *halos)


def attention_kernel(quads, pos_ref, bias_ref, *rest):
    sides, rest = [rest[:6], rest[6:12]], rest[12:]
    copies = []
    if len(quads) == 1:
        *rest, part, sems = rest
        at = slice(quads[0] * (part.shape[2]), (quads[0] + 1) * part.shape[2])
        copies = [
            pltpu.make_async_copy(sides[1][2 + i].at[:, at], part.at[i], sems.at[i]) for i in range(4)
        ]
        sides[1] = (*sides[1][:2], *(part.at[i] for i in range(4)))
        for copy in copies:
            copy.start()
    if quads == (3,):
        kin_ref, rest = rest[0], rest[1:]
    if quads == (1,):
        att_ref, dq_ref, dk_ref, dv_ref, keep_ref, send_ref, kout_ref, att_t = rest
    elif quads == (3,):
        att_ref, dq_ref, dk_ref, dv_ref, keep_ref, send_ref, att_t = rest
    else:
        att_ref, dq_ref, dk_ref, dv_ref, keep_ref, send_ref, gok_ref, gos_ref, att_t = rest
    width = sides[0][0].shape[0]
    cols = width // QUADS
    head = 64
    lat0 = pos_ref[LAT] == 0
    x0 = lax.rem(pos_ref[LON], X)
    first = lax.broadcasted_iota(jnp.int32, (GROUP, 2 * head), 1) < head
    upper = lax.broadcasted_iota(jnp.int32, (2 * head, GROUP), 0) < head
    zero = jnp.zeros((GROUP, 2 * head), BF)

    def split(pair):
        return jnp.concatenate([jnp.where(first, pair, zero), jnp.where(first, zero, pair)], axis=0)

    def beside(turned):
        return jnp.concatenate(
            [jnp.where(upper, turned, zero), jnp.where(upper, zero, turned)], axis=1
        )

    def stacked(both):
        return jnp.concatenate([both[:, :GROUP], both[:, GROUP:]], axis=0)

    def lanes(start, size):
        return pl.ds(start if isinstance(start, int) else pl.multiple_of(start, 128), size)

    def unit(refs, side, group, wr, pair, src, dst):
        _, _, q_ref, k_ref, v_ref, da_ref = refs
        at = (pl.ds(pl.multiple_of(group * GROUP, GROUP), GROUP), lanes(src + pair * 128, 128))
        here = pl.ds(pl.multiple_of(side * HALF + group * GROUP, GROUP), GROUP)
        both = lanes(dst + pair * 128, 128)
        bias = bias_ref[side * 2 + wr]
        q, k, v, da = q_ref[at], k_ref[at], v_ref[at], da_ref[at]
        q2, da2 = split(q * SCALE), split(da)
        scores = dot_nt(k, q2)
        d_prob = dot_nt(v, da2)
        yield
        scores = scores + jnp.concatenate([bias, bias], axis=1)
        top = jnp.max(scores, axis=0, keepdims=True)
        expd = jnp.exp(scores - top)
        prob = expd * (1.0 / jnp.sum(expd, axis=0, keepdims=True))
        prob16 = prob.astype(BF)
        part = prob * d_prob
        delta = jnp.sum(part, axis=0, keepdims=True)
        d_score = (part - prob * delta).astype(BF)
        yield
        out_t = dot(beside(v.T), stacked(prob16)).astype(BF)
        dq_t = dot(beside((k * SCALE).T), stacked(d_score)).astype(BF)
        dv_ref[here, both] = dot(prob16, da2).astype(BF)
        dk_ref[here, both] = dot(d_score, q2).astype(BF)
        yield
        att_ref[here, both] = out_t.T
        for block in range(128 // UNIT):
            row = lax.rem(block - x0 + X, X) * (2 * UNIT) + pair * UNIT
            att_t[pl.ds(pl.multiple_of(row, UNIT), UNIT), here] = out_t[
                block * UNIT : (block + 1) * UNIT
            ]
        dq_ref[here, both] = dq_t.T
        yield

    low, high = slice(0, HALF), slice(HALF, 2 * HALF)

    def units(src, dst):
        for side in range(2):
            if side == 1:
                for copy in copies:
                    copy.wait()

            def sample(b, carry):
                works = [
                    unit(sides[side], side, b * 2 + wr, wr, pair, src, dst)
                    for wr in range(2)
                    for pair in range(2)
                ]
                for _ in range(4):
                    for work in works:
                        next(work)
                return carry

            lax.fori_loop(0, HALF // (2 * GROUP), sample, 0)

    def out_sums():
        grad_out = dot(att_t[:, low], sides[0][1][...]) + dot(att_t[:, high], sides[1][1][...])
        left, right = grad_out[:, : width // 2], grad_out[:, width // 2 :]
        return jnp.where(lat0, left, right).astype(BF), jnp.where(lat0, right, left).astype(BF)

    def qkv_sums(store, dst):
        def piece(i, carry):
            at = pl.ds(pl.multiple_of(i * 256, 256), 256)
            left = (sides[0][0][at, :], sides[1][0][at, :])
            of_q, of_k, of_v = (
                dot(left[0], ref[low, lanes(dst, cols)]) + dot(left[1], ref[high, lanes(dst, cols)])
                for ref in (dq_ref, dk_ref, dv_ref)
            )
            mine = jnp.where(lat0, of_q, of_v).astype(BF)
            other = jnp.where(lat0, of_v, of_q).astype(BF)
            store(at, mine, other, of_k.astype(BF))
            return carry

        lax.fori_loop(0, width // 256, piece, 0)

    if quads == (0, 2):

        units(0, 0)
        gok_ref[...], gos_ref[...] = out_sums()
        n = pl.program_id(0)
        stays = jnp.logical_xor(lat0, n == 1)

        def store(at, mine, other, of_k):
            keep_ref[at, lanes(n * cols, cols)] = mine
            send_ref[at, lanes(n * cols, cols)] = other

            @pl.when(stays)
            def _():
                keep_ref[at, 2 * cols :] = of_k

            @pl.when(jnp.logical_not(stays))
            def _():
                send_ref[at, 2 * cols :] = of_k

        qkv_sums(store, 0)
        return

    units(0, 0)
    mine, other = out_sums()
    if quads == (1,):
        for half in range(2):
            below = slice(width + half * cols, width + (half + 1) * cols)
            keep_ref[below, :] = mine[:, half * cols : (half + 1) * cols]
            send_ref[below, :] = other[:, half * cols : (half + 1) * cols]
    else:
        keep_ref[width:, :] = mine
        send_ref[width:, :] = other

    def store(at, mine, other, of_k):
        keep_ref[at, :cols] = mine
        send_ref[at, :cols] = other
        if quads == (1,):
            kout_ref[at, :] = of_k
        else:
            before = kin_ref[at, :]
            keep_ref[at, cols:] = jnp.where(lat0, before, of_k)
            send_ref[at, cols:] = jnp.where(lat0, of_k, before)

    qkv_sums(store, 0)


def attention(quads, pos, bias, sides, before=None):
    width = sides[0][0].shape[1]
    cols = width // QUADS
    count = len(quads)
    rows = 2 * HALF

    def quad(n):
        return 2 * n if count == 2 else quads[0]

    whole = lambda n: (0, 0)
    in_specs = [SCALARS, pl.BlockSpec(bias.shape, lambda n: (0, 0, 0))]
    operands = [pos, bias]
    for side, (_, gw, nt, *columns) in enumerate(sides):
        in_specs += [pl.BlockSpec((width, HALF), whole), pl.BlockSpec((HALF, width), whole)]
        operands += [nt, gw]
        if count == 1 and side == 1:
            in_specs += [IN_HBM] * 4
            operands += [in_hbm(a) for a in columns]
        else:
            in_specs += [pl.BlockSpec((HALF, cols), lambda n: (0, quad(n)))] * 4
            operands += columns
    if before is not None:
        in_specs.append(pl.BlockSpec((width, cols), whole))
        operands.append(before)
    out_specs = [pl.BlockSpec((rows, cols), lambda n: (0, n))] * 4
    shapes = [(rows, count * cols)] * 4
    sums = {0: (width, 3 * cols), 1: (width + 2 * cols, cols), 3: (width + cols, 2 * cols)}[quads[0]]
    out_specs += [pl.BlockSpec(sums, whole)] * 2
    shapes += [sums] * 2
    if quads == (0, 2):
        out_specs += [pl.BlockSpec((cols, width // 2), lambda n: (n, 0))] * 2
        shapes += [(count * cols, width // 2)] * 2
    elif quads == (1,):
        out_specs += [pl.BlockSpec((width, cols), whole)]
        shapes += [(width, cols)]
    return pl.pallas_call(
        functools.partial(attention_kernel, quads),
        grid=(count,),
        in_specs=in_specs,
        out_specs=out_specs,
        out_shape=[pltpu.HBM(s, BF) if n < 4 and count == 2 else jax.ShapeDtypeStruct(s, BF) for n, s in enumerate(shapes)],
        scratch_shapes=[pltpu.VMEM((cols, 2 * HALF), BF)]
        + ([pltpu.VMEM((4, HALF, cols), BF), pltpu.SemaphoreType.DMA((4,))] if count == 1 else []),
        compiler_params=params(20),
        cost_estimate=cost(11 * count),
        name="attention",
    )(*operands)


def output_kernel(side, out_ref, back_ref, x_ref, dy_ref, wqkv_ref, wo_ref, *rest):
    first, second, last = rest[:4], rest[4:8], rest[8:12]
    if side == 0:
        y_ref, gx_ref, rim_ref, branch_at, g_at = rest[12:]
    else:
        y_ref, gx_ref, rim_ref, lon_ref, branch_at, g_at = rest[12:]
    levels = y_ref.shape[1]
    cols = last[0].shape[1]
    step = pl.program_id(0)

    def by_quad(i):
        return [first[i][:, :cols], second[i][...], first[i][:, cols:], last[i][...]]

    branch_at[step] = dot(jnp.concatenate(by_quad(0), axis=1), wo_ref[...]).astype(BF)
    d_all = jnp.concatenate([a for i in (1, 2, 3) for a in by_quad(i)], axis=1)
    g_at[step] = dot_nt(d_all, wqkv_ref[...]).astype(BF)

    @pl.when(step == pl.num_programs(0) - 1)
    def _():
        def sample(b, carry):
            at = pl.ds(pl.multiple_of(b * 2 * GROUP, 2 * GROUP), 2 * GROUP)
            joined = lambda ref: jnp.concatenate([ref[n, at] for n in range(QUADS)], axis=1).astype(F32)
            x = x_ref[at, :].astype(F32)
            y = (x + joined(branch_at)).astype(BF)
            g = joined(g_at)
            centred = x - jnp.mean(x, axis=-1, keepdims=True)
            inv = lax.rsqrt(jnp.mean(centred * centred, axis=-1, keepdims=True) + EPS)
            normed = centred * inv
            gx = dy_ref[at, :].astype(F32) + inv * (
                g
                - jnp.mean(g, axis=-1, keepdims=True)
                - normed * jnp.mean(g * normed, axis=-1, keepdims=True)
            )
            for arr, (value, ref) in enumerate(((y, y_ref), (gx.astype(BF), gx_ref))):
                placed = dot(out_ref[...], value).astype(BF)
                back = dot(back_ref[...], value[GROUP:]).astype(BF)
                rim_ref[arr, b] = back
                kept = (SIDE if side == 0 else SIDE - SLON) * ROWS
                for level in range(levels):
                    start = level * SIDE * ROWS
                    ref[b, level] = placed[start : start + kept]
                    if side == 1:
                        lon_ref[arr, b, level] = placed[start + kept : start + SIDE * ROWS]
            return carry

        lax.fori_loop(0, HALF // (2 * GROUP), sample, 0)


def outputs(side, samples, xw, gw, w_qkv, w_out, first, second, last):
    width = w_out.shape[0]
    cols = width // QUADS
    out, back = pick_out(), pick_back()
    full = lambda shape: pl.BlockSpec(shape, lambda n: (0,) * len(shape))
    kept = (SIDE if side == 0 else SIDE - SLON) * ROWS
    shapes = [(samples, LEV, kept, width)] * 2 + [(2, samples, BACK, width)]
    if side == 1:
        shapes += [(2, samples, LEV, SLON * ROWS, width)]
    return pl.pallas_call(
        functools.partial(output_kernel, side),
        grid=(QUADS,),
        in_specs=[full(a.shape) for a in (out, back, xw, gw)]
        + [
            pl.BlockSpec((cols, 3 * width), lambda n: (n, 0)),
            pl.BlockSpec((width, cols), lambda n: (0, n)),
        ]
        + [pl.BlockSpec((HALF, 2 * cols), lambda n: (side, 0))] * 4
        + [pl.BlockSpec((HALF, cols), lambda n: (side, 0))] * 8,
        out_specs=[full(s) for s in shapes],
        out_shape=[jax.ShapeDtypeStruct(s, BF) for s in shapes],
        scratch_shapes=[pltpu.VMEM((QUADS, HALF, cols), BF)] * 2,
        compiler_params=params(14),
        cost_estimate=cost(8),
        name="outputs",
    )(out, back, xw, gw, w_qkv, w_out, *first[:4], *second[:4], *last[:4])


def replaced(mine, pick, rim):
    here = lax.broadcasted_iota(jnp.int32, mine.shape, 0) % ROWS < SLAT
    return jnp.where(here, dot(pick, rim).astype(BF), mine)


def patch_kernel(pick_ref, lon_ref, rim_ref, out_ref):
    for arr in range(2):
        for b in range(lon_ref.shape[1]):
            for level in range(lon_ref.shape[2]):
                out_ref[arr, b, level] = replaced(lon_ref[arr, b, level], pick_ref[level], rim_ref[arr, b])


def patch(lon, rim):
    return pl.pallas_call(
        patch_kernel,
        out_shape=jax.ShapeDtypeStruct(lon.shape, BF),
        compiler_params=params(12),
        cost_estimate=cost(1),
        name="patch",
    )(pick_place(SLON, SIDE - SLON), lon, rim)


def merge_kernel(place0_ref, place1_ref, y0, g0, y1, g1, rim0, rim1, lon, y_ref, gx_ref):
    levels = y_ref.shape[1]
    first, second = SLON * ROWS, (SLON + SIDE) * ROWS
    for arr, (low, high, out) in enumerate(((y0, y1, y_ref), (g0, g1, gx_ref))):
        for level in range(levels):
            out[0, level, :first] = lon[arr, 0, level]
            out[0, level, first:second] = replaced(low[0, level], place0_ref[level], rim0[arr, 0])
            out[0, level, second:] = replaced(high[0, level], place1_ref[level], rim1[arr, 0])


def merge(y0, g0, y1, g1, rim0, rim1, lon):
    samples, levels, _, width = y0.shape
    picks = [pick_place(SIDE, 0), pick_place(SIDE - SLON, 0)]
    full = lambda a: pl.BlockSpec(a.shape, lambda b: (0,) * a.ndim)
    own = lambda a: pl.BlockSpec((1,) + a.shape[1:], lambda b: (b,) + (0,) * (a.ndim - 1))
    strip = lambda a: pl.BlockSpec((2, 1) + a.shape[2:], lambda b: (0, b) + (0,) * (a.ndim - 2))
    shape = jax.ShapeDtypeStruct((samples, levels, COLS * ROWS, width), BF)
    return pl.pallas_call(
        merge_kernel,
        grid=(samples,),
        in_specs=[full(a) for a in picks]
        + [own(a) for a in (y0, g0, y1, g1)]
        + [strip(a) for a in (rim0, rim1, lon)],
        out_specs=[own(shape)] * 2,
        out_shape=[shape] * 2,
        compiler_params=params(12),
        cost_estimate=cost(4),
        name="merge",
    )(*picks, y0, g0, y1, g1, rim0, rim1, lon)


def shifted(value, axis, steps):
    count = lax.axis_size(axis)
    pairs = [(source, (source + steps) % count) for source in range(count)]
    return lax.ppermute(value, axis, pairs)


def shifted_both(value, steps):
    lon, lat = lax.axis_size("lon"), lax.axis_size("lat")
    pairs = [
        (i * lat + j, ((i + steps) % lon) * lat + (j + steps) % lat)
        for i in range(lon)
        for j in range(lat)
    ]
    return lax.ppermute(value, ("lon", "lat"), pairs)


def allowed_bias(mask_ids):
    lat_total = mask_ids.shape[0]
    start = lax.axis_index("lat") * ROWS + SLAT
    lat_global = (start + np.arange(ROWS, dtype=np.int32)) % lat_total
    wide = jnp.concatenate([mask_ids, mask_ids[:, :SLON]], axis=1)
    wide = jnp.concatenate([wide, wide[:SLAT]], axis=0)
    ids = lax.dynamic_slice(wide, (start, lax.axis_index("lon") * COLS + SLON), (ROWS, COLS))
    code = ids * 2 + (lat_global < SLAT).astype(jnp.int32)[:, None]
    code = code + 16 * (np.arange(COLS, dtype=np.int32) // WLON)[None, :]
    code = code.reshape(2, WLAT, 2, SIDE).transpose(2, 0, 1, 3).reshape(4, 1, WLAT * SIDE)
    code = jnp.broadcast_to(code, (4, LEV, WLAT * SIDE)).reshape(4, -1)
    code = jnp.pad(code, ((0, 0), (0, GROUP - code.shape[1])), constant_values=-1)
    same = code[:, :, None] == code[:, None, :]
    return jnp.where(same, 0.0, -jnp.inf).astype(F32)


def swapped(value, axis):
    return lax.ppermute(value, axis, [(0, 1), (1, 0)])


def to_distance(value, dx=0, dy=0, dz=0):
    pairs = []
    for lon in range(X * Y * Z):
        x, y, z = place_of(lon)
        pairs.append((lon, ((z + dz) % Z * Y + (y + dy) % Y) * X + (x + dx) % X))
    return lax.ppermute(value, "lon", pairs)


def added(*terms):
    total = terms[0].astype(F32)
    for term in terms[1:]:
        total = total + term.astype(F32)
    return total


def ring_sum(chunks, name):
    got = [to_distance(chunks[d], **{name: d}) for d in range(1, len(chunks))]
    return added(chunks[0], *got)


def relay(chunks, name):
    half = chunks[2].shape[0] // 2
    return [to_distance(chunks[2][:half], **{name: 1}), to_distance(chunks[2][half:], **{name: 3})]


def with_relayed(chunks, got):
    half = got[0].shape[0]
    up = jnp.concatenate([added(chunks[1][:half], got[0]).astype(BF), chunks[1][half:]], axis=0)
    down = jnp.concatenate([chunks[3][:half], added(chunks[3][half:], got[1]).astype(BF)], axis=0)
    return [up, down]


def both_ways(pair, name):
    return [to_distance(pair[0], **{name: 1}), to_distance(pair[1], **{name: 3})]


def swap_sum(keep, got):
    return added(keep, got).astype(BF)


def chunks_by_z(total):
    total = total.reshape(X, Z, Y * UNIT, -1)
    return [total[:, d].reshape(X * Y * UNIT, -1) for d in range(Z)]


def chunks_by_x(total):
    return jnp.split(total, X)


def chunks_with_out(qkv, outs):
    _, y0, z0 = place_of(lax.axis_index("lon"))
    outs = jnp.stack(outs).reshape(Z, X, Y, UNIT, -1)
    outs = jnp.where(y0 == 0, outs, outs[:, :, ::-1]).reshape(Z, X * Y * UNIT, -1)
    return [
        jnp.concatenate([chunk, lax.dynamic_index_in_dim(outs, (z0 + d) % Z, keepdims=False)], axis=1)
        for d, chunk in enumerate(chunks_by_z(qkv))
    ]


def final_sums(total):
    cols = total.shape[1] // 8
    piece = [total[:, i * cols : (i + 1) * cols] for i in range(8)]
    pick = lambda *which: jnp.concatenate([piece[i] for i in which], axis=1)
    lat0 = lax.axis_index("lat") == 0
    low = jnp.where(lat0, pick(0, 3, 1, 4), pick(2, 7, 0, 4))
    high = jnp.where(lat0, pick(6, 2, 7, 5), pick(3, 1, 6, 5))
    dp0 = lax.axis_index("dp") == 0
    got = swapped(jnp.where(dp0, high, low), "dp")
    total = added(jnp.where(dp0, low, high), got)
    return total[:, : 3 * cols], total[:, 3 * cols :]


def per_device(fields, grad_y, w_qkv, w_out, mask_ids):
    samples, levels, lat_rows, lon_cols, width = fields.shape
    flat = lambda a: a.transpose(0, 1, 3, 2, 4).reshape(samples, levels, lon_cols * lat_rows, width)
    f, g = flat(fields), flat(grad_y)
    pos = jnp.stack([lax.axis_index("lon"), lax.axis_index("lat")]).astype(jnp.int32)
    lon_out, rim_out, cor_out = strips(f, g)
    rim_in = shifted(rim_out, "lat", -1)
    cor_in = shifted_both(cor_out, -1)
    lon_in = shifted(lon_out, "lon", -1)
    bias = allowed_bias(mask_ids)
    side0 = project(0, pos, f, g, lon_out, rim_in, cor_out, w_qkv, w_out)
    side1 = project(1, pos, f, g, lon_in, rim_in, cor_in, w_qkv, w_out)
    sides = (side0, side1)
    barrier = lax.optimization_barrier
    first = attention((0, 2), pos, bias, sides)
    by_z = chunks_by_z(swap_sum(first[4], swapped(first[5], "lat")))
    outs = swap_sum(first[6], swapped(first[7], "lat"))
    by_z, pos1 = barrier((by_z, pos))
    got_z = relay(by_z, "dz")
    second = attention((1,), pos1, bias, sides)
    got_z, before, send = barrier((got_z, second[6], second[5]))
    ways, before = barrier((with_relayed(by_z, got_z), before))
    got_z = both_ways(ways, "dz")
    last = attention((3,), pos, bias, sides, before=before)
    got_z, send, send_last = barrier((got_z, send, last[5]))
    first_total = added(by_z[0], *got_z).astype(BF).reshape(X, Y * UNIT, -1)
    got, got_last = swapped(send, "lat"), swapped(send_last, "lat")
    total = swap_sum(second[4], got)
    cols = total.shape[1]
    out = jnp.concatenate([total[-2 * cols : -cols], total[-cols:]], axis=1)
    total_last = swap_sum(last[4], got_last)
    outs = [outs[:cols], out, outs[cols:], total_last[-cols:]]
    by_x = chunks_by_x(total_last[:-cols])
    by_z = chunks_with_out(total[: -2 * cols], outs)
    by_x, by_z, att = barrier((by_x, by_z, last[0]))
    got_x, got_z = relay(by_x, "dx"), relay(by_z, "dz")
    last = (att, *last[1:])
    y1, g1, rim1, lon = outputs(1, samples, *side1[:2], w_qkv, w_out, first, second, last)
    rim1 = shifted(rim1, "lat", 1)
    got_x, got_z, lon = barrier((got_x, got_z, lon))
    ways_x, ways_z = with_relayed(by_x, got_x), with_relayed(by_z, got_z)
    lon = patch(lon, rim1)
    ways_x, ways_z, lon, xw0 = barrier((ways_x, ways_z, lon, side0[0]))
    got_x, got_z = both_ways(ways_x, "dx"), both_ways(ways_z, "dz")
    lon = shifted(lon, "lon", 1)
    y0, g0, rim0 = outputs(0, samples, xw0, side0[1], w_qkv, w_out, first, second, last)
    got_x, got_z, rim0 = barrier((got_x, got_z, rim0))
    rim0 = shifted(rim0, "lat", 1)
    by_z_own = by_z[0]
    by_z = added(by_x[0], *got_x).astype(BF).reshape(Z, Y * UNIT, -1)
    total_z = added(by_z_own, *got_z).astype(BF).reshape(X, Y * UNIT, -1)
    by_x = [jnp.concatenate([first_total[d], total_z[d]], axis=1) for d in range(X)]
    total_z = ring_sum(list(by_z), "dz")
    total = jnp.concatenate([ring_sum(by_x, "dx").astype(BF), total_z.astype(BF)], axis=1)
    total = total.reshape(Y, UNIT, -1)
    got_y = to_distance(total[1], dy=1)
    y, gx = merge(y0, g0, y1, g1, rim0, rim1, lon)
    got_y, y, gx = barrier((got_y, y, gx))
    sums = final_sums(added(total[0], got_y).astype(BF))
    unflat = lambda a: a.reshape(samples, levels, lon_cols, lat_rows, width).transpose(0, 1, 3, 2, 4)
    return (unflat(y), unflat(gx), *sums)


def solution(mesh):
    grid = P("dp", None, "lat", "lon", None)
    return jax.shard_map(
        per_device,
        mesh=mesh,
        in_specs=(grid, grid, P(), P(), P()),
        out_specs=(grid, grid, P("lon", ("lat", "dp")), P("lon", ("lat", "dp"))),
        check_vma=False,
    )
```

```python
import functools

import jax
import jax.numpy as jnp
import numpy as np
from jax import lax
from jax.experimental import pallas as pl
from jax.experimental.pallas import tpu as pltpu
from jax.sharding import PartitionSpec as P

HEADS = 16
LEV = 3
WLAT = 4
WLON = 5
SLAT = 2
SLON = 2
ROWS = 8
COLS = 20
EPS = 1e-05

SIDE = 2 * WLON
GROUP = 128
HALF = 4 * GROUP
OWN = LEV * SIDE * ROWS
RIM = 128
COR = 16
BACK = 64
QUADS = 4
SCALE = 0.125
BF = jnp.bfloat16
F32 = jnp.float32
NT = (((1,), (1,)), ((), ()))

X, Y, Z = 4, 2, 4
UNIT = 32
LON, LAT = 0, 1


def params(mebibytes):
    return pltpu.CompilerParams(vmem_limit_bytes=mebibytes * 1024 * 1024)


def cost(micros):
    return pl.CostEstimate(flops=int(micros * 1.1e9), bytes_accessed=10**6, transcendentals=0)


SCALARS = pl.BlockSpec(memory_space=pltpu.SMEM)
IN_HBM = pl.BlockSpec(memory_space=pltpu.HBM)


def in_hbm(a):
    return pltpu.with_memory_space_constraint(a, pltpu.HBM)


def dot(a, b):
    return jnp.dot(a, b, preferred_element_type=F32)


def dot_nt(a, b):
    return lax.dot_general(a, b, NT, preferred_element_type=F32)


def place_of(lon):
    return lon % X, (lon // X) % Y, lon // (X * Y)


def relative(block, pos_ref):
    lon = pos_ref[LON]
    x, y, z = place_of(block)
    x0, y0, z0 = lax.rem(lon, X), lax.rem(lax.div(lon, X), Y), lax.div(lon, X * Y)
    dx, dy, dz = lax.rem(x - x0 + X, X), lax.rem(y - y0 + Y, Y), lax.rem(z - z0 + Z, Z)
    return (dx * Z + dz) * Y + dy


def token(level, r, c):
    return (level * WLAT + r) * SIDE + c


def every():
    for level in range(LEV):
        for c in range(SIDE):
            for i in range(ROWS):
                wr, r = divmod((i - SLAT) % ROWS, WLAT)
                yield level, c, i, wr, r


def one_hot(shape, places):
    out = np.zeros(shape, np.float32)
    for at in places:
        out[at] = 1.0
    return jnp.asarray(out.astype(jnp.bfloat16))


def pick_own():
    return one_hot(
        (2, GROUP, OWN),
        [
            (wr, token(level, r, c), (level * SIDE + c) * ROWS + i)
            for level, c, i, wr, r in every()
            if i >= SLAT
        ],
    )


def pick_rim(side):
    places = []
    for level, c, i, wr, r in every():
        if i < SLAT:
            column = SLON + side * SIDE + c
            if column < COLS:
                src = (level * COLS + column) * SLAT + i
            else:
                src = RIM + (level * SLON + column - COLS) * SLAT + i
            places.append((token(level, r, c), src))
    return one_hot((GROUP, RIM + COR), places)


def pick_out():
    return one_hot(
        (OWN, 2 * GROUP),
        [
            ((level * SIDE + c) * ROWS + i, wr * GROUP + token(level, r, c))
            for level, c, i, wr, r in every()
        ],
    )


def pick_back():
    return one_hot(
        (BACK, GROUP),
        [
            ((level * SIDE + c) * SLAT + i, token(level, r, c))
            for level, c, i, wr, r in every()
            if i < SLAT
        ],
    )


def pick_strip():
    rim = [
        ((level * COLS + column) * SLAT + i, (level * COLS + column) * ROWS + i)
        for level in range(LEV)
        for column in range(COLS)
        for i in range(SLAT)
    ]
    cor = [
        (RIM + (level * SLON + column) * SLAT + i, (level * COLS + column) * ROWS + i)
        for level in range(LEV)
        for column in range(SLON)
        for i in range(SLAT)
    ]
    return one_hot((RIM + COR, LEV * COLS * ROWS), rim + cor)


def pick_place(columns, start):
    return one_hot(
        (LEV, columns * ROWS, BACK),
        [
            (level, c * ROWS + i, (level * SIDE + start + c) * SLAT + i)
            for level in range(LEV)
            for c in range(columns)
            for i in range(SLAT)
        ],
    )


def strips_kernel(pick_ref, f_ref, g_ref, lon_ref, rim_ref, cor_ref):
    for arr, ref in enumerate((f_ref, g_ref)):
        block = ref[0]
        lon_ref[arr, 0] = block[:, : SLON * ROWS]
        strip = dot(pick_ref[...], block.reshape(-1, block.shape[-1])).astype(BF)
        rim_ref[arr, 0] = strip[:RIM]
        cor_ref[arr, 0] = strip[RIM:]


def strips(f, g):
    samples, levels, rows, width = f.shape
    pick = pick_strip()
    block = pl.BlockSpec((1, levels, rows, width), lambda b: (b, 0, 0, 0))
    shapes = [(levels, SLON * ROWS, width), (RIM, width), (COR, width)]
    return pl.pallas_call(
        strips_kernel,
        grid=(samples,),
        in_specs=[pl.BlockSpec(pick.shape, lambda b: (0, 0)), block, block],
        out_specs=[
            pl.BlockSpec((2, 1) + s, lambda b, n=len(s): (0, b) + (0,) * n) for s in shapes
        ],
        out_shape=[jax.ShapeDtypeStruct((2, samples) + s, BF) for s in shapes],
        compiler_params=params(56),
        cost_estimate=cost(3),
        name="strips",
    )(pick, f, g)


def project_kernel(side, pos_ref, own_ref, pick_ref, f_ref, g_ref, wq_ref, wk_ref, wv_ref, wo_ref, rim_ref, *rest):
    if side == 1:
        lon_ref, cor_ref, rest = rest[0], rest[1], rest[2:]
    xw_ref, gw_ref, nt_ref, q_ref, k_ref, v_ref, da_ref, nw, tokens, sems = rest
    samples, levels, _, width = f_ref.shape
    kept = (SIDE if side == 0 else SIDE - SLON) * ROWS
    start = (SLON if side == 0 else SLON + SIDE) * ROWS

    @pl.when(pl.program_id(0) == 0)
    def _():
        copies = [
            pltpu.make_async_copy(ref.at[:, :, start : start + kept], tokens.at[arr], sems.at[arr])
            for arr, ref in enumerate((f_ref, g_ref))
            if side == 0
        ]
        for copy in copies:
            copy.start()
        for copy in copies:
            copy.wait()
        for b in range(samples):
            got = []
            for arr in range(2):
                parts = []
                for level in range(levels):
                    if side == 0:
                        parts.append(tokens[arr, b, level])
                    else:
                        parts.append((f_ref, g_ref)[arr][b, level, start : start + kept])
                        parts.append(lon_ref[arr, b, level])
                rim = rim_ref[arr, b]
                if side == 1:
                    rim = jnp.concatenate([rim, cor_ref[arr, b]], axis=0)
                got.append((jnp.concatenate(parts, axis=0), rim))
            for wr in range(2):
                at = slice((b * 2 + wr) * GROUP, (b * 2 + wr + 1) * GROUP)
                x, g = (dot(own_ref[wr], own) for own, _ in got)
                if wr == 1:
                    x, g = (a + dot(pick_ref[...], rim) for a, (_, rim) in zip((x, g), got))
                gw_ref[at, :] = g.astype(BF)
                xw_ref[at, :] = x.astype(BF)
                centred = x - jnp.mean(x, axis=-1, keepdims=True)
                inv = lax.rsqrt(jnp.mean(centred * centred, axis=-1, keepdims=True) + EPS)
                normed = (centred * inv).astype(BF)
                nw[at, :] = normed
                turned = normed.T
                for block in range(width // UNIT):
                    dst = pl.multiple_of(relative(block, pos_ref) * UNIT, UNIT)
                    nt_ref[pl.ds(dst, UNIT), at] = turned[block * UNIT : (block + 1) * UNIT]

    q_ref[...] = dot(nw[...], wq_ref[...]).astype(BF)
    k_ref[...] = dot(nw[...], wk_ref[...]).astype(BF)
    v_ref[...] = dot(nw[...], wv_ref[...]).astype(BF)
    da_ref[...] = dot_nt(gw_ref[...], wo_ref[...]).astype(BF)


def project(side, pos, f, g, lon_in, rim_in, cor_in, w_qkv, w_out):
    samples, levels, _, width = f.shape
    cols = width // QUADS
    whole = lambda n: (0, 0)
    full = lambda a: pl.BlockSpec(a.shape, lambda n: (0,) * a.ndim)
    kept = (SIDE if side == 0 else SIDE - SLON) * ROWS
    own, pick = pick_own(), pick_rim(side)
    if side == 0:
        pick = pick[:, :RIM]
    halos = (rim_in,) if side == 0 else (rim_in, lon_in, cor_in)
    tokens = (in_hbm(f), in_hbm(g)) if side == 0 else (f, g)
    tall = jax.ShapeDtypeStruct((HALF, width), BF)
    return pl.pallas_call(
        functools.partial(project_kernel, side),
        grid=(QUADS,),
        in_specs=[SCALARS, full(own), full(pick)]
        + ([IN_HBM, IN_HBM] if side == 0 else [full(f), full(g)])
        + [
            pl.BlockSpec((width, cols), lambda n: (0, n)),
            pl.BlockSpec((width, cols), lambda n: (0, QUADS + n)),
            pl.BlockSpec((width, cols), lambda n: (0, 2 * QUADS + n)),
            pl.BlockSpec((cols, width), lambda n: (n, 0)),
        ]
        + [full(a) for a in halos],
        out_specs=[
            pl.BlockSpec((HALF, width), whole),
            pl.BlockSpec((HALF, width), whole),
            pl.BlockSpec((width, HALF), whole),
        ]
        + [pl.BlockSpec((HALF, cols), lambda n: (0, n))] * 4,
        out_shape=[pltpu.HBM((HALF, width), BF), tall, jax.ShapeDtypeStruct((width, HALF), BF)] + [tall] * 4,
        scratch_shapes=[
            pltpu.VMEM((HALF, width), BF),
            pltpu.VMEM((2, samples, levels, kept if side == 0 else 16, width), BF),
            pltpu.SemaphoreType.DMA((2,)),
        ],
        compiler_params=params(20),
        cost_estimate=cost(9),
        name="project",
    )(pos, own, pick, *tokens, w_qkv, w_qkv, w_qkv, w_out, *halos)


def attention_kernel(quads, pos_ref, bias_ref, *rest):
    sides, rest = [rest[:6], rest[6:12]], rest[12:]
    copies = []
    if len(quads) == 1:
        *rest, part, sems = rest
        at = slice(quads[0] * (part.shape[2]), (quads[0] + 1) * part.shape[2])
        copies = [
            pltpu.make_async_copy(sides[1][2 + i].at[:, at], part.at[i], sems.at[i]) for i in range(4)
        ]
        sides[1] = (*sides[1][:2], *(part.at[i] for i in range(4)))
        for copy in copies:
            copy.start()
    if quads == (3,):
        kin_ref, rest = rest[0], rest[1:]
    if quads == (1,):
        att_ref, dq_ref, dk_ref, dv_ref, keep_ref, send_ref, kout_ref, att_t = rest
    elif quads == (3,):
        att_ref, dq_ref, dk_ref, dv_ref, keep_ref, send_ref, att_t = rest
    else:
        att_ref, dq_ref, dk_ref, dv_ref, keep_ref, send_ref, gok_ref, gos_ref, att_t = rest
    width = sides[0][0].shape[0]
    cols = width // QUADS
    head = 64
    lat0 = pos_ref[LAT] == 0
    x0 = lax.rem(pos_ref[LON], X)
    first = lax.broadcasted_iota(jnp.int32, (GROUP, 2 * head), 1) < head
    upper = lax.broadcasted_iota(jnp.int32, (2 * head, GROUP), 0) < head
    zero = jnp.zeros((GROUP, 2 * head), BF)

    def split(pair):
        return jnp.concatenate([jnp.where(first, pair, zero), jnp.where(first, zero, pair)], axis=0)

    def beside(turned):
        return jnp.concatenate(
            [jnp.where(upper, turned, zero), jnp.where(upper, zero, turned)], axis=1
        )

    def stacked(both):
        return jnp.concatenate([both[:, :GROUP], both[:, GROUP:]], axis=0)

    def lanes(start, size):
        return pl.ds(start if isinstance(start, int) else pl.multiple_of(start, 128), size)

    def unit(refs, side, group, wr, pair, src, dst):
        _, _, q_ref, k_ref, v_ref, da_ref = refs
        at = (pl.ds(pl.multiple_of(group * GROUP, GROUP), GROUP), lanes(src + pair * 128, 128))
        here = pl.ds(pl.multiple_of(side * HALF + group * GROUP, GROUP), GROUP)
        both = lanes(dst + pair * 128, 128)
        bias = bias_ref[side * 2 + wr]
        q, k, v, da = q_ref[at], k_ref[at], v_ref[at], da_ref[at]
        q2, da2 = split(q * SCALE), split(da)
        scores = dot_nt(k, q2)
        d_prob = dot_nt(v, da2)
        yield
        scores = scores + jnp.concatenate([bias, bias], axis=1)
        top = jnp.max(scores, axis=0, keepdims=True)
        expd = jnp.exp(scores - top)
        prob = expd * (1.0 / jnp.sum(expd, axis=0, keepdims=True))
        prob16 = prob.astype(BF)
        part = prob * d_prob
        delta = jnp.sum(part, axis=0, keepdims=True)
        d_score = (part - prob * delta).astype(BF)
        yield
        out_t = dot(beside(v.T), stacked(prob16)).astype(BF)
        dq_t = dot(beside((k * SCALE).T), stacked(d_score)).astype(BF)
        dv_ref[here, both] = dot(prob16, da2).astype(BF)
        dk_ref[here, both] = dot(d_score, q2).astype(BF)
        yield
        att_ref[here, both] = out_t.T
        for block in range(128 // UNIT):
            row = lax.rem(block - x0 + X, X) * (2 * UNIT) + pair * UNIT
            att_t[pl.ds(pl.multiple_of(row, UNIT), UNIT), here] = out_t[
                block * UNIT : (block + 1) * UNIT
            ]
        dq_ref[here, both] = dq_t.T
        yield

    low, high = slice(0, HALF), slice(HALF, 2 * HALF)

    def units(src, dst):
        for side in range(2):
            if side == 1:
                for copy in copies:
                    copy.wait()

            def sample(b, carry):
                works = [
                    unit(sides[side], side, b * 2 + wr, wr, pair, src, dst)
                    for wr in range(2)
                    for pair in range(2)
                ]
                for _ in range(4):
                    for work in works:
                        next(work)
                return carry

            lax.fori_loop(0, HALF // (2 * GROUP), sample, 0)

    def out_sums():
        grad_out = dot(att_t[:, low], sides[0][1][...]) + dot(att_t[:, high], sides[1][1][...])
        left, right = grad_out[:, : width // 2], grad_out[:, width // 2 :]
        return jnp.where(lat0, left, right).astype(BF), jnp.where(lat0, right, left).astype(BF)

    def qkv_sums(store, dst):
        def piece(i, carry):
            at = pl.ds(pl.multiple_of(i * 256, 256), 256)
            left = (sides[0][0][at, :], sides[1][0][at, :])
            of_q, of_k, of_v = (
                dot(left[0], ref[low, lanes(dst, cols)]) + dot(left[1], ref[high, lanes(dst, cols)])
                for ref in (dq_ref, dk_ref, dv_ref)
            )
            mine = jnp.where(lat0, of_q, of_v).astype(BF)
            other = jnp.where(lat0, of_v, of_q).astype(BF)
            store(at, mine, other, of_k.astype(BF))
            return carry

        lax.fori_loop(0, width // 256, piece, 0)

    if quads == (0, 2):

        units(0, 0)
        gok_ref[...], gos_ref[...] = out_sums()
        n = pl.program_id(0)
        stays = jnp.logical_xor(lat0, n == 1)

        def store(at, mine, other, of_k):
            keep_ref[at, lanes(n * cols, cols)] = mine
            send_ref[at, lanes(n * cols, cols)] = other

            @pl.when(stays)
            def _():
                keep_ref[at, 2 * cols :] = of_k

            @pl.when(jnp.logical_not(stays))
            def _():
                send_ref[at, 2 * cols :] = of_k

        qkv_sums(store, 0)
        return

    units(0, 0)
    mine, other = out_sums()
    if quads == (1,):
        for half in range(2):
            below = slice(width + half * cols, width + (half + 1) * cols)
            keep_ref[below, :] = mine[:, half * cols : (half + 1) * cols]
            send_ref[below, :] = other[:, half * cols : (half + 1) * cols]
    else:
        keep_ref[width:, :] = mine
        send_ref[width:, :] = other

    def store(at, mine, other, of_k):
        keep_ref[at, :cols] = mine
        send_ref[at, :cols] = other
        if quads == (1,):
            kout_ref[at, :] = of_k
        else:
            before = kin_ref[at, :]
            keep_ref[at, cols:] = jnp.where(lat0, before, of_k)
            send_ref[at, cols:] = jnp.where(lat0, of_k, before)

    qkv_sums(store, 0)


def attention(quads, pos, bias, sides, before=None):
    width = sides[0][0].shape[1]
    cols = width // QUADS
    count = len(quads)
    rows = 2 * HALF

    def quad(n):
        return 2 * n if count == 2 else quads[0]

    whole = lambda n: (0, 0)
    in_specs = [SCALARS, pl.BlockSpec(bias.shape, lambda n: (0, 0, 0))]
    operands = [pos, bias]
    for side, (_, gw, nt, *columns) in enumerate(sides):
        in_specs += [pl.BlockSpec((width, HALF), whole), pl.BlockSpec((HALF, width), whole)]
        operands += [nt, gw]
        if count == 1 and side == 1:
            in_specs += [IN_HBM] * 4
            operands += [in_hbm(a) for a in columns]
        else:
            in_specs += [pl.BlockSpec((HALF, cols), lambda n: (0, quad(n)))] * 4
            operands += columns
    if before is not None:
        in_specs.append(pl.BlockSpec((width, cols), whole))
        operands.append(before)
    out_specs = [pl.BlockSpec((rows, cols), lambda n: (0, n))] * 4
    shapes = [(rows, count * cols)] * 4
    sums = {0: (width, 3 * cols), 1: (width + 2 * cols, cols), 3: (width + cols, 2 * cols)}[quads[0]]
    out_specs += [pl.BlockSpec(sums, whole)] * 2
    shapes += [sums] * 2
    if quads == (0, 2):
        out_specs += [pl.BlockSpec((cols, width // 2), lambda n: (n, 0))] * 2
        shapes += [(count * cols, width // 2)] * 2
    elif quads == (1,):
        out_specs += [pl.BlockSpec((width, cols), whole)]
        shapes += [(width, cols)]
    return pl.pallas_call(
        functools.partial(attention_kernel, quads),
        grid=(count,),
        in_specs=in_specs,
        out_specs=out_specs,
        out_shape=[pltpu.HBM(s, BF) if n < 4 and count == 2 else jax.ShapeDtypeStruct(s, BF) for n, s in enumerate(shapes)],
        scratch_shapes=[pltpu.VMEM((cols, 2 * HALF), BF)]
        + ([pltpu.VMEM((4, HALF, cols), BF), pltpu.SemaphoreType.DMA((4,))] if count == 1 else []),
        compiler_params=params(20),
        cost_estimate=cost(11 * count),
        name="attention",
    )(*operands)


def output_kernel(side, out_ref, back_ref, x_ref, dy_ref, wqkv_ref, wo_ref, *rest):
    first, second, last = rest[:4], rest[4:8], rest[8:12]
    if side == 0:
        y_ref, gx_ref, rim_ref, branch_at, g_at = rest[12:]
    else:
        y_ref, gx_ref, rim_ref, lon_ref, branch_at, g_at = rest[12:]
    levels = y_ref.shape[1]
    cols = last[0].shape[1]
    step = pl.program_id(0)

    def by_quad(i):
        return [first[i][:, :cols], second[i][...], first[i][:, cols:], last[i][...]]

    branch_at[step] = dot(jnp.concatenate(by_quad(0), axis=1), wo_ref[...]).astype(BF)
    d_all = jnp.concatenate([a for i in (1, 2, 3) for a in by_quad(i)], axis=1)
    g_at[step] = dot_nt(d_all, wqkv_ref[...]).astype(BF)

    @pl.when(step == pl.num_programs(0) - 1)
    def _():
        def sample(b, carry):
            at = pl.ds(pl.multiple_of(b * 2 * GROUP, 2 * GROUP), 2 * GROUP)
            joined = lambda ref: jnp.concatenate([ref[n, at] for n in range(QUADS)], axis=1).astype(F32)
            x = x_ref[at, :].astype(F32)
            y = (x + joined(branch_at)).astype(BF)
            g = joined(g_at)
            centred = x - jnp.mean(x, axis=-1, keepdims=True)
            inv = lax.rsqrt(jnp.mean(centred * centred, axis=-1, keepdims=True) + EPS)
            normed = centred * inv
            gx = dy_ref[at, :].astype(F32) + inv * (
                g
                - jnp.mean(g, axis=-1, keepdims=True)
                - normed * jnp.mean(g * normed, axis=-1, keepdims=True)
            )
            for arr, (value, ref) in enumerate(((y, y_ref), (gx.astype(BF), gx_ref))):
                placed = dot(out_ref[...], value).astype(BF)
                back = dot(back_ref[...], value[GROUP:]).astype(BF)
                rim_ref[arr, b] = back
                kept = (SIDE if side == 0 else SIDE - SLON) * ROWS
                for level in range(levels):
                    start = level * SIDE * ROWS
                    ref[b, level] = placed[start : start + kept]
                    if side == 1:
                        lon_ref[arr, b, level] = placed[start + kept : start + SIDE * ROWS]
            return carry

        lax.fori_loop(0, HALF // (2 * GROUP), sample, 0)


def outputs(side, samples, xw, gw, w_qkv, w_out, first, second, last):
    width = w_out.shape[0]
    cols = width // QUADS
    out, back = pick_out(), pick_back()
    full = lambda shape: pl.BlockSpec(shape, lambda n: (0,) * len(shape))
    kept = (SIDE if side == 0 else SIDE - SLON) * ROWS
    shapes = [(samples, LEV, kept, width)] * 2 + [(2, samples, BACK, width)]
    if side == 1:
        shapes += [(2, samples, LEV, SLON * ROWS, width)]
    return pl.pallas_call(
        functools.partial(output_kernel, side),
        grid=(QUADS,),
        in_specs=[full(a.shape) for a in (out, back, xw, gw)]
        + [
            pl.BlockSpec((cols, 3 * width), lambda n: (n, 0)),
            pl.BlockSpec((width, cols), lambda n: (0, n)),
        ]
        + [pl.BlockSpec((HALF, 2 * cols), lambda n: (side, 0))] * 4
        + [pl.BlockSpec((HALF, cols), lambda n: (side, 0))] * 8,
        out_specs=[full(s) for s in shapes],
        out_shape=[jax.ShapeDtypeStruct(s, BF) for s in shapes],
        scratch_shapes=[pltpu.VMEM((QUADS, HALF, cols), BF)] * 2,
        compiler_params=params(14),
        cost_estimate=cost(8),
        name="outputs",
    )(out, back, xw, gw, w_qkv, w_out, *first[:4], *second[:4], *last[:4])


def replaced(mine, pick, rim):
    here = lax.broadcasted_iota(jnp.int32, mine.shape, 0) % ROWS < SLAT
    return jnp.where(here, dot(pick, rim).astype(BF), mine)


def patch_kernel(pick_ref, lon_ref, rim_ref, out_ref):
    for arr in range(2):
        for b in range(lon_ref.shape[1]):
            for level in range(lon_ref.shape[2]):
                out_ref[arr, b, level] = replaced(lon_ref[arr, b, level], pick_ref[level], rim_ref[arr, b])


def patch(lon, rim):
    return pl.pallas_call(
        patch_kernel,
        out_shape=jax.ShapeDtypeStruct(lon.shape, BF),
        compiler_params=params(12),
        cost_estimate=cost(1),
        name="patch",
    )(pick_place(SLON, SIDE - SLON), lon, rim)


def merge_kernel(place0_ref, place1_ref, y0, g0, y1, g1, rim0, rim1, lon, y_ref, gx_ref):
    levels = y_ref.shape[1]
    first, second = SLON * ROWS, (SLON + SIDE) * ROWS
    for arr, (low, high, out) in enumerate(((y0, y1, y_ref), (g0, g1, gx_ref))):
        for level in range(levels):
            out[0, level, :first] = lon[arr, 0, level]
            out[0, level, first:second] = replaced(low[0, level], place0_ref[level], rim0[arr, 0])
            out[0, level, second:] = replaced(high[0, level], place1_ref[level], rim1[arr, 0])


def merge(y0, g0, y1, g1, rim0, rim1, lon):
    samples, levels, _, width = y0.shape
    picks = [pick_place(SIDE, 0), pick_place(SIDE - SLON, 0)]
    full = lambda a: pl.BlockSpec(a.shape, lambda b: (0,) * a.ndim)
    own = lambda a: pl.BlockSpec((1,) + a.shape[1:], lambda b: (b,) + (0,) * (a.ndim - 1))
    strip = lambda a: pl.BlockSpec((2, 1) + a.shape[2:], lambda b: (0, b) + (0,) * (a.ndim - 2))
    shape = jax.ShapeDtypeStruct((samples, levels, COLS * ROWS, width), BF)
    return pl.pallas_call(
        merge_kernel,
        grid=(samples,),
        in_specs=[full(a) for a in picks]
        + [own(a) for a in (y0, g0, y1, g1)]
        + [strip(a) for a in (rim0, rim1, lon)],
        out_specs=[own(shape)] * 2,
        out_shape=[shape] * 2,
        compiler_params=params(12),
        cost_estimate=cost(4),
        name="merge",
    )(*picks, y0, g0, y1, g1, rim0, rim1, lon)


def shifted(value, axis, steps):
    count = lax.axis_size(axis)
    pairs = [(source, (source + steps) % count) for source in range(count)]
    return lax.ppermute(value, axis, pairs)


def shifted_both(value, steps):
    lon, lat = lax.axis_size("lon"), lax.axis_size("lat")
    pairs = [
        (i * lat + j, ((i + steps) % lon) * lat + (j + steps) % lat)
        for i in range(lon)
        for j in range(lat)
    ]
    return lax.ppermute(value, ("lon", "lat"), pairs)


def allowed_bias(mask_ids):
    lat_total = mask_ids.shape[0]
    start = lax.axis_index("lat") * ROWS + SLAT
    lat_global = (start + np.arange(ROWS, dtype=np.int32)) % lat_total
    wide = jnp.concatenate([mask_ids, mask_ids[:, :SLON]], axis=1)
    wide = jnp.concatenate([wide, wide[:SLAT]], axis=0)
    ids = lax.dynamic_slice(wide, (start, lax.axis_index("lon") * COLS + SLON), (ROWS, COLS))
    code = ids * 2 + (lat_global < SLAT).astype(jnp.int32)[:, None]
    code = code + 16 * (np.arange(COLS, dtype=np.int32) // WLON)[None, :]
    code = code.reshape(2, WLAT, 2, SIDE).transpose(2, 0, 1, 3).reshape(4, 1, WLAT * SIDE)
    code = jnp.broadcast_to(code, (4, LEV, WLAT * SIDE)).reshape(4, -1)
    code = jnp.pad(code, ((0, 0), (0, GROUP - code.shape[1])), constant_values=-1)
    same = code[:, :, None] == code[:, None, :]
    return jnp.where(same, 0.0, -jnp.inf).astype(F32)


def swapped(value, axis):
    return lax.ppermute(value, axis, [(0, 1), (1, 0)])


def to_distance(value, dx=0, dy=0, dz=0):
    pairs = []
    for lon in range(X * Y * Z):
        x, y, z = place_of(lon)
        pairs.append((lon, ((z + dz) % Z * Y + (y + dy) % Y) * X + (x + dx) % X))
    return lax.ppermute(value, "lon", pairs)


def added(*terms):
    total = terms[0].astype(F32)
    for term in terms[1:]:
        total = total + term.astype(F32)
    return total


def ring_sum(chunks, name):
    got = [to_distance(chunks[d], **{name: d}) for d in range(1, len(chunks))]
    return added(chunks[0], *got)


def relay(chunks, name):
    half = chunks[2].shape[0] // 2
    return [to_distance(chunks[2][:half], **{name: 1}), to_distance(chunks[2][half:], **{name: 3})]


def with_relayed(chunks, got):
    half = got[0].shape[0]
    up = jnp.concatenate([added(chunks[1][:half], got[0]).astype(BF), chunks[1][half:]], axis=0)
    down = jnp.concatenate([chunks[3][:half], added(chunks[3][half:], got[1]).astype(BF)], axis=0)
    return [up, down]


def both_ways(pair, name):
    return [to_distance(pair[0], **{name: 1}), to_distance(pair[1], **{name: 3})]


def swap_sum(keep, got):
    return added(keep, got).astype(BF)


def chunks_by_z(total):
    total = total.reshape(X, Z, Y * UNIT, -1)
    return [total[:, d].reshape(X * Y * UNIT, -1) for d in range(Z)]


def chunks_by_x(total):
    return jnp.split(total, X)


def chunks_with_out(qkv, outs):
    _, y0, z0 = place_of(lax.axis_index("lon"))
    outs = jnp.stack(outs).reshape(Z, X, Y, UNIT, -1)
    outs = jnp.where(y0 == 0, outs, outs[:, :, ::-1]).reshape(Z, X * Y * UNIT, -1)
    return [
        jnp.concatenate([chunk, lax.dynamic_index_in_dim(outs, (z0 + d) % Z, keepdims=False)], axis=1)
        for d, chunk in enumerate(chunks_by_z(qkv))
    ]


def final_sums(total):
    cols = total.shape[1] // 8
    piece = [total[:, i * cols : (i + 1) * cols] for i in range(8)]
    pick = lambda *which: jnp.concatenate([piece[i] for i in which], axis=1)
    lat0 = lax.axis_index("lat") == 0
    low = jnp.where(lat0, pick(0, 3, 1, 4), pick(2, 7, 0, 4))
    high = jnp.where(lat0, pick(6, 2, 7, 5), pick(3, 1, 6, 5))
    dp0 = lax.axis_index("dp") == 0
    got = swapped(jnp.where(dp0, high, low), "dp")
    total = added(jnp.where(dp0, low, high), got)
    return total[:, : 3 * cols], total[:, 3 * cols :]


def per_device(fields, grad_y, w_qkv, w_out, mask_ids):
    samples, levels, lat_rows, lon_cols, width = fields.shape
    flat = lambda a: a.transpose(0, 1, 3, 2, 4).reshape(samples, levels, lon_cols * lat_rows, width)
    f, g = flat(fields), flat(grad_y)
    pos = jnp.stack([lax.axis_index("lon"), lax.axis_index("lat")]).astype(jnp.int32)
    lon_out, rim_out, cor_out = strips(f, g)
    rim_in = shifted(rim_out, "lat", -1)
    cor_in = shifted_both(cor_out, -1)
    lon_in = shifted(lon_out, "lon", -1)
    bias = allowed_bias(mask_ids)
    side0 = project(0, pos, f, g, lon_out, rim_in, cor_out, w_qkv, w_out)
    side1 = project(1, pos, f, g, lon_in, rim_in, cor_in, w_qkv, w_out)
    sides = (side0, side1)
    barrier = lax.optimization_barrier
    first = attention((0, 2), pos, bias, sides)
    by_z = chunks_by_z(swap_sum(first[4], swapped(first[5], "lat")))
    outs = swap_sum(first[6], swapped(first[7], "lat"))
    by_z, pos1 = barrier((by_z, pos))
    got_z = relay(by_z, "dz")
    second = attention((1,), pos1, bias, sides)
    got_z, before, send = barrier((got_z, second[6], second[5]))
    ways, before = barrier((with_relayed(by_z, got_z), before))
    got_z = both_ways(ways, "dz")
    last = attention((3,), pos, bias, sides, before=before)
    got_z, send, send_last = barrier((got_z, send, last[5]))
    first_total = added(by_z[0], *got_z).astype(BF).reshape(X, Y * UNIT, -1)
    got, got_last = swapped(send, "lat"), swapped(send_last, "lat")
    total = swap_sum(second[4], got)
    cols = total.shape[1]
    out = jnp.concatenate([total[-2 * cols : -cols], total[-cols:]], axis=1)
    total_last = swap_sum(last[4], got_last)
    outs = [outs[:cols], out, outs[cols:], total_last[-cols:]]
    by_x = chunks_by_x(total_last[:-cols])
    by_z = chunks_with_out(total[: -2 * cols], outs)
    by_x, by_z, att = barrier((by_x, by_z, last[0]))
    got_x, got_z = relay(by_x, "dx"), relay(by_z, "dz")
    last = (att, *last[1:])
    y1, g1, rim1, lon = outputs(1, samples, *side1[:2], w_qkv, w_out, first, second, last)
    rim1 = shifted(rim1, "lat", 1)
    got_x, got_z, lon = barrier((got_x, got_z, lon))
    ways_x, ways_z = with_relayed(by_x, got_x), with_relayed(by_z, got_z)
    lon = patch(lon, rim1)
    ways_x, ways_z, lon, xw0 = barrier((ways_x, ways_z, lon, side0[0]))
    got_x, got_z = both_ways(ways_x, "dx"), both_ways(ways_z, "dz")
    lon = shifted(lon, "lon", 1)
    y0, g0, rim0 = outputs(0, samples, xw0, side0[1], w_qkv, w_out, first, second, last)
    got_x, got_z, rim0 = barrier((got_x, got_z, rim0))
    rim0 = shifted(rim0, "lat", 1)
    by_z_own = by_z[0]
    by_z = added(by_x[0], *got_x).astype(BF).reshape(Z, Y * UNIT, -1)
    total_z = added(by_z_own, *got_z).astype(BF).reshape(X, Y * UNIT, -1)
    by_x = [jnp.concatenate([first_total[d], total_z[d]], axis=1) for d in range(X)]
    total_z = ring_sum(list(by_z), "dz")
    total = jnp.concatenate([ring_sum(by_x, "dx").astype(BF), total_z.astype(BF)], axis=1)
    total = total.reshape(Y, UNIT, -1)
    got_y = to_distance(total[1], dy=1)
    y, gx = merge(y0, g0, y1, g1, rim0, rim1, lon)
    got_y, y, gx = barrier((got_y, y, gx))
    sums = final_sums(added(total[0], got_y).astype(BF))
    unflat = lambda a: a.reshape(samples, levels, lon_cols, lat_rows, width).transpose(0, 1, 3, 2, 4)
    return (unflat(y), unflat(gx), *sums)


def solution(mesh):
    grid = P("dp", None, "lat", "lon", None)
    return jax.shard_map(
        per_device,
        mesh=mesh,
        in_specs=(grid, grid, P(), P(), P()),
        out_specs=(grid, grid, P("lon", ("lat", "dp")), P("lon", ("lat", "dp"))),
        check_vma=False,
    )
```
